32 devices in a mesh: grp: 1, gx: 32 (over z, y, x, core), gy: 1.
Axes of the slice: x: 2, y: 2, z: 4, core: 2. Of those that a mesh axis runs over, the one named last changes fastest.
Arguments:
- incident: float32 [2, 16, 128, 128], P('grp', None, 'gx', 'gy'), may hold values from -6 to 6
- material: int32 [16, 128, 128], P('grp', 'gx', 'gy'), may hold values from 0 to 7
- contrast: float32 [8, 2], P('grp'), may hold values from 0.1 to 1.2
- w_first: bfloat16 [32, 4, 3, 3, 3], replicated, may hold values from -0.625 to 0.625
- w_middle: bfloat16 [32, 32, 3, 3, 3], replicated, may hold values from -0.21875 to 0.21875
- w_last: bfloat16 [2, 32, 3, 3, 3], replicated, may hold values from -0.21875 to 0.21875
- z_kernel: float32 [2, 16, 16], P('grp'), may hold values from -1 to 1
- spectral: float32 [2, 128, 128], P('grp', 'gx'), may hold values from -3 to 3
Outputs:
- total_field: float32 [2, 16, 128, 128], P('grp', None, 'gx', 'gy')
The draws below stay inside these ranges and needn't reach their ends.
Inputs may be any that keep to these rules, and one draw needn't show every extreme that they name: `material`: selects a row of contrast.
All inputs are finite; a program needn't handle non-finite values.
Results may differ from the reference program's by a relative error of at most 0.0013.
Values may be sent and summed in bfloat16 or wider, within the bound.
No kernel may reach another device: no remote copies, remote signals or barrier semaphores. Data moves between devices by JAX's collectives and lax.ppermute only.
A program may use at most 64 MiB of HBM per device.

```python
import math
import jax
import jax.numpy as jnp
from jax import lax

NZ = 16
HID = 32
CLASSES = 8
ITERS = 1
NX = 128
NY = 128


def plant(values, key, smallest, largest):
    dims = values.shape
    place = [jax.random.randint(jax.random.fold_in(key, axis), (), 0, dims[axis]) for axis in range(len(dims))]
    values = values.at[tuple(place)].set(smallest)
    longest = dims.index(max(dims))
    place[longest] = (place[longest] + 1) % dims[longest]
    return values.at[tuple(place)].set(largest)


def steps_of(key, dims, pieces, least, top_value):
    gain, own = 1.0, jax.random.fold_in(key, 6)
    for dim, parts in pieces:
        heights = jnp.exp(jax.random.uniform(jax.random.fold_in(own, dim), (parts,), jnp.float32, least / len(pieces), top_value / len(pieces)))
        gain = gain * jnp.repeat(heights, dims[dim] // parts).reshape([-1 if axis == dim else 1 for axis in range(len(dims))])
    return gain


def gaussian(own_key, extent, scale, limit, pieces=(), kind=jnp.bfloat16):
    loudness = steps_of(own_key, extent, pieces, -0.22, 0.18) if pieces else 1.0
    values = jax.random.normal(own_key, extent, jnp.float32) * scale * loudness
    return jnp.minimum(jnp.maximum(values, -limit), limit).astype(kind)


def setup_inputs(seed: int = 0, part: int = 0) -> dict:
    splits = jax.random.split(jax.random.key(seed), 9)
    own_keys = jax.random.split(jax.random.fold_in(splits[8], part), 9)
    incident = gaussian(own_keys[0], (2, NZ, NX, NY), 1.0, 6.0, ((2, 32),), jnp.float32)
    material = plant(jax.random.randint(own_keys[1], (NZ, NX, NY), 0, CLASSES), jax.random.fold_in(own_keys[1], 1), 0, CLASSES - 1).astype(jnp.int32)
    contrast = jnp.clip(jax.random.uniform(own_keys[2], (CLASSES, 2), jnp.float32, 0.1, 1.2), 0.1, 1.2)
    w_first = gaussian(splits[3], (HID, 4, 3, 3, 3), 108 ** -0.5, 0.625)
    w_middle = gaussian(splits[4], (HID, HID, 3, 3, 3), (27 * HID) ** -0.5, 0.21875)
    w_last = gaussian(splits[5], (2, HID, 3, 3, 3), (27 * HID) ** -0.5, 0.21875)
    z_kernel = gaussian(own_keys[6], (2, NZ, NZ), (2 * NZ) ** -0.5, 1.0, (), jnp.float32)
    spectral = gaussian(own_keys[7], (2, NY, NX), 0.5, 3.0, ((1, 32),), jnp.float32)
    return dict(incident=incident, material=material, contrast=contrast, w_first=w_first, w_middle=w_middle, w_last=w_last, z_kernel=z_kernel, spectral=spectral)


def conv_layer(values, weights):
    return lax.conv_general_dilated(values[None], weights, (1, 1, 1), ((1, 1), (0, 0), (0, 0)), dimension_numbers=("NCDHW", "OIDHW", "NCDHW"), preferred_element_type=jnp.float32)[0]


def corrector_chain(padded, w_first, w_middle, w_last):
    hidden = jax.nn.gelu(conv_layer(padded, w_first), approximate=False).astype(jnp.bfloat16)
    hidden = jax.nn.gelu(conv_layer(hidden, w_middle), approximate=False).astype(jnp.bfloat16)
    return conv_layer(hidden, w_last)


def correction_field(features, w_first, w_middle, w_last):
    padded = jnp.pad(features, ((0, 0), (0, 0), (3, 3), (3, 3)), mode="wrap")
    block = math.gcd(NX, 64)
    count = NX // block

    def one_block(index):
        start = (index * block).astype(jnp.int32)
        piece = lax.dynamic_slice_in_dim(padded, start, block + 6, 2)
        return corrector_chain(piece, w_first, w_middle, w_last)

    result = lax.map(one_block, jnp.arange(count, dtype=jnp.int32))
    return jnp.moveaxis(result, 0, 2).reshape(2, NZ, NX, NY)


def green_apply(source, z_kernel, spectral):
    high = lax.Precision.HIGHEST
    kr, ki = z_kernel[0], z_kernel[1]
    lre = jnp.einsum("zw,wxy->zxy", kr, source[0], precision=high) - jnp.einsum("zw,wxy->zxy", ki, source[1], precision=high)
    lim = jnp.einsum("zw,wxy->zxy", kr, source[1], precision=high) + jnp.einsum("zw,wxy->zxy", ki, source[0], precision=high)
    spectrum = jnp.fft.fft2(lax.complex(lre, lim), axes=(1, 2))
    weight = jnp.transpose(lax.complex(spectral[0], spectral[1]))
    result = jnp.fft.ifft2(spectrum * weight[None], axes=(1, 2))
    return jnp.stack([jnp.real(result), jnp.imag(result)])


def reference(incident, material, contrast, w_first, w_middle, w_last, z_kernel, spectral):
    chi_re = contrast[:, 0][material]
    chi_im = contrast[:, 1][material]
    field = incident
    for step in range(ITERS):
        pol_re = chi_re * field[0] - chi_im * field[1]
        pol_im = chi_re * field[1] + chi_im * field[0]
        features = jnp.stack([field[0], field[1], pol_re, pol_im]).astype(jnp.bfloat16)
        source = jnp.stack([pol_re, pol_im]) + correction_field(features, w_first, w_middle, w_last)
        field = incident + green_apply(source, z_kernel, spectral)
    return field
```

```python
import functools
import math

import jax
import jax.numpy as jnp
import ml_dtypes
import numpy as np
from jax import lax
from jax.experimental import pallas as pl
from jax.experimental.pallas import tpu as pltpu
from jax.sharding import PartitionSpec as P

F32 = jnp.float32
BF16 = jnp.bfloat16
VMEM_LIMIT = 48 * 1024 * 1024


def padded_2(x, sides, width):
    for axis, dim in sides:
        count, length = (lax.axis_size(axis), x.shape[dim])
        up = [(i, (i + 1) % count) for i in range(count)]
        down = [(j, i) for i, j in up]
        last = lax.slice_in_dim(x, length - width, length, axis=dim)
        leading = lax.slice_in_dim(x, 0, width, axis=dim)
        before = lax.ppermute(last, axis, up)
        after = lax.ppermute(leading, axis, down)
        x = jnp.concatenate([before, x, after], axis=dim)
    return x


def conv_layer(values, weights):
    return lax.conv_general_dilated(
        values[None],
        weights,
        (1, 1, 1),
        ((1, 1), (0, 0), (0, 0)),
        dimension_numbers=("NCDHW", "OIDHW", "NCDHW"),
        preferred_element_type=jnp.float32,
    )[0]


def activate(values):
    return jax.nn.gelu(values, approximate=False).astype(jnp.bfloat16)


def dft_tables(length):
    positions = jnp.arange(length, dtype=jnp.int32)
    product = positions[:, None] * positions[None, :] % length
    angle = product.astype(jnp.float32) * (2.0 * math.pi / length)
    return (jnp.cos(angle), jnp.sin(angle))


def green_apply(source, z_kernel, spectral):
    high = lax.Precision.HIGHEST
    kr, ki = (z_kernel[0], z_kernel[1])
    lre = jnp.einsum("zw,wxy->zxy", kr, source[0], precision=high) - jnp.einsum(
        "zw,wxy->zxy", ki, source[1], precision=high
    )
    lim = jnp.einsum("zw,wxy->zxy", kr, source[1], precision=high) + jnp.einsum(
        "zw,wxy->zxy", ki, source[0], precision=high
    )
    columns = lax.all_to_all(jnp.stack([lre, lim]), "gy", split_axis=1, concat_axis=3, tiled=True)
    count_y = columns.shape[3]
    cos_y, sin_y = dft_tables(count_y)
    fwd_re = jnp.dot(columns[0], cos_y, precision=high) + jnp.dot(columns[1], sin_y, precision=high)
    fwd_im = jnp.dot(columns[1], cos_y, precision=high) - jnp.dot(columns[0], sin_y, precision=high)
    count_x = columns.shape[2] * lax.axis_size("gx")
    cos_x, sin_x = dft_tables(count_x)
    piece = lax.all_to_all(
        jnp.stack([fwd_re, fwd_im]), "gx", split_axis=3, concat_axis=2, tiled=True
    )
    ar = jnp.einsum("zxk,xq->zkq", piece[0], cos_x, precision=high) + jnp.einsum(
        "zxk,xq->zkq", piece[1], sin_x, precision=high
    )
    ai = jnp.einsum("zxk,xq->zkq", piece[1], cos_x, precision=high) - jnp.einsum(
        "zxk,xq->zkq", piece[0], sin_x, precision=high
    )
    br = spectral[0] * ar - spectral[1] * ai
    bi = spectral[0] * ai + spectral[1] * ar
    gr = jnp.einsum("zkq,qx->zxk", br, cos_x, precision=high) - jnp.einsum(
        "zkq,qx->zxk", bi, sin_x, precision=high
    )
    gi = jnp.einsum("zkq,qx->zxk", bi, cos_x, precision=high) + jnp.einsum(
        "zkq,qx->zxk", br, sin_x, precision=high
    )
    spread = jnp.stack([gr, gi]) / count_x
    rows = lax.all_to_all(spread, "gx", split_axis=2, concat_axis=3, tiled=True)
    inv_re = jnp.dot(rows[0], cos_y, precision=high) - jnp.dot(rows[1], sin_y, precision=high)
    inv_im = jnp.dot(rows[1], cos_y, precision=high) + jnp.dot(rows[0], sin_y, precision=high)
    scattered = jnp.stack([inv_re, inv_im]) / count_y
    return lax.all_to_all(scattered, "gy", split_axis=3, concat_axis=1, tiled=True)


def general_device(incident, material, contrast, w_first, w_middle, w_last, z_kernel, spectral):
    high = lax.Precision.HIGHEST
    classes = contrast.shape[0]
    selector = (material[None] == jnp.arange(classes, dtype=jnp.int32)[:, None, None, None]).astype(
        jnp.float32
    )
    chi_re = jnp.einsum("k,kzxy->zxy", contrast[:, 0], selector, precision=high)
    chi_im = jnp.einsum("k,kzxy->zxy", contrast[:, 1], selector, precision=high)
    field = incident
    pol_re = chi_re * field[0] - chi_im * field[1]
    pol_im = chi_re * field[1] + chi_im * field[0]
    features = jnp.stack([field[0], field[1], pol_re, pol_im]).astype(jnp.bfloat16)
    padded = padded_2(features, (("gx", 2), ("gy", 3)), 3)
    hidden = activate(conv_layer(padded, w_first))
    hidden = activate(conv_layer(hidden, w_middle))
    correction = conv_layer(hidden, w_last)
    source = jnp.stack([pol_re, pol_im]) + correction
    field = incident + green_apply(source, z_kernel, spectral)
    return field


def split(values):
    high = values.astype(BF16)
    low = (values - high.astype(F32)).astype(BF16)
    return high, low


def split_np(values):
    high = values.astype(ml_dtypes.bfloat16)
    low = (values - high.astype(np.float64)).astype(ml_dtypes.bfloat16)
    return high, low


def angles(rows, cols, length):
    product = (np.asarray(rows)[:, None] * np.asarray(cols)[None, :]) % length
    angle = product.astype(np.float64) * (2.0 * math.pi / length)
    return np.cos(angle), np.sin(angle)


def left_table(rows, cols, length, scale=1.0):
    high, low = split_np(np.concatenate(angles(rows, cols, length), axis=1) * scale)
    return np.concatenate([high, high, low], axis=1)


def right_table(rows, cols, length):
    high, low = split_np(np.concatenate(angles(rows, cols, length), axis=0))
    return np.concatenate([high, high, low], axis=0)


def left_split(values):
    high, low = split(values)
    return jnp.concatenate([high, low, high], axis=1)


def right_split(values):
    high, low = split(values)
    return jnp.concatenate([high, low, high], axis=0)


def mm(a, b):
    return jnp.dot(a, b, preferred_element_type=F32)


def iota(shape, dim):
    return lax.broadcasted_iota(jnp.int32, shape, dim)


def other_part(values, nz, sign):
    lanes = values.shape[1]
    real = (iota(values.shape, 1) // nz) % 2 == 0
    ahead = pltpu.roll(values, lanes - nz, 1)
    behind = pltpu.roll(values, nz, 1)
    return jnp.where(real, sign * ahead, -sign * behind)


def swap_blocks(ref, count):
    pieces = [ref[:, q, :] for q in range(count)]
    lanes = pieces[0].shape[1]
    inner = lanes // count
    block = iota(pieces[0].shape, 1) // inner
    rows = []
    for x in range(count):
        total = None
        for q in range(count):
            shift = ((q - x) * inner) % lanes
            moved = pltpu.roll(pieces[q], shift, 1) if shift else pieces[q]
            total = moved if total is None else jnp.where(block == q, moved, total)
        rows.append(total)
    return jnp.concatenate(rows, axis=0)


def prepare_kernel(nz, hid, w1_ref, w2_ref, w3_ref, zk_ref, sp_ref, t1_ref, t2_ref, t3_ref, z_ref, sr_ref, si_ref):
    taps, cols = w1_ref.shape[1], t1_ref.shape[1]
    pick = (iota((taps, cols), 0) == iota((taps, cols), 1) // nz).astype(BF16)
    spread = [
        lax.dot_general(w1_ref[a], pick, (((0,), (0,)), ((), ())), preferred_element_type=F32)
        for a in range(3)
    ]
    place = iota((hid, cols), 1) % nz
    for z in range(nz):
        rows = jnp.zeros((hid, cols), F32)
        for a in range(3):
            rows = jnp.where(place == z + a - 1, spread[a], rows)
        t1_ref[z * hid : (z + 1) * hid, :] = rows.astype(BF16)
    half = nz // 2
    wide = half * hid
    pick = (iota((hid, wide), 0) == iota((hid, wide), 1) % hid).astype(BF16)
    place = iota((hid, wide), 1) // hid
    for b in range(3):
        for d in range(3):
            spread = [mm(w2_ref[a, b, d], pick) for a in range(3)]
            for r in range(half + 2):
                rows = jnp.zeros((hid, wide), F32)
                for a in range(3):
                    rows = jnp.where(place == r + a - 2, spread[a], rows)
                t2_ref[d, r * hid : (r + 1) * hid, b * wide : (b + 1) * wide] = rows.astype(BF16)
    rows3, cols3 = t3_ref.shape
    taps = w3_ref.shape[1]
    repeat = (iota((rows3, taps), 0) // nz == iota((rows3, taps), 1)).astype(BF16)
    pick = (iota((hid, cols3), 0) == iota((hid, cols3), 1) % hid).astype(BF16)
    offset = iota((rows3, cols3), 1) // hid - iota((rows3, cols3), 0) % nz
    total = jnp.zeros((rows3, cols3), F32)
    for a in range(3):
        spread = mm(mm(repeat, w3_ref[a]).astype(BF16), pick)
        total = jnp.where(offset == a - 1, spread, total)
    t3_ref[...] = total.astype(BF16)
    kr, ki = zk_ref[0], zk_ref[1]
    top = jnp.concatenate([kr, -ki], axis=1)
    bottom = jnp.concatenate([ki, kr], axis=1)
    high, low = split(jnp.concatenate([top, bottom, bottom, -top], axis=0))
    z_ref[...] = jnp.concatenate([high, high, low], axis=1)
    count, lanes = sp_ref.shape[1], sr_ref.shape[1]
    pick = (iota((count, lanes), 0) == iota((count, lanes), 1) // (lanes // count)).astype(F32)
    for part, ref in ((0, sr_ref), (1, si_ref)):
        ref[...] = lax.dot_general(
            sp_ref[part],
            pick,
            (((0,), (0,)), ((), ())),
            precision=lax.Precision.HIGHEST,
            preferred_element_type=F32,
        )


def polarised(inc_ref, mat_ref, con_ref, x):
    re, im, cells = inc_ref[0, :, x, :], inc_ref[1, :, x, :], mat_ref[:, x, :]
    chi_re = jnp.zeros_like(re)
    chi_im = jnp.zeros_like(re)
    for k in range(con_ref.shape[0]):
        here = cells == k
        chi_re = jnp.where(here, con_ref[k, 0], chi_re)
        chi_im = jnp.where(here, con_ref[k, 1], chi_im)
    return re, im, chi_re * re - chi_im * im, chi_re * im + chi_im * re


def gelu(values):
    return 0.5 * values * (1.0 + lax.erf(values * math.sqrt(0.5)))


def corrector_kernel(
    con_ref, left_ref, inc_ref, right_ref, mleft_ref, mat_ref, mright_ref, t1_ref, t2_ref, t3_ref,
    z_ref, dft_ref, out_ref, feat, hid1, hid2,
):
    xl, ny = inc_ref.shape[2], inc_ref.shape[3]
    nz = inc_ref.shape[1]
    columns = [(left_ref, mleft_ref, x) for x in range(xl - 3, xl)]
    columns += [(inc_ref, mat_ref, x) for x in range(xl)]
    columns += [(right_ref, mright_ref, x) for x in range(3)]
    own = []
    deep = 12 * nz
    for place, (field, cells, x) in enumerate(columns):
        re, im, pol_re, pol_im = polarised(field, cells, con_ref, x)
        if field is inc_ref:
            own.append(jnp.concatenate([pol_re, pol_im], axis=0))
        stack = jnp.concatenate([re, im, pol_re, pol_im], axis=0)
        rolled = [pltpu.roll(stack, 1, 1), stack, pltpu.roll(stack, ny - 1, 1)]
        feat[place * deep : (place + 1) * deep, :] = jnp.concatenate(rolled, axis=0).astype(BF16)
    for j in range(0, xl + 4, 2):
        window = [feat[(j + i) * deep : (j + i + 3) * deep, :] for i in range(2)]
        made = mm(t1_ref[...], jnp.concatenate(window, axis=1))
        hid1[:, j * ny : (j + 2) * ny] = gelu(made).astype(BF16)
    rows, half = hid1.shape[0], hid1.shape[0] // 2
    hid = rows // nz
    tall = half + hid
    for j in range(0, xl + 2, 2):
        sums = []
        for part, first in ((0, hid), (1, 0)):
            taps = jnp.concatenate([t2_ref[d, first : first + tall, :] for d in range(3)], axis=0)
            window = [
                hid1[part * half : (part + 1) * half, (j + b) * ny : (j + b + 2) * ny] for b in range(3)
            ]
            made = mm(taps, jnp.concatenate(window, axis=0))
            sides = []
            for i in range(2):
                lanes = slice(i * ny, (i + 1) * ny)
                sides.append(
                    pltpu.roll(made[:tall, lanes], 1, 1)
                    + made[tall : 2 * tall, lanes]
                    + pltpu.roll(made[2 * tall :, lanes], ny - 1, 1)
                )
            sums.append(jnp.concatenate(sides, axis=1))
        low, high = sums
        middle = low[half - hid :] + high[: 2 * hid]
        total = jnp.concatenate([low[: half - hid], middle, high[2 * hid :]], axis=0)
        hid2[:, j * ny : (j + 2) * ny] = gelu(total).astype(BF16)
    made = mm(t3_ref[...], hid2[...])
    deep = 2 * nz
    sources = []
    for x in range(xl):
        parts = []
        for d in range(3):
            total = None
            for b in range(3):
                first = (b * 3 + d) * deep
                piece = made[first : first + deep, (x + b) * ny : (x + b + 1) * ny]
                total = piece if total is None else total + piece
            parts.append(total)
        correction = pltpu.roll(parts[0], 1, 1) + parts[1] + pltpu.roll(parts[2], ny - 1, 1)
        sources.append(own[x] + correction)
    lifted = mm(z_ref[...], right_split(jnp.concatenate(sources, axis=1)))
    plain = [lifted[:deep, x * ny : (x + 1) * ny] for x in range(xl)]
    turned = [lifted[deep:, x * ny : (x + 1) * ny] for x in range(xl)]
    both = jnp.concatenate([jnp.concatenate(plain, axis=0), jnp.concatenate(turned, axis=0)], axis=1)
    spectrum = mm(left_split(both), dft_ref[...])
    out_ref[...] = jnp.transpose(spectrum).reshape(out_ref.shape)


def spectral_kernel(nz, in_ref, fwd_ref, inv_ref, sr_ref, si_ref, out_ref):
    values = swap_blocks(in_ref, in_ref.shape[1])
    both = jnp.concatenate([values, other_part(values, nz, 1.0)], axis=0)
    spectrum = mm(fwd_ref[...], right_split(both))
    scaled = sr_ref[...] * spectrum + si_ref[...] * other_part(spectrum, nz, -1.0)
    both = jnp.concatenate([scaled, other_part(scaled, nz, -1.0)], axis=0)
    out_ref[...] = mm(inv_ref[...], right_split(both)).reshape(out_ref.shape)


def finish_kernel(nz, in_ref, tab_ref, inc_ref, out_ref):
    values = swap_blocks(in_ref, in_ref.shape[1])
    both = jnp.concatenate([values, other_part(values, nz, -1.0)], axis=0)
    field = jnp.transpose(mm(tab_ref[...], right_split(both)))
    for x in range(inc_ref.shape[2]):
        for part in range(2):
            first = (2 * x + part) * nz
            out_ref[part, :, x, :] = inc_ref[part, :, x, :] + field[first : first + nz, :]


def call(kernel, out_shapes, args, scratch=(), smem=(), flops=0):
    vmem = pl.BlockSpec(memory_space=pltpu.VMEM)
    specs = [pl.BlockSpec(memory_space=pltpu.SMEM) if i in smem else vmem for i in range(len(args))]
    single = not isinstance(out_shapes, list)
    return pl.pallas_call(
        kernel,
        out_shape=out_shapes,
        in_specs=specs,
        out_specs=vmem if single else [vmem] * len(out_shapes),
        scratch_shapes=scratch,
        compiler_params=pltpu.CompilerParams(vmem_limit_bytes=VMEM_LIMIT),
        cost_estimate=pl.CostEstimate(flops=flops, bytes_accessed=4 * 1024 * 1024, transcendentals=0),
    )(*args)


def lane_device(incident, material, contrast, w_first, w_middle, w_last, z_kernel, spectral):
    count = lax.axis_size("gx")
    nz, xl, ny = material.shape
    hid = w_middle.shape[0]
    ql, nx = spectral.shape[1], spectral.shape[2]
    struct = jax.ShapeDtypeStruct
    up = [(i, (i + 1) % count) for i in range(count)]
    down = [(j, i) for i, j in up]
    left, right = lax.ppermute(incident, "gx", up), lax.ppermute(incident, "gx", down)
    mleft, mright = lax.ppermute(material, "gx", up), lax.ppermute(material, "gx", down)
    t1, t2, t3, zmat, sr, si = call(
        functools.partial(prepare_kernel, nz, hid),
        [
            struct((nz * hid, 36 * nz), BF16),
            struct((3, (nz // 2 + 2) * hid, 3 * nz // 2 * hid), BF16),
            struct((18 * nz, nz * hid), BF16),
            struct((4 * nz, 6 * nz), BF16),
            struct((nx, ql * 2 * nz), F32),
            struct((nx, ql * 2 * nz), F32),
        ],
        (
            jnp.transpose(w_first, (2, 3, 4, 1, 0)).reshape(3, 36, hid),
            jnp.transpose(w_middle, (2, 3, 4, 0, 1)),
            jnp.transpose(w_last, (2, 3, 4, 0, 1)).reshape(3, 18, hid),
            z_kernel,
            spectral,
        ),
        flops=10**9,
    )
    alternate = [xl * s + x for x in range(xl) for s in range(count)]
    natural = list(range(nx))
    lanes = 2 * nz * xl
    spectrum = call(
        corrector_kernel,
        struct((count, ql, lanes), F32),
        (
            contrast, left, incident, right, mleft, material, mright, t1, t2, t3, zmat,
            right_table(range(ny), range(ny), ny),
        ),
        scratch=[
            pltpu.VMEM(((xl + 6) * 12 * nz, ny), BF16),
            pltpu.VMEM((nz * hid, (xl + 4) * ny), BF16),
            pltpu.VMEM((nz * hid, (xl + 2) * ny), BF16),
        ],
        smem=(0,),
        flops=10**9,
    )
    piece = lax.all_to_all(spectrum, "gx", 0, 0, tiled=True)
    spread = call(
        functools.partial(spectral_kernel, nz),
        struct((count, xl, lanes), F32),
        (
            piece,
            left_table(natural, alternate, nx),
            left_table(natural, natural, nx, 1.0 / (nx * ny)),
            sr,
            si,
        ),
        flops=10**8,
    )
    rows = lax.all_to_all(spread, "gx", 0, 0, tiled=True)
    return call(
        functools.partial(finish_kernel, nz),
        struct(incident.shape, F32),
        (rows, left_table(natural, alternate, ny), incident),
        flops=10**8,
    )


def per_device(incident, material, contrast, w_first, w_middle, w_last, z_kernel, spectral):
    nz, xl, ny = material.shape
    ql, nx = spectral.shape[1], spectral.shape[2]
    lanes = (
        lax.axis_size("gy") == 1
        and ny == 128
        and nx == 128
        and xl == 4
        and ql == 4
        and 2 * nz * xl == 128
        and w_middle.shape[0] == 32
    )
    device = lane_device if lanes else general_device
    return device(incident, material, contrast, w_first, w_middle, w_last, z_kernel, spectral)


def solution(mesh):
    placed = (
        P("grp", None, "gx", "gy"),
        P("grp", "gx", "gy"),
        P("grp", None),
        P(),
        P(),
        P(),
        P("grp", None, None),
        P("grp", "gx", None),
    )
    return jax.shard_map(
        per_device,
        mesh=mesh,
        in_specs=placed,
        out_specs=P("grp", None, "gx", "gy"),
        check_vma=False,
    )
```

```python
import functools
import math

import jax
import jax.numpy as jnp
from jax import lax
from jax.experimental import pallas as pl
from jax.experimental.pallas import tpu as pltpu
from jax.sharding import PartitionSpec as P

F32 = jnp.float32
BF16 = jnp.bfloat16
VMEM_LIMIT = 48 * 1024 * 1024


def padded_2(x, sides, width):
    for axis, dim in sides:
        count, length = (lax.axis_size(axis), x.shape[dim])
        up = [(i, (i + 1) % count) for i in range(count)]
        down = [(j, i) for i, j in up]
        last = lax.slice_in_dim(x, length - width, length, axis=dim)
        leading = lax.slice_in_dim(x, 0, width, axis=dim)
        before = lax.ppermute(last, axis, up)
        after = lax.ppermute(leading, axis, down)
        x = jnp.concatenate([before, x, after], axis=dim)
    return x


def conv_layer(values, weights):
    return lax.conv_general_dilated(
        values[None],
        weights,
        (1, 1, 1),
        ((1, 1), (0, 0), (0, 0)),
        dimension_numbers=("NCDHW", "OIDHW", "NCDHW"),
        preferred_element_type=jnp.float32,
    )[0]


def activate(values):
    return jax.nn.gelu(values, approximate=False).astype(jnp.bfloat16)


def dft_tables(length):
    positions = jnp.arange(length, dtype=jnp.int32)
    product = positions[:, None] * positions[None, :] % length
    angle = product.astype(jnp.float32) * (2.0 * math.pi / length)
    return (jnp.cos(angle), jnp.sin(angle))


def green_apply(source, z_kernel, spectral):
    high = lax.Precision.HIGHEST
    kr, ki = (z_kernel[0], z_kernel[1])
    lre = jnp.einsum("zw,wxy->zxy", kr, source[0], precision=high) - jnp.einsum(
        "zw,wxy->zxy", ki, source[1], precision=high
    )
    lim = jnp.einsum("zw,wxy->zxy", kr, source[1], precision=high) + jnp.einsum(
        "zw,wxy->zxy", ki, source[0], precision=high
    )
    columns = lax.all_to_all(jnp.stack([lre, lim]), "gy", split_axis=1, concat_axis=3, tiled=True)
    count_y = columns.shape[3]
    cos_y, sin_y = dft_tables(count_y)
    fwd_re = jnp.dot(columns[0], cos_y, precision=high) + jnp.dot(columns[1], sin_y, precision=high)
    fwd_im = jnp.dot(columns[1], cos_y, precision=high) - jnp.dot(columns[0], sin_y, precision=high)
    count_x = columns.shape[2] * lax.axis_size("gx")
    cos_x, sin_x = dft_tables(count_x)
    piece = lax.all_to_all(
        jnp.stack([fwd_re, fwd_im]), "gx", split_axis=3, concat_axis=2, tiled=True
    )
    ar = jnp.einsum("zxk,xq->zkq", piece[0], cos_x, precision=high) + jnp.einsum(
        "zxk,xq->zkq", piece[1], sin_x, precision=high
    )
    ai = jnp.einsum("zxk,xq->zkq", piece[1], cos_x, precision=high) - jnp.einsum(
        "zxk,xq->zkq", piece[0], sin_x, precision=high
    )
    br = spectral[0] * ar - spectral[1] * ai
    bi = spectral[0] * ai + spectral[1] * ar
    gr = jnp.einsum("zkq,qx->zxk", br, cos_x, precision=high) - jnp.einsum(
        "zkq,qx->zxk", bi, sin_x, precision=high
    )
    gi = jnp.einsum("zkq,qx->zxk", bi, cos_x, precision=high) + jnp.einsum(
        "zkq,qx->zxk", br, sin_x, precision=high
    )
    spread = jnp.stack([gr, gi]) / count_x
    rows = lax.all_to_all(spread, "gx", split_axis=2, concat_axis=3, tiled=True)
    inv_re = jnp.dot(rows[0], cos_y, precision=high) - jnp.dot(rows[1], sin_y, precision=high)
    inv_im = jnp.dot(rows[1], cos_y, precision=high) + jnp.dot(rows[0], sin_y, precision=high)
    scattered = jnp.stack([inv_re, inv_im]) / count_y
    return lax.all_to_all(scattered, "gy", split_axis=3, concat_axis=1, tiled=True)


def general_device(incident, material, contrast, w_first, w_middle, w_last, z_kernel, spectral):
    high = lax.Precision.HIGHEST
    classes = contrast.shape[0]
    selector = (material[None] == jnp.arange(classes, dtype=jnp.int32)[:, None, None, None]).astype(
        jnp.float32
    )
    chi_re = jnp.einsum("k,kzxy->zxy", contrast[:, 0], selector, precision=high)
    chi_im = jnp.einsum("k,kzxy->zxy", contrast[:, 1], selector, precision=high)
    field = incident
    pol_re = chi_re * field[0] - chi_im * field[1]
    pol_im = chi_re * field[1] + chi_im * field[0]
    features = jnp.stack([field[0], field[1], pol_re, pol_im]).astype(jnp.bfloat16)
    padded = padded_2(features, (("gx", 2), ("gy", 3)), 3)
    hidden = activate(conv_layer(padded, w_first))
    hidden = activate(conv_layer(hidden, w_middle))
    correction = conv_layer(hidden, w_last)
    source = jnp.stack([pol_re, pol_im]) + correction
    field = incident + green_apply(source, z_kernel, spectral)
    return field


def split(values):
    high = values.astype(BF16)
    low = (values - high.astype(F32)).astype(BF16)
    return high, low


def cosine(steps, length):
    turn = 2.0 * math.pi / length
    angle = (length // 4 - jnp.minimum(steps, length - steps)).astype(F32) * turn
    square = angle * angle
    total = jnp.full_like(angle, 1.0 / math.factorial(13))
    for power in (11, 9, 7, 5, 3, 1):
        sign = 1.0 if power % 4 == 1 else -1.0
        total = total * square + sign / math.factorial(power)
    return total * angle


def dft_parts(rows, cols, length, axis, scale=1.0):
    steps = lax.rem(rows * cols, length)
    later = lax.rem(steps + 3 * length // 4, length)
    high, low = split(jnp.concatenate([cosine(steps, length), cosine(later, length)], axis=axis) * scale)
    return jnp.concatenate([high, high, low], axis=axis)


def left_split(values):
    high, low = split(values)
    return jnp.concatenate([high, low, high], axis=1)


def right_split(values):
    high, low = split(values)
    return jnp.concatenate([high, low, high], axis=0)


def mm(a, b):
    return jnp.dot(a, b, preferred_element_type=F32)


def iota(shape, dim):
    return lax.broadcasted_iota(jnp.int32, shape, dim)


def other_part(values, nz, sign):
    lanes = values.shape[1]
    real = (iota(values.shape, 1) // nz) % 2 == 0
    ahead = pltpu.roll(values, lanes - nz, 1)
    behind = pltpu.roll(values, nz, 1)
    return jnp.where(real, sign * ahead, -sign * behind)


def swap_blocks(ref, count):
    pieces = [ref[:, q, :] for q in range(count)]
    lanes = pieces[0].shape[1]
    inner = lanes // count
    block = iota(pieces[0].shape, 1) // inner
    rows = []
    for x in range(count):
        total = None
        for q in range(count):
            shift = ((q - x) * inner) % lanes
            moved = pltpu.roll(pieces[q], shift, 1) if shift else pieces[q]
            total = moved if total is None else jnp.where(block == q, moved, total)
        rows.append(total)
    return jnp.concatenate(rows, axis=0)


def middle_kernel(nz, w2_ref, t2_ref):
    hid = w2_ref.shape[3]
    half = nz // 2
    wide = half * hid
    pick = (iota((hid, wide), 0) == iota((hid, wide), 1) % hid).astype(BF16)
    place = iota((hid, wide), 1) // hid
    for b in range(3):
        for d in range(3):
            spread = [mm(w2_ref[a, b, d], pick) for a in range(3)]
            for r in range(half + 2):
                rows = jnp.zeros((hid, wide), F32)
                for a in range(3):
                    rows = jnp.where(place == r + a - 2, spread[a], rows)
                t2_ref[d, r * hid : (r + 1) * hid, b * wide : (b + 1) * wide] = rows.astype(BF16)


def prepare_kernel(
    nz, xl, w1_ref, w3_ref, zk_ref, sp_ref,
    t1_ref, t3_ref, z_ref, sr_ref, si_ref, dft_ref, fwd_ref, inv_ref,
):
    channels, hid = w1_ref.shape[3:]
    taps, cols = 9 * channels, t1_ref.shape[1]
    pick = (iota((taps, cols), 0) == iota((taps, cols), 1) // nz).astype(BF16)
    spread = []
    for a in range(3):
        stack = jnp.concatenate(
            [w1_ref[a, b, d].astype(F32) for b in range(3) for d in range(3)], axis=0
        ).astype(BF16)
        spread.append(
            lax.dot_general(stack, pick, (((0,), (0,)), ((), ())), preferred_element_type=F32)
        )
    place = iota((hid, cols), 1) % nz
    for z in range(nz):
        rows = jnp.zeros((hid, cols), F32)
        for a in range(3):
            rows = jnp.where(place == z + a - 1, spread[a], rows)
        t1_ref[z * hid : (z + 1) * hid, :] = rows.astype(BF16)
    rows3, cols3 = t3_ref.shape
    taps = 9 * w3_ref.shape[3]
    repeat = (iota((rows3, taps), 0) // nz == iota((rows3, taps), 1)).astype(BF16)
    pick = (iota((hid, cols3), 0) == iota((hid, cols3), 1) % hid).astype(BF16)
    offset = iota((rows3, cols3), 1) // hid - iota((rows3, cols3), 0) % nz
    total = jnp.zeros((rows3, cols3), F32)
    for a in range(3):
        stack = jnp.concatenate(
            [w3_ref[a, b, d].astype(F32) for b in range(3) for d in range(3)], axis=0
        ).astype(BF16)
        spread = mm(mm(repeat, stack).astype(BF16), pick)
        total = jnp.where(offset == a - 1, spread, total)
    t3_ref[...] = total.astype(BF16)
    kr, ki = zk_ref[0], zk_ref[1]
    top = jnp.concatenate([kr, -ki], axis=1)
    bottom = jnp.concatenate([ki, kr], axis=1)
    high, low = split(jnp.concatenate([top, bottom, bottom, -top], axis=0))
    z_ref[...] = jnp.concatenate([high, high, low], axis=1)
    count, lanes = sp_ref.shape[1], sr_ref.shape[1]
    pick = (iota((count, lanes), 0) == iota((count, lanes), 1) // (lanes // count)).astype(F32)
    for part, ref in ((0, sr_ref), (1, si_ref)):
        ref[...] = lax.dot_general(
            sp_ref[part],
            pick,
            (((0,), (0,)), ((), ())),
            precision=lax.Precision.HIGHEST,
            preferred_element_type=F32,
        )
    nx, ny = inv_ref.shape[0], dft_ref.shape[1]
    dft_ref[...] = dft_parts(iota((ny, ny), 0), iota((ny, ny), 1), ny, 0)
    first, second = iota((nx, nx), 0), iota((nx, nx), 1)
    inv_ref[...] = dft_parts(first, second, nx, 1, 1.0 / (nx * ny))
    count = nx // xl
    second = lax.rem(second, count) * xl + second // count
    fwd_ref[...] = dft_parts(first, second, nx, 1)


def polarised(column, con_ref):
    re, im, cells = column
    chi_re = jnp.zeros_like(re)
    chi_im = jnp.zeros_like(re)
    for k in range(con_ref.shape[1]):
        here = cells == float(k)
        chi_re = jnp.where(here, con_ref[0, k], chi_re)
        chi_im = jnp.where(here, con_ref[1, k], chi_im)
    return re, im, chi_re * re - chi_im * im, chi_re * im + chi_im * re


def gelu(values):
    return 0.5 * values * (1.0 + lax.erf(values * math.sqrt(0.5)))


def corrector_kernel(
    con_ref, own_ref, chip_ref, far_ref, t1_ref, t2_ref, t3_ref, z_ref, dft_ref, out_ref,
    feat, hid1, hid2,
):
    nz, xl, ny = own_ref.shape[1:]
    even = lax.axis_index("gx") % 2 == 0

    def column(x):
        if x < 0:
            x += xl
            return [jnp.where(even, far_ref[i, :, x, :], chip_ref[i, :, x, :]) for i in range(3)]
        if x >= xl:
            x -= xl
            return [jnp.where(even, chip_ref[i, :, x, :], far_ref[i, :, x, :]) for i in range(3)]
        return [own_ref[i, :, x, :] for i in range(3)]

    own = []
    deep = 12 * nz
    for place in range(xl + 6):
        re, im, pol_re, pol_im = polarised(column(place - 3), con_ref)
        if 0 <= place - 3 < xl:
            own.append(jnp.concatenate([pol_re, pol_im], axis=0))
        stack = jnp.concatenate([re, im, pol_re, pol_im], axis=0)
        rolled = [pltpu.roll(stack, 1, 1), stack, pltpu.roll(stack, ny - 1, 1)]
        feat[place * deep : (place + 1) * deep, :] = jnp.concatenate(rolled, axis=0).astype(BF16)
    for j in range(0, xl + 4, 2):
        window = [feat[(j + i) * deep : (j + i + 3) * deep, :] for i in range(2)]
        made = mm(t1_ref[...], jnp.concatenate(window, axis=1))
        hid1[:, j * ny : (j + 2) * ny] = gelu(made).astype(BF16)
    rows, half = hid1.shape[0], hid1.shape[0] // 2
    hid = rows // nz
    tall = half + hid
    for j in range(0, xl + 2, 2):
        sums = []
        for part, first in ((0, hid), (1, 0)):
            taps = jnp.concatenate([t2_ref[d, first : first + tall, :] for d in range(3)], axis=0)
            window = [
                hid1[part * half : (part + 1) * half, (j + b) * ny : (j + b + 2) * ny] for b in range(3)
            ]
            made = mm(taps, jnp.concatenate(window, axis=0))
            sides = []
            for i in range(2):
                lanes = slice(i * ny, (i + 1) * ny)
                sides.append(
                    pltpu.roll(made[:tall, lanes], 1, 1)
                    + made[tall : 2 * tall, lanes]
                    + pltpu.roll(made[2 * tall :, lanes], ny - 1, 1)
                )
            sums.append(jnp.concatenate(sides, axis=1))
        low, high = sums
        middle = low[half - hid :] + high[: 2 * hid]
        total = jnp.concatenate([low[: half - hid], middle, high[2 * hid :]], axis=0)
        hid2[:, j * ny : (j + 2) * ny] = gelu(total).astype(BF16)
    made = mm(t3_ref[...], hid2[...])
    deep = 2 * nz
    sources = []
    for x in range(xl):
        parts = []
        for d in range(3):
            total = None
            for b in range(3):
                first = (b * 3 + d) * deep
                piece = made[first : first + deep, (x + b) * ny : (x + b + 1) * ny]
                total = piece if total is None else total + piece
            parts.append(total)
        correction = pltpu.roll(parts[0], 1, 1) + parts[1] + pltpu.roll(parts[2], ny - 1, 1)
        sources.append(own[x] + correction)
    lifted = mm(z_ref[...], right_split(jnp.concatenate(sources, axis=1)))
    plain = [lifted[:deep, x * ny : (x + 1) * ny] for x in range(xl)]
    turned = [lifted[deep:, x * ny : (x + 1) * ny] for x in range(xl)]
    both = jnp.concatenate([jnp.concatenate(plain, axis=0), jnp.concatenate(turned, axis=0)], axis=1)
    spectrum = mm(left_split(both), dft_ref[...])
    out_ref[...] = jnp.transpose(spectrum).reshape(out_ref.shape)


def spectral_kernel(nz, in_ref, fwd_ref, inv_ref, sr_ref, si_ref, out_ref):
    values = swap_blocks(in_ref, in_ref.shape[1])
    both = jnp.concatenate([values, other_part(values, nz, 1.0)], axis=0)
    spectrum = mm(fwd_ref[...], right_split(both))
    scaled = sr_ref[...] * spectrum + si_ref[...] * other_part(spectrum, nz, -1.0)
    both = jnp.concatenate([scaled, other_part(scaled, nz, -1.0)], axis=0)
    out_ref[...] = mm(inv_ref[...], right_split(both)).reshape(out_ref.shape)


def finish_kernel(nz, in_ref, tab_ref, inc_ref, out_ref):
    values = swap_blocks(in_ref, in_ref.shape[1])
    both = jnp.concatenate([values, other_part(values, nz, -1.0)], axis=0)
    field = jnp.transpose(mm(tab_ref[...], right_split(both)))
    for x in range(inc_ref.shape[2]):
        for part in range(2):
            first = (2 * x + part) * nz
            out_ref[part, :, x, :] = inc_ref[part, :, x, :] + field[first : first + nz, :]


def call(kernel, out_shapes, args, scratch=(), smem=(), flops=0):
    vmem = pl.BlockSpec(memory_space=pltpu.VMEM)
    specs = [vmem] * len(args)
    for i in smem:
        specs[i] = pl.BlockSpec(memory_space=pltpu.SMEM)
    single = not isinstance(out_shapes, list)
    return pl.pallas_call(
        kernel,
        out_shape=out_shapes,
        in_specs=specs,
        out_specs=vmem if single else [vmem] * len(out_shapes),
        scratch_shapes=scratch,
        compiler_params=pltpu.CompilerParams(vmem_limit_bytes=VMEM_LIMIT),
        cost_estimate=pl.CostEstimate(flops=flops, bytes_accessed=4 * 1024 * 1024, transcendentals=0),
    )(*args)


def lane_device(incident, material, contrast, w_first, w_middle, w_last, z_kernel, spectral):
    count = lax.axis_size("gx")
    nz, xl, ny = material.shape
    hid = w_middle.shape[0]
    ql, nx = spectral.shape[1], spectral.shape[2]
    struct = jax.ShapeDtypeStruct
    last = lax.broadcasted_iota(jnp.int32, (3, 1, 1, 1), 0) == 2
    own = jnp.where(last, material.astype(F32)[None], jnp.pad(incident, ((0, 1),) + ((0, 0),) * 3))
    chip = lax.ppermute(own, "gx", [(i, i ^ 1) for i in range(count)])
    pairs = [(i, (i + 1) % count) for i in range(1, count, 2)]
    far = lax.ppermute(own, "gx", pairs + [(j, i) for i, j in pairs])
    lanes = 2 * nz * xl
    t2 = call(
        functools.partial(middle_kernel, nz),
        struct((3, (nz // 2 + 2) * hid, 3 * nz // 2 * hid), BF16),
        (jnp.transpose(w_middle, (2, 3, 4, 0, 1)),),
        flops=10**9,
    )
    t1, t3, zmat, sr, si, dft, fwd, inv = call(
        functools.partial(prepare_kernel, nz, xl),
        [
            struct((nz * hid, 36 * nz), BF16),
            struct((18 * nz, nz * hid), BF16),
            struct((4 * nz, 6 * nz), BF16),
            struct((nx, ql * 2 * nz), F32),
            struct((nx, ql * 2 * nz), F32),
            struct((6 * ny, ny), BF16),
            struct((nx, 6 * nx), BF16),
            struct((nx, 6 * nx), BF16),
        ],
        (
            jnp.transpose(w_first, (2, 3, 4, 1, 0)),
            jnp.transpose(w_last, (2, 3, 4, 0, 1)),
            z_kernel,
            spectral,
        ),
        flops=10**9,
    )
    spectrum = call(
        corrector_kernel,
        struct((count, ql, lanes), F32),
        (jnp.transpose(contrast), own, chip, far, t1, t2, t3, zmat, dft),
        scratch=[
            pltpu.VMEM(((xl + 6) * 12 * nz, ny), BF16),
            pltpu.VMEM((nz * hid, (xl + 4) * ny), BF16),
            pltpu.VMEM((nz * hid, (xl + 2) * ny), BF16),
        ],
        smem=(0,),
        flops=10**9,
    )
    piece = lax.all_to_all(spectrum, "gx", 0, 0, tiled=True)
    spread = call(
        functools.partial(spectral_kernel, nz),
        struct((count, xl, lanes), F32),
        (piece, fwd, inv, sr, si),
        flops=10**8,
    )
    rows = lax.all_to_all(spread, "gx", 0, 0, tiled=True)
    return call(
        functools.partial(finish_kernel, nz),
        struct(incident.shape, F32),
        (rows, fwd, own),
        flops=10**8,
    )


def per_device(incident, material, contrast, w_first, w_middle, w_last, z_kernel, spectral):
    nz, xl, ny = material.shape
    ql, nx = spectral.shape[1], spectral.shape[2]
    lanes = (
        lax.axis_size("gy") == 1
        and ny == 128
        and nx == 128
        and xl == 4
        and ql == 4
        and 2 * nz * xl == 128
        and w_middle.shape[0] == 32
    )
    device = lane_device if lanes else general_device
    return device(incident, material, contrast, w_first, w_middle, w_last, z_kernel, spectral)


def solution(mesh):
    placed = (
        P("grp", None, "gx", "gy"),
        P("grp", "gx", "gy"),
        P("grp", None),
        P(),
        P(),
        P(),
        P("grp", None, None),
        P("grp", "gx", None),
    )
    return jax.shard_map(
        per_device,
        mesh=mesh,
        in_specs=placed,
        out_specs=P("grp", None, "gx", "gy"),
        check_vma=False,
    )
```

```python
import functools
import math

import jax
import jax.numpy as jnp
from jax import lax
from jax.experimental import pallas as pl
from jax.experimental.pallas import tpu as pltpu
from jax.sharding import PartitionSpec as P

F32 = jnp.float32
BF16 = jnp.bfloat16
VMEM_LIMIT = 48 * 1024 * 1024


def padded_2(x, sides, width):
    for axis, dim in sides:
        count, length = (lax.axis_size(axis), x.shape[dim])
        up = [(i, (i + 1) % count) for i in range(count)]
        down = [(j, i) for i, j in up]
        last = lax.slice_in_dim(x, length - width, length, axis=dim)
        leading = lax.slice_in_dim(x, 0, width, axis=dim)
        before = lax.ppermute(last, axis, up)
        after = lax.ppermute(leading, axis, down)
        x = jnp.concatenate([before, x, after], axis=dim)
    return x


def conv_layer(values, weights):
    return lax.conv_general_dilated(
        values[None],
        weights,
        (1, 1, 1),
        ((1, 1), (0, 0), (0, 0)),
        dimension_numbers=("NCDHW", "OIDHW", "NCDHW"),
        preferred_element_type=jnp.float32,
    )[0]


def activate(values):
    return jax.nn.gelu(values, approximate=False).astype(jnp.bfloat16)


def dft_tables(length):
    positions = jnp.arange(length, dtype=jnp.int32)
    product = positions[:, None] * positions[None, :] % length
    angle = product.astype(jnp.float32) * (2.0 * math.pi / length)
    return (jnp.cos(angle), jnp.sin(angle))


def green_apply(source, z_kernel, spectral):
    high = lax.Precision.HIGHEST
    kr, ki = (z_kernel[0], z_kernel[1])
    lre = jnp.einsum("zw,wxy->zxy", kr, source[0], precision=high) - jnp.einsum(
        "zw,wxy->zxy", ki, source[1], precision=high
    )
    lim = jnp.einsum("zw,wxy->zxy", kr, source[1], precision=high) + jnp.einsum(
        "zw,wxy->zxy", ki, source[0], precision=high
    )
    columns = lax.all_to_all(jnp.stack([lre, lim]), "gy", split_axis=1, concat_axis=3, tiled=True)
    count_y = columns.shape[3]
    cos_y, sin_y = dft_tables(count_y)
    fwd_re = jnp.dot(columns[0], cos_y, precision=high) + jnp.dot(columns[1], sin_y, precision=high)
    fwd_im = jnp.dot(columns[1], cos_y, precision=high) - jnp.dot(columns[0], sin_y, precision=high)
    count_x = columns.shape[2] * lax.axis_size("gx")
    cos_x, sin_x = dft_tables(count_x)
    piece = lax.all_to_all(
        jnp.stack([fwd_re, fwd_im]), "gx", split_axis=3, concat_axis=2, tiled=True
    )
    ar = jnp.einsum("zxk,xq->zkq", piece[0], cos_x, precision=high) + jnp.einsum(
        "zxk,xq->zkq", piece[1], sin_x, precision=high
    )
    ai = jnp.einsum("zxk,xq->zkq", piece[1], cos_x, precision=high) - jnp.einsum(
        "zxk,xq->zkq", piece[0], sin_x, precision=high
    )
    br = spectral[0] * ar - spectral[1] * ai
    bi = spectral[0] * ai + spectral[1] * ar
    gr = jnp.einsum("zkq,qx->zxk", br, cos_x, precision=high) - jnp.einsum(
        "zkq,qx->zxk", bi, sin_x, precision=high
    )
    gi = jnp.einsum("zkq,qx->zxk", bi, cos_x, precision=high) + jnp.einsum(
        "zkq,qx->zxk", br, sin_x, precision=high
    )
    spread = jnp.stack([gr, gi]) / count_x
    rows = lax.all_to_all(spread, "gx", split_axis=2, concat_axis=3, tiled=True)
    inv_re = jnp.dot(rows[0], cos_y, precision=high) - jnp.dot(rows[1], sin_y, precision=high)
    inv_im = jnp.dot(rows[1], cos_y, precision=high) + jnp.dot(rows[0], sin_y, precision=high)
    scattered = jnp.stack([inv_re, inv_im]) / count_y
    return lax.all_to_all(scattered, "gy", split_axis=3, concat_axis=1, tiled=True)


def general_device(incident, material, contrast, w_first, w_middle, w_last, z_kernel, spectral):
    high = lax.Precision.HIGHEST
    classes = contrast.shape[0]
    selector = (material[None] == jnp.arange(classes, dtype=jnp.int32)[:, None, None, None]).astype(
        jnp.float32
    )
    chi_re = jnp.einsum("k,kzxy->zxy", contrast[:, 0], selector, precision=high)
    chi_im = jnp.einsum("k,kzxy->zxy", contrast[:, 1], selector, precision=high)
    field = incident
    pol_re = chi_re * field[0] - chi_im * field[1]
    pol_im = chi_re * field[1] + chi_im * field[0]
    features = jnp.stack([field[0], field[1], pol_re, pol_im]).astype(jnp.bfloat16)
    padded = padded_2(features, (("gx", 2), ("gy", 3)), 3)
    hidden = activate(conv_layer(padded, w_first))
    hidden = activate(conv_layer(hidden, w_middle))
    correction = conv_layer(hidden, w_last)
    source = jnp.stack([pol_re, pol_im]) + correction
    field = incident + green_apply(source, z_kernel, spectral)
    return field


def split(values):
    high = values.astype(BF16)
    low = (values - high.astype(F32)).astype(BF16)
    return high, low


def cosine(steps, length):
    turn = 2.0 * math.pi / length
    angle = (length // 4 - jnp.minimum(steps, length - steps)).astype(F32) * turn
    square = angle * angle
    total = jnp.full_like(angle, 1.0 / math.factorial(13))
    for power in (11, 9, 7, 5, 3, 1):
        sign = 1.0 if power % 4 == 1 else -1.0
        total = total * square + sign / math.factorial(power)
    return total * angle


def dft_parts(rows, cols, length, axis, scale=1.0):
    steps = lax.rem(rows * cols, length)
    later = lax.rem(steps + 3 * length // 4, length)
    high, low = split(jnp.concatenate([cosine(steps, length), cosine(later, length)], axis=axis) * scale)
    return jnp.concatenate([high, high, low], axis=axis)


def left_split(values):
    high, low = split(values)
    return jnp.concatenate([high, low, high], axis=1)


def right_split(values):
    high, low = split(values)
    return jnp.concatenate([high, low, high], axis=0)


def mm(a, b):
    return jnp.dot(a, b, preferred_element_type=F32)


def iota(shape, dim):
    return lax.broadcasted_iota(jnp.int32, shape, dim)


def other_part(values, nz, sign):
    lanes = values.shape[1]
    real = (iota(values.shape, 1) // nz) % 2 == 0
    ahead = pltpu.roll(values, lanes - nz, 1)
    behind = pltpu.roll(values, nz, 1)
    return jnp.where(real, sign * ahead, -sign * behind)


def swap_blocks(ref, count):
    pieces = [ref[:, q, :] for q in range(count)]
    lanes = pieces[0].shape[1]
    inner = lanes // count
    block = iota(pieces[0].shape, 1) // inner
    rows = []
    for x in range(count):
        total = None
        for q in range(count):
            shift = ((q - x) * inner) % lanes
            moved = pltpu.roll(pieces[q], shift, 1) if shift else pieces[q]
            total = moved if total is None else jnp.where(block == q, moved, total)
        rows.append(total)
    return jnp.concatenate(rows, axis=0)


def table_kernel(xl, shift, dft_ref, fwd_ref, inv_ref):
    nx, ny = inv_ref.shape[0], dft_ref.shape[1]
    dft_ref[...] = dft_parts(iota((ny, ny), 0), iota((ny, ny), 1), ny, 0)
    first, second = iota((nx, nx), 0), iota((nx, nx), 1)
    inv_ref[...] = dft_parts(lax.rem(first + shift, nx), second, nx, 1, 1.0 / (nx * ny))
    count = nx // xl
    second = lax.rem(second, count) * xl + second // count
    fwd_ref[...] = dft_parts(first, second, nx, 1)


def banded(spread, place, start):
    rows = jnp.zeros_like(spread[0])
    for a in range(3):
        rows = jnp.where(place == start + a, spread[a], rows)
    return rows.astype(BF16)


def weight_kernel(
    nz, w1_ref, w2_ref, w3_ref, zk_ref, sp_ref, dft_ref,
    t1_ref, t2_ref, t2m_ref, t3_ref, z_ref, sr_ref, si_ref,
):
    hid = w2_ref.shape[3]
    half = nz // 2
    wide = half * hid
    pick = (iota((hid, wide), 0) == iota((hid, wide), 1) % hid).astype(BF16)
    place = iota((hid, wide), 1) // hid
    tall = (half - 1) * hid
    for b in range(3):
        for d in range(3):
            spread = [mm(w2_ref[a, b, d], pick) for a in range(3)]
            for r in range(half):
                block = banded(spread, place, r - 1)
                lanes = slice(b * wide, (b + 1) * wide)
                if r < half - 1:
                    t2_ref[0, d * tall + r * hid : d * tall + (r + 1) * hid, lanes] = block
                if r > 0:
                    t2_ref[1, d * tall + (r - 1) * hid : d * tall + r * hid, lanes] = block
                if 0 < r < 3:
                    top = (d * 2 + r - 1) * hid
                    t2m_ref[top : top + hid, b * 4 * hid : (b + 1) * 4 * hid] = block[:, : 4 * hid]
    channels = w1_ref.shape[3]
    taps, cols = 9 * channels, t1_ref.shape[1]
    pick = (iota((taps, cols), 0) == iota((taps, cols), 1) // nz).astype(BF16)
    spread = []
    for a in range(3):
        stack = jnp.concatenate(
            [w1_ref[a, b, d].astype(F32) for b in range(3) for d in range(3)], axis=0
        ).astype(BF16)
        spread.append(
            lax.dot_general(stack, pick, (((0,), (0,)), ((), ())), preferred_element_type=F32)
        )
    place = iota((hid, cols), 1) % nz
    for z in range(nz):
        t1_ref[z * hid : (z + 1) * hid, :] = banded(spread, place, z - 1)
    rows3, cols3 = t3_ref.shape
    taps = 9 * w3_ref.shape[3]
    repeat = (iota((rows3, taps), 0) // nz == iota((rows3, taps), 1)).astype(BF16)
    pick = (iota((hid, cols3), 0) == iota((hid, cols3), 1) % hid).astype(BF16)
    offset = iota((rows3, cols3), 1) // hid - iota((rows3, cols3), 0) % nz
    spread = []
    for a in range(3):
        stack = jnp.concatenate(
            [w3_ref[a, b, d].astype(F32) for b in range(3) for d in range(3)], axis=0
        ).astype(BF16)
        spread.append(mm(mm(repeat, stack).astype(BF16), pick))
    t3_ref[...] = banded(spread, offset, -1)
    kr, ki = zk_ref[0], zk_ref[1]
    top = jnp.concatenate([kr, -ki], axis=1)
    bottom = jnp.concatenate([ki, kr], axis=1)
    high, low = split(jnp.concatenate([top, bottom, bottom, -top], axis=0))
    z_ref[...] = jnp.concatenate([high, high, low], axis=1)
    count, lanes = sp_ref.shape[1], sr_ref.shape[1]
    pick = (iota((count, lanes), 0) == iota((count, lanes), 1) // (lanes // count)).astype(F32)
    for part, ref in ((0, sr_ref), (1, si_ref)):
        ref[...] = lax.dot_general(
            sp_ref[part],
            pick,
            (((0,), (0,)), ((), ())),
            precision=lax.Precision.HIGHEST,
            preferred_element_type=F32,
        )


def polarised(column, con_ref):
    re, im, cells = column
    chi_re = jnp.zeros_like(re)
    chi_im = jnp.zeros_like(re)
    for k in range(con_ref.shape[1]):
        here = cells == float(k)
        chi_re = jnp.where(here, con_ref[0, k], chi_re)
        chi_im = jnp.where(here, con_ref[1, k], chi_im)
    return re, im, chi_re * re - chi_im * im, chi_re * im + chi_im * re


def gelu(values):
    return 0.5 * values * (1.0 + lax.erf(values * math.sqrt(0.5)))


def corrector_kernel(
    con_ref, own_ref, first_ref, second_ref, t1_ref, t2_ref, t2m_ref, t3_ref, z_ref, dft_ref, out_ref,
    feat, hid1, hid2,
):
    nz, xl, ny = own_ref.shape[1:]
    columns = [(second_ref, x) for x in range(2)]
    columns += [(first_ref, x) for x in range(xl)]
    columns += [(own_ref, x) for x in range(xl)]
    own = []
    depth = 12 * nz
    half = hid1.shape[0] // 2
    hid = 2 * half // nz
    tall = half - hid
    deep = 2 * nz
    last = {}

    def features(place):
        ref, x = columns[place]
        re, im, pol_re, pol_im = polarised([ref[i, :, x, :] for i in range(3)], con_ref)
        if 3 <= place < xl + 3:
            own.append(jnp.concatenate([pol_re, pol_im], axis=0))
        stack = jnp.concatenate([re, im, pol_re, pol_im], axis=0)
        rolled = [pltpu.roll(stack, 1, 1), stack, pltpu.roll(stack, ny - 1, 1)]
        feat[place * depth : (place + 1) * depth, :] = jnp.concatenate(rolled, axis=0).astype(BF16)

    def first_layer(j):
        window = [feat[(j + i) * depth : (j + i + 3) * depth, :] for i in range(2)]
        return mm(t1_ref[...], jnp.concatenate(window, axis=1))

    def first_done(j, made):
        hid1[:, j * ny : (j + 2) * ny] = gelu(made).astype(BF16)

    def tap_sum(weights, top, bottom, j):
        window = [hid1[top:bottom, (j + b) * ny : (j + b + 2) * ny] for b in range(3)]
        made = mm(weights, jnp.concatenate(window, axis=0))
        rows = weights.shape[0] // 3
        sides = []
        for i in range(2):
            lanes = slice(i * ny, (i + 1) * ny)
            sides.append(
                pltpu.roll(made[:rows, lanes], 1, 1)
                + made[rows : 2 * rows, lanes]
                + pltpu.roll(made[2 * rows :, lanes], ny - 1, 1)
            )
        return jnp.concatenate(sides, axis=1)

    def second_layer(j):
        return [
            tap_sum(t2_ref[0], 0, half, j),
            tap_sum(t2m_ref[...], half - 2 * hid, half + 2 * hid, j),
            tap_sum(t2_ref[1], half, 2 * half, j),
        ]

    def second_done(j, made):
        lanes = slice(j * ny, (j + 2) * ny)
        for top, part in zip((0, tall, tall + 2 * hid), made):
            hid2[top : top + part.shape[0], lanes] = gelu(part).astype(BF16)

    def third_layer(j):
        made = mm(t3_ref[...], hid2[:, j * ny : (j + 2) * ny])
        last[j], last[j + 1] = made[:, :ny], made[:, ny:]

    for place in range(4):
        features(place)
    pairs1, pairs2 = range(0, xl + 4, 2), range(0, xl + 2, 2)
    made1, made2 = {}, {}
    for j in pairs1:
        made1[j] = first_layer(j)
        for place in range(j + 4, min(j + 6, xl + 6)):
            features(place)
        if j >= 2:
            first_done(j - 2, made1.pop(j - 2))
    first_done(pairs1[-1], made1.pop(pairs1[-1]))
    for j in pairs2:
        made2[j] = second_layer(j)
        if j >= 2:
            second_done(j - 2, made2.pop(j - 2))
            third_layer(j - 2)
    second_done(pairs2[-1], made2.pop(pairs2[-1]))
    third_layer(pairs2[-1])
    sources = []
    for x in range(xl):
        parts = []
        for d in range(3):
            total = None
            for b in range(3):
                top = (b * 3 + d) * deep
                piece = last[x + b][top : top + deep]
                total = piece if total is None else total + piece
            parts.append(total)
        correction = pltpu.roll(parts[0], 1, 1) + parts[1] + pltpu.roll(parts[2], ny - 1, 1)
        sources.append(own[x] + correction)
    lifted = mm(z_ref[...], right_split(jnp.concatenate(sources, axis=1)))
    plain = [lifted[:deep, x * ny : (x + 1) * ny] for x in range(xl)]
    turned = [lifted[deep:, x * ny : (x + 1) * ny] for x in range(xl)]
    both = jnp.concatenate([jnp.concatenate(plain, axis=0), jnp.concatenate(turned, axis=0)], axis=1)
    spectrum = mm(left_split(both), dft_ref[...])
    out_ref[...] = jnp.transpose(spectrum).reshape(out_ref.shape)


def spectral_kernel(nz, in_ref, fwd_ref, inv_ref, sr_ref, si_ref, out_ref):
    values = swap_blocks(in_ref, in_ref.shape[1])
    both = jnp.concatenate([values, other_part(values, nz, 1.0)], axis=0)
    spectrum = mm(fwd_ref[...], right_split(both))
    scaled = sr_ref[...] * spectrum + si_ref[...] * other_part(spectrum, nz, -1.0)
    both = jnp.concatenate([scaled, other_part(scaled, nz, -1.0)], axis=0)
    out_ref[...] = mm(inv_ref[...], right_split(both)).reshape(out_ref.shape)


def finish_kernel(nz, in_ref, tab_ref, inc_ref, out_ref):
    values = swap_blocks(in_ref, in_ref.shape[1])
    both = jnp.concatenate([values, other_part(values, nz, -1.0)], axis=0)
    field = jnp.transpose(mm(tab_ref[...], right_split(both)))
    for x in range(inc_ref.shape[2]):
        for part in range(2):
            first = (2 * x + part) * nz
            out_ref[part, :, x, :] = inc_ref[part, :, x, :] + field[first : first + nz, :]


def call(kernel, out_shapes, args, scratch=(), smem=(), flops=0):
    vmem = pl.BlockSpec(memory_space=pltpu.VMEM)
    specs = [vmem] * len(args)
    for i in smem:
        specs[i] = pl.BlockSpec(memory_space=pltpu.SMEM)
    single = not isinstance(out_shapes, list)
    return pl.pallas_call(
        kernel,
        out_shape=out_shapes,
        in_specs=specs,
        out_specs=vmem if single else [vmem] * len(out_shapes),
        scratch_shapes=scratch,
        compiler_params=pltpu.CompilerParams(vmem_limit_bytes=VMEM_LIMIT),
        cost_estimate=pl.CostEstimate(flops=flops, bytes_accessed=4 * 1024 * 1024, transcendentals=0),
    )(*args)


def lane_device(incident, material, contrast, w_first, w_middle, w_last, z_kernel, spectral):
    count = lax.axis_size("gx")
    nz, xl, ny = material.shape
    hid = w_middle.shape[0]
    ql, nx = spectral.shape[1], spectral.shape[2]
    struct = jax.ShapeDtypeStruct
    still = ((0, 0),) * 3
    own = jnp.pad(material[None], ((2, 0),) + still).astype(F32) + jnp.pad(incident, ((0, 1),) + still)
    second = lax.ppermute(own[:, :, xl - 2 :], "gx", [(i, (i + 2) % count) for i in range(count)])
    first = lax.ppermute(own, "gx", [(i, (i + 1) % count) for i in range(count)])
    lanes = 2 * nz * xl
    dft, fwd, inv = call(
        functools.partial(table_kernel, xl, 3),
        [struct((6 * ny, ny), BF16), struct((nx, 6 * nx), BF16), struct((nx, 6 * nx), BF16)],
        (),
        flops=10**9,
    )
    t1, t2, t2m, t3, zmat, sr, si = call(
        functools.partial(weight_kernel, nz),
        [
            struct((nz * hid, 36 * nz), BF16),
            struct((2, 3 * (nz // 2 - 1) * hid, 3 * nz // 2 * hid), BF16),
            struct((6 * hid, 12 * hid), BF16),
            struct((18 * nz, nz * hid), BF16),
            struct((4 * nz, 6 * nz), BF16),
            struct((nx, ql * 2 * nz), F32),
            struct((nx, ql * 2 * nz), F32),
        ],
        (
            jnp.transpose(w_first, (2, 3, 4, 1, 0)),
            jnp.transpose(w_middle, (2, 3, 4, 0, 1)),
            jnp.transpose(w_last, (2, 3, 4, 0, 1)),
            z_kernel,
            spectral,
            dft,
        ),
        flops=10**9,
    )
    spectrum = call(
        corrector_kernel,
        struct((count, ql, lanes), F32),
        (jnp.transpose(contrast), own, first, second, t1, t2, t2m, t3, zmat, dft),
        scratch=[
            pltpu.VMEM(((xl + 6) * 12 * nz, ny), BF16),
            pltpu.VMEM((nz * hid, (xl + 4) * ny), BF16),
            pltpu.VMEM((nz * hid, (xl + 2) * ny), BF16),
        ],
        smem=(0,),
        flops=10**9,
    )
    piece = lax.all_to_all(spectrum, "gx", 0, 0, tiled=True)
    spread = call(
        functools.partial(spectral_kernel, nz),
        struct((count, xl, lanes), F32),
        (piece, fwd, inv, sr, si),
        flops=10**8,
    )
    rows = lax.all_to_all(spread, "gx", 0, 0, tiled=True)
    return call(
        functools.partial(finish_kernel, nz),
        struct(incident.shape, F32),
        (rows, fwd, own),
        flops=10**8,
    )


def per_device(incident, material, contrast, w_first, w_middle, w_last, z_kernel, spectral):
    nz, xl, ny = material.shape
    ql, nx = spectral.shape[1], spectral.shape[2]
    lanes = (
        lax.axis_size("gy") == 1
        and ny == 128
        and nx == 128
        and xl == 4
        and ql == 4
        and 2 * nz * xl == 128
        and w_middle.shape[0] == 32
    )
    device = lane_device if lanes else general_device
    return device(incident, material, contrast, w_first, w_middle, w_last, z_kernel, spectral)


def solution(mesh):
    placed = (
        P("grp", None, "gx", "gy"),
        P("grp", "gx", "gy"),
        P("grp", None),
        P(),
        P(),
        P(),
        P("grp", None, None),
        P("grp", "gx", None),
    )
    return jax.shard_map(
        per_device,
        mesh=mesh,
        in_specs=placed,
        out_specs=P("grp", None, "gx", "gy"),
        check_vma=False,
    )
```

```python
import functools
import math

import jax
import jax.numpy as jnp
from jax import lax
from jax.experimental import pallas as pl
from jax.experimental.pallas import tpu as pltpu
from jax.sharding import PartitionSpec as P

F32 = jnp.float32
BF16 = jnp.bfloat16
VMEM_LIMIT = 48 * 1024 * 1024


def padded_2(x, sides, width):
    for axis, dim in sides:
        count, length = (lax.axis_size(axis), x.shape[dim])
        up = [(i, (i + 1) % count) for i in range(count)]
        down = [(j, i) for i, j in up]
        last = lax.slice_in_dim(x, length - width, length, axis=dim)
        leading = lax.slice_in_dim(x, 0, width, axis=dim)
        before = lax.ppermute(last, axis, up)
        after = lax.ppermute(leading, axis, down)
        x = jnp.concatenate([before, x, after], axis=dim)
    return x


def conv_layer(values, weights):
    return lax.conv_general_dilated(
        values[None],
        weights,
        (1, 1, 1),
        ((1, 1), (0, 0), (0, 0)),
        dimension_numbers=("NCDHW", "OIDHW", "NCDHW"),
        preferred_element_type=jnp.float32,
    )[0]


def activate(values):
    return jax.nn.gelu(values, approximate=False).astype(jnp.bfloat16)


def dft_tables(length):
    positions = jnp.arange(length, dtype=jnp.int32)
    product = positions[:, None] * positions[None, :] % length
    angle = product.astype(jnp.float32) * (2.0 * math.pi / length)
    return (jnp.cos(angle), jnp.sin(angle))


def green_apply(source, z_kernel, spectral):
    high = lax.Precision.HIGHEST
    kr, ki = (z_kernel[0], z_kernel[1])
    lre = jnp.einsum("zw,wxy->zxy", kr, source[0], precision=high) - jnp.einsum(
        "zw,wxy->zxy", ki, source[1], precision=high
    )
    lim = jnp.einsum("zw,wxy->zxy", kr, source[1], precision=high) + jnp.einsum(
        "zw,wxy->zxy", ki, source[0], precision=high
    )
    columns = lax.all_to_all(jnp.stack([lre, lim]), "gy", split_axis=1, concat_axis=3, tiled=True)
    count_y = columns.shape[3]
    cos_y, sin_y = dft_tables(count_y)
    fwd_re = jnp.dot(columns[0], cos_y, precision=high) + jnp.dot(columns[1], sin_y, precision=high)
    fwd_im = jnp.dot(columns[1], cos_y, precision=high) - jnp.dot(columns[0], sin_y, precision=high)
    count_x = columns.shape[2] * lax.axis_size("gx")
    cos_x, sin_x = dft_tables(count_x)
    piece = lax.all_to_all(
        jnp.stack([fwd_re, fwd_im]), "gx", split_axis=3, concat_axis=2, tiled=True
    )
    ar = jnp.einsum("zxk,xq->zkq", piece[0], cos_x, precision=high) + jnp.einsum(
        "zxk,xq->zkq", piece[1], sin_x, precision=high
    )
    ai = jnp.einsum("zxk,xq->zkq", piece[1], cos_x, precision=high) - jnp.einsum(
        "zxk,xq->zkq", piece[0], sin_x, precision=high
    )
    br = spectral[0] * ar - spectral[1] * ai
    bi = spectral[0] * ai + spectral[1] * ar
    gr = jnp.einsum("zkq,qx->zxk", br, cos_x, precision=high) - jnp.einsum(
        "zkq,qx->zxk", bi, sin_x, precision=high
    )
    gi = jnp.einsum("zkq,qx->zxk", bi, cos_x, precision=high) + jnp.einsum(
        "zkq,qx->zxk", br, sin_x, precision=high
    )
    spread = jnp.stack([gr, gi]) / count_x
    rows = lax.all_to_all(spread, "gx", split_axis=2, concat_axis=3, tiled=True)
    inv_re = jnp.dot(rows[0], cos_y, precision=high) - jnp.dot(rows[1], sin_y, precision=high)
    inv_im = jnp.dot(rows[1], cos_y, precision=high) + jnp.dot(rows[0], sin_y, precision=high)
    scattered = jnp.stack([inv_re, inv_im]) / count_y
    return lax.all_to_all(scattered, "gy", split_axis=3, concat_axis=1, tiled=True)


def general_device(incident, material, contrast, w_first, w_middle, w_last, z_kernel, spectral):
    high = lax.Precision.HIGHEST
    classes = contrast.shape[0]
    selector = (material[None] == jnp.arange(classes, dtype=jnp.int32)[:, None, None, None]).astype(
        jnp.float32
    )
    chi_re = jnp.einsum("k,kzxy->zxy", contrast[:, 0], selector, precision=high)
    chi_im = jnp.einsum("k,kzxy->zxy", contrast[:, 1], selector, precision=high)
    field = incident
    pol_re = chi_re * field[0] - chi_im * field[1]
    pol_im = chi_re * field[1] + chi_im * field[0]
    features = jnp.stack([field[0], field[1], pol_re, pol_im]).astype(jnp.bfloat16)
    padded = padded_2(features, (("gx", 2), ("gy", 3)), 3)
    hidden = activate(conv_layer(padded, w_first))
    hidden = activate(conv_layer(hidden, w_middle))
    correction = conv_layer(hidden, w_last)
    source = jnp.stack([pol_re, pol_im]) + correction
    field = incident + green_apply(source, z_kernel, spectral)
    return field


def split(values):
    high = values.astype(BF16)
    low = (values - high.astype(F32)).astype(BF16)
    return high, low


def cosine(steps, length):
    turn = 2.0 * math.pi / length
    angle = (length // 4 - jnp.minimum(steps, length - steps)).astype(F32) * turn
    square = angle * angle
    total = jnp.full_like(angle, 1.0 / math.factorial(13))
    for power in (11, 9, 7, 5, 3, 1):
        sign = 1.0 if power % 4 == 1 else -1.0
        total = total * square + sign / math.factorial(power)
    return total * angle


def dft_parts(rows, cols, length, axis, scale=1.0):
    steps = lax.rem(rows * cols, length)
    later = lax.rem(steps + 3 * length // 4, length)
    high, low = split(jnp.concatenate([cosine(steps, length), cosine(later, length)], axis=axis) * scale)
    return jnp.concatenate([high, high, low], axis=axis)


def left_split(values):
    high, low = split(values)
    return jnp.concatenate([high, low, high], axis=1)


def right_split(values):
    high, low = split(values)
    return jnp.concatenate([high, low, high], axis=0)


def mm(a, b):
    return jnp.dot(a, b, preferred_element_type=F32)


def iota(shape, dim):
    return lax.broadcasted_iota(jnp.int32, shape, dim)


def other_part(values, nz, sign):
    lanes = values.shape[1]
    real = (iota(values.shape, 1) // nz) % 2 == 0
    ahead = pltpu.roll(values, lanes - nz, 1)
    behind = pltpu.roll(values, nz, 1)
    return jnp.where(real, sign * ahead, -sign * behind)


def swap_blocks(ref, count):
    pieces = [ref[:, q, :] for q in range(count)]
    lanes = pieces[0].shape[1]
    inner = lanes // count
    block = iota(pieces[0].shape, 1) // inner
    rows = []
    for x in range(count):
        total = None
        for q in range(count):
            shift = ((q - x) * inner) % lanes
            moved = pltpu.roll(pieces[q], shift, 1) if shift else pieces[q]
            total = moved if total is None else jnp.where(block == q, moved, total)
        rows.append(total)
    return jnp.concatenate(rows, axis=0)


def pack_kernel(own_ref, planes_ref, whole_ref):
    xl = own_ref.shape[2]
    for x in range(xl):
        for i in range(3):
            values = own_ref[i, :, x, :]
            high, low = split(values)
            planes_ref[3 * x + i] = values
            whole_ref[3 * x + i] = high
            if x > 0 and i < 2:
                whole_ref[3 * xl + 2 * (x - 1) + i] = low


def near_kernel(whole_ref, near_ref):
    count = near_ref.shape[0]
    top = 3 * (whole_ref.shape[0] + 2) // 5 - count
    near_ref[...] = whole_ref[top : top + count]


def table_kernel(xl, shift, dft_ref, fwd_ref, inv_ref):
    nx, ny = inv_ref.shape[0], dft_ref.shape[1]
    dft_ref[...] = dft_parts(iota((ny, ny), 0), iota((ny, ny), 1), ny, 0)
    first, second = iota((nx, nx), 0), iota((nx, nx), 1)
    inv_ref[...] = dft_parts(lax.rem(first + shift, nx), second, nx, 1, 1.0 / (nx * ny))
    count = nx // xl
    second = lax.rem(second, count) * xl + second // count
    fwd_ref[...] = dft_parts(first, second, nx, 1)


def banded(spread, place, start):
    rows = jnp.zeros_like(spread[0])
    for a in range(3):
        rows = jnp.where(place == start + a, spread[a], rows)
    return rows.astype(BF16)


def weight_kernel(
    nz, w1_ref, w2_ref, w3_ref, zk_ref, sp_ref, dft_ref,
    t1_ref, t2_ref, t2m_ref, t3_ref, z_ref, sr_ref, si_ref,
):
    hid = w2_ref.shape[3]
    half = nz // 2
    wide = half * hid
    pick = (iota((hid, wide), 0) == iota((hid, wide), 1) % hid).astype(BF16)
    place = iota((hid, wide), 1) // hid
    tall = (half - 1) * hid
    for b in range(3):
        for d in range(3):
            spread = [mm(w2_ref[a, b, d], pick) for a in range(3)]
            for r in range(half):
                block = banded(spread, place, r - 1)
                lanes = slice(b * wide, (b + 1) * wide)
                if r < half - 1:
                    t2_ref[0, d * tall + r * hid : d * tall + (r + 1) * hid, lanes] = block
                if r > 0:
                    t2_ref[1, d * tall + (r - 1) * hid : d * tall + r * hid, lanes] = block
                if 0 < r < 3:
                    top = (d * 2 + r - 1) * hid
                    t2m_ref[top : top + hid, b * 4 * hid : (b + 1) * 4 * hid] = block[:, : 4 * hid]
    channels = w1_ref.shape[3]
    taps, cols = 9 * channels, t1_ref.shape[1]
    pick = (iota((taps, cols), 0) == iota((taps, cols), 1) // nz).astype(BF16)
    spread = []
    for a in range(3):
        stack = jnp.concatenate(
            [w1_ref[a, b, d].astype(F32) for b in range(3) for d in range(3)], axis=0
        ).astype(BF16)
        spread.append(
            lax.dot_general(stack, pick, (((0,), (0,)), ((), ())), preferred_element_type=F32)
        )
    place = iota((hid, cols), 1) % nz
    for z in range(nz):
        t1_ref[z * hid : (z + 1) * hid, :] = banded(spread, place, z - 1)
    rows3, cols3 = t3_ref.shape
    taps = 9 * w3_ref.shape[3]
    repeat = (iota((rows3, taps), 0) // nz == iota((rows3, taps), 1)).astype(BF16)
    pick = (iota((hid, cols3), 0) == iota((hid, cols3), 1) % hid).astype(BF16)
    offset = iota((rows3, cols3), 1) // hid - iota((rows3, cols3), 0) % nz
    spread = []
    for a in range(3):
        stack = jnp.concatenate(
            [w3_ref[a, b, d].astype(F32) for b in range(3) for d in range(3)], axis=0
        ).astype(BF16)
        spread.append(mm(mm(repeat, stack).astype(BF16), pick))
    t3_ref[...] = banded(spread, offset, -1)
    kr, ki = zk_ref[0], zk_ref[1]
    top = jnp.concatenate([kr, -ki], axis=1)
    bottom = jnp.concatenate([ki, kr], axis=1)
    high, low = split(jnp.concatenate([top, bottom, bottom, -top], axis=0))
    z_ref[...] = jnp.concatenate([high, high, low], axis=1)
    count, lanes = sp_ref.shape[1], sr_ref.shape[1]
    pick = (iota((count, lanes), 0) == iota((count, lanes), 1) // (lanes // count)).astype(F32)
    for part, ref in ((0, sr_ref), (1, si_ref)):
        ref[...] = lax.dot_general(
            sp_ref[part],
            pick,
            (((0,), (0,)), ((), ())),
            precision=lax.Precision.HIGHEST,
            preferred_element_type=F32,
        )


def polarised(column, con_ref):
    re, im, cells = column
    chi_re = jnp.zeros_like(re)
    chi_im = jnp.zeros_like(re)
    for k in range(con_ref.shape[1]):
        here = cells == float(k)
        chi_re = jnp.where(here, con_ref[0, k], chi_re)
        chi_im = jnp.where(here, con_ref[1, k], chi_im)
    return re, im, chi_re * re - chi_im * im, chi_re * im + chi_im * re


def gelu(values):
    return 0.5 * values * (1.0 + lax.erf(values * math.sqrt(0.5)))


def corrector_kernel(
    con_ref, own_ref, first_ref, second_ref, t1_ref, t2_ref, t2m_ref, t3_ref, z_ref, dft_ref, out_ref,
    feat, hid1, hid2,
):
    nz, ny = own_ref.shape[1:]
    xl = own_ref.shape[0] // 3
    columns = [[second_ref[3 * x + i].astype(F32) for i in range(3)] for x in range(2)]
    columns += [[first_ref[3 * x + i].astype(F32) for i in range(3)] for x in range(xl)]
    columns += [[own_ref[3 * x + i] for i in range(3)] for x in range(xl)]
    for x in range(1, xl):
        for i in range(2):
            columns[x + 2][i] += first_ref[3 * xl + 2 * (x - 1) + i].astype(F32)
    own = []
    depth = 12 * nz
    half = hid1.shape[0] // 2
    hid = 2 * half // nz
    tall = half - hid
    deep = 2 * nz
    last = {}

    def features(place):
        re, im, pol_re, pol_im = polarised(columns[place], con_ref)
        if 3 <= place < xl + 3:
            own.append(jnp.concatenate([pol_re, pol_im], axis=0))
        stack = jnp.concatenate([re, im, pol_re, pol_im], axis=0)
        rolled = [pltpu.roll(stack, 1, 1), stack, pltpu.roll(stack, ny - 1, 1)]
        feat[place * depth : (place + 1) * depth, :] = jnp.concatenate(rolled, axis=0).astype(BF16)

    def first_layer(j):
        window = [feat[(j + i) * depth : (j + i + 3) * depth, :] for i in range(2)]
        return mm(t1_ref[...], jnp.concatenate(window, axis=1))

    def first_done(j, made):
        hid1[:, j * ny : (j + 2) * ny] = gelu(made).astype(BF16)

    def tap_sum(weights, top, bottom, j):
        window = [hid1[top:bottom, (j + b) * ny : (j + b + 2) * ny] for b in range(3)]
        made = mm(weights, jnp.concatenate(window, axis=0))
        rows = weights.shape[0] // 3
        sides = []
        for i in range(2):
            lanes = slice(i * ny, (i + 1) * ny)
            sides.append(
                pltpu.roll(made[:rows, lanes], 1, 1)
                + made[rows : 2 * rows, lanes]
                + pltpu.roll(made[2 * rows :, lanes], ny - 1, 1)
            )
        return jnp.concatenate(sides, axis=1)

    def second_layer(j):
        return [
            tap_sum(t2_ref[0], 0, half, j),
            tap_sum(t2m_ref[...], half - 2 * hid, half + 2 * hid, j),
            tap_sum(t2_ref[1], half, 2 * half, j),
        ]

    def second_done(j, made):
        lanes = slice(j * ny, (j + 2) * ny)
        for top, part in zip((0, tall, tall + 2 * hid), made):
            hid2[top : top + part.shape[0], lanes] = gelu(part).astype(BF16)

    def third_layer(j):
        made = mm(t3_ref[...], hid2[:, j * ny : (j + 2) * ny])
        last[j], last[j + 1] = made[:, :ny], made[:, ny:]

    for place in range(4):
        features(place)
    pairs1, pairs2 = range(0, xl + 4, 2), range(0, xl + 2, 2)
    made1, made2 = {}, {}
    for j in pairs1:
        made1[j] = first_layer(j)
        for place in range(j + 4, min(j + 6, xl + 6)):
            features(place)
        if j >= 2:
            first_done(j - 2, made1.pop(j - 2))
    first_done(pairs1[-1], made1.pop(pairs1[-1]))
    for j in pairs2:
        made2[j] = second_layer(j)
        if j >= 2:
            second_done(j - 2, made2.pop(j - 2))
            third_layer(j - 2)
    second_done(pairs2[-1], made2.pop(pairs2[-1]))
    third_layer(pairs2[-1])
    sources = []
    for x in range(xl):
        parts = []
        for d in range(3):
            total = None
            for b in range(3):
                top = (b * 3 + d) * deep
                piece = last[x + b][top : top + deep]
                total = piece if total is None else total + piece
            parts.append(total)
        correction = pltpu.roll(parts[0], 1, 1) + parts[1] + pltpu.roll(parts[2], ny - 1, 1)
        sources.append(own[x] + correction)
    lifted = mm(z_ref[...], right_split(jnp.concatenate(sources, axis=1)))
    plain = [lifted[:deep, x * ny : (x + 1) * ny] for x in range(xl)]
    turned = [lifted[deep:, x * ny : (x + 1) * ny] for x in range(xl)]
    both = jnp.concatenate([jnp.concatenate(plain, axis=0), jnp.concatenate(turned, axis=0)], axis=1)
    spectrum = mm(left_split(both), dft_ref[...])
    out_ref[...] = jnp.transpose(spectrum).reshape(out_ref.shape)


def spectral_kernel(nz, in_ref, fwd_ref, inv_ref, sr_ref, si_ref, out_ref):
    values = swap_blocks(in_ref, in_ref.shape[1])
    both = jnp.concatenate([values, other_part(values, nz, 1.0)], axis=0)
    spectrum = mm(fwd_ref[...], right_split(both))
    scaled = sr_ref[...] * spectrum + si_ref[...] * other_part(spectrum, nz, -1.0)
    both = jnp.concatenate([scaled, other_part(scaled, nz, -1.0)], axis=0)
    out_ref[...] = mm(inv_ref[...], right_split(both)).reshape(out_ref.shape)


def finish_kernel(nz, in_ref, tab_ref, inc_ref, out_ref):
    values = swap_blocks(in_ref, in_ref.shape[1])
    both = jnp.concatenate([values, other_part(values, nz, -1.0)], axis=0)
    field = jnp.transpose(mm(tab_ref[...], right_split(both)))
    for x in range(inc_ref.shape[2]):
        for part in range(2):
            first = (2 * x + part) * nz
            out_ref[part, :, x, :] = inc_ref[part, :, x, :] + field[first : first + nz, :]


def call(kernel, out_shapes, args, scratch=(), smem=(), flops=0):
    vmem = pl.BlockSpec(memory_space=pltpu.VMEM)
    specs = [vmem] * len(args)
    for i in smem:
        specs[i] = pl.BlockSpec(memory_space=pltpu.SMEM)
    single = not isinstance(out_shapes, list)
    return pl.pallas_call(
        kernel,
        out_shape=out_shapes,
        in_specs=specs,
        out_specs=vmem if single else [vmem] * len(out_shapes),
        scratch_shapes=scratch,
        compiler_params=pltpu.CompilerParams(vmem_limit_bytes=VMEM_LIMIT),
        cost_estimate=pl.CostEstimate(flops=flops, bytes_accessed=4 * 1024 * 1024, transcendentals=0),
    )(*args)


def lane_device(incident, material, contrast, w_first, w_middle, w_last, z_kernel, spectral):
    count = lax.axis_size("gx")
    nz, xl, ny = material.shape
    hid = w_middle.shape[0]
    ql, nx = spectral.shape[1], spectral.shape[2]
    struct = jax.ShapeDtypeStruct
    still = ((0, 0),) * 3
    own = jnp.pad(material[None], ((2, 0),) + still).astype(F32) + jnp.pad(incident, ((0, 1),) + still)
    planes, whole = call(
        pack_kernel,
        [struct((3 * xl, nz, ny), F32), struct((5 * xl - 2, nz, ny), BF16)],
        (own,),
        flops=10**6,
    )
    near = call(near_kernel, struct((6, nz, ny), BF16), (whole,), flops=10**6)
    first = lax.ppermute(whole, "gx", [(i, (i + 1) % count) for i in range(count)])
    second = lax.ppermute(near, "gx", [(i, (i + 2) % count) for i in range(count)])
    lanes = 2 * nz * xl
    dft, fwd, inv = call(
        functools.partial(table_kernel, xl, 3),
        [struct((6 * ny, ny), BF16), struct((nx, 6 * nx), BF16), struct((nx, 6 * nx), BF16)],
        (),
        flops=10**9,
    )
    t1, t2, t2m, t3, zmat, sr, si = call(
        functools.partial(weight_kernel, nz),
        [
            struct((nz * hid, 36 * nz), BF16),
            struct((2, 3 * (nz // 2 - 1) * hid, 3 * nz // 2 * hid), BF16),
            struct((6 * hid, 12 * hid), BF16),
            struct((18 * nz, nz * hid), BF16),
            struct((4 * nz, 6 * nz), BF16),
            struct((nx, ql * 2 * nz), F32),
            struct((nx, ql * 2 * nz), F32),
        ],
        (
            jnp.transpose(w_first, (2, 3, 4, 1, 0)),
            jnp.transpose(w_middle, (2, 3, 4, 0, 1)),
            jnp.transpose(w_last, (2, 3, 4, 0, 1)),
            z_kernel,
            spectral,
            dft,
        ),
        flops=10**9,
    )
    spectrum = call(
        corrector_kernel,
        struct((count, ql, lanes), F32),
        (jnp.transpose(contrast), planes, first, second, t1, t2, t2m, t3, zmat, dft),
        scratch=[
            pltpu.VMEM(((xl + 6) * 12 * nz, ny), BF16),
            pltpu.VMEM((nz * hid, (xl + 4) * ny), BF16),
            pltpu.VMEM((nz * hid, (xl + 2) * ny), BF16),
        ],
        smem=(0,),
        flops=10**9,
    )
    piece = lax.all_to_all(spectrum, "gx", 0, 0, tiled=True)
    spread = call(
        functools.partial(spectral_kernel, nz),
        struct((count, xl, lanes), F32),
        (piece, fwd, inv, sr, si),
        flops=10**8,
    )
    rows = lax.all_to_all(spread, "gx", 0, 0, tiled=True)
    return call(
        functools.partial(finish_kernel, nz),
        struct(incident.shape, F32),
        (rows, fwd, own),
        flops=10**8,
    )


def per_device(incident, material, contrast, w_first, w_middle, w_last, z_kernel, spectral):
    nz, xl, ny = material.shape
    ql, nx = spectral.shape[1], spectral.shape[2]
    lanes = (
        lax.axis_size("gy") == 1
        and ny == 128
        and nx == 128
        and xl == 4
        and ql == 4
        and 2 * nz * xl == 128
        and w_middle.shape[0] == 32
    )
    device = lane_device if lanes else general_device
    return device(incident, material, contrast, w_first, w_middle, w_last, z_kernel, spectral)


def solution(mesh):
    placed = (
        P("grp", None, "gx", "gy"),
        P("grp", "gx", "gy"),
        P("grp", None),
        P(),
        P(),
        P(),
        P("grp", None, None),
        P("grp", "gx", None),
    )
    return jax.shard_map(
        per_device,
        mesh=mesh,
        in_specs=placed,
        out_specs=P("grp", None, "gx", "gy"),
        check_vma=False,
    )
```

```python
import functools
import math

import jax
import jax.numpy as jnp
from jax import lax
from jax.experimental import pallas as pl
from jax.experimental.pallas import tpu as pltpu
from jax.sharding import PartitionSpec as P

F32 = jnp.float32
BF16 = jnp.bfloat16
VMEM_LIMIT = 48 * 1024 * 1024


def padded_2(x, sides, width):
    for axis, dim in sides:
        count, length = (lax.axis_size(axis), x.shape[dim])
        up = [(i, (i + 1) % count) for i in range(count)]
        down = [(j, i) for i, j in up]
        last = lax.slice_in_dim(x, length - width, length, axis=dim)
        leading = lax.slice_in_dim(x, 0, width, axis=dim)
        before = lax.ppermute(last, axis, up)
        after = lax.ppermute(leading, axis, down)
        x = jnp.concatenate([before, x, after], axis=dim)
    return x


def conv_layer(values, weights):
    return lax.conv_general_dilated(
        values[None],
        weights,
        (1, 1, 1),
        ((1, 1), (0, 0), (0, 0)),
        dimension_numbers=("NCDHW", "OIDHW", "NCDHW"),
        preferred_element_type=jnp.float32,
    )[0]


def activate(values):
    return jax.nn.gelu(values, approximate=False).astype(jnp.bfloat16)


def dft_tables(length):
    positions = jnp.arange(length, dtype=jnp.int32)
    product = positions[:, None] * positions[None, :] % length
    angle = product.astype(jnp.float32) * (2.0 * math.pi / length)
    return (jnp.cos(angle), jnp.sin(angle))


def green_apply(source, z_kernel, spectral):
    high = lax.Precision.HIGHEST
    kr, ki = (z_kernel[0], z_kernel[1])
    lre = jnp.einsum("zw,wxy->zxy", kr, source[0], precision=high) - jnp.einsum(
        "zw,wxy->zxy", ki, source[1], precision=high
    )
    lim = jnp.einsum("zw,wxy->zxy", kr, source[1], precision=high) + jnp.einsum(
        "zw,wxy->zxy", ki, source[0], precision=high
    )
    columns = lax.all_to_all(jnp.stack([lre, lim]), "gy", split_axis=1, concat_axis=3, tiled=True)
    count_y = columns.shape[3]
    cos_y, sin_y = dft_tables(count_y)
    fwd_re = jnp.dot(columns[0], cos_y, precision=high) + jnp.dot(columns[1], sin_y, precision=high)
    fwd_im = jnp.dot(columns[1], cos_y, precision=high) - jnp.dot(columns[0], sin_y, precision=high)
    count_x = columns.shape[2] * lax.axis_size("gx")
    cos_x, sin_x = dft_tables(count_x)
    piece = lax.all_to_all(
        jnp.stack([fwd_re, fwd_im]), "gx", split_axis=3, concat_axis=2, tiled=True
    )
    ar = jnp.einsum("zxk,xq->zkq", piece[0], cos_x, precision=high) + jnp.einsum(
        "zxk,xq->zkq", piece[1], sin_x, precision=high
    )
    ai = jnp.einsum("zxk,xq->zkq", piece[1], cos_x, precision=high) - jnp.einsum(
        "zxk,xq->zkq", piece[0], sin_x, precision=high
    )
    br = spectral[0] * ar - spectral[1] * ai
    bi = spectral[0] * ai + spectral[1] * ar
    gr = jnp.einsum("zkq,qx->zxk", br, cos_x, precision=high) - jnp.einsum(
        "zkq,qx->zxk", bi, sin_x, precision=high
    )
    gi = jnp.einsum("zkq,qx->zxk", bi, cos_x, precision=high) + jnp.einsum(
        "zkq,qx->zxk", br, sin_x, precision=high
    )
    spread = jnp.stack([gr, gi]) / count_x
    rows = lax.all_to_all(spread, "gx", split_axis=2, concat_axis=3, tiled=True)
    inv_re = jnp.dot(rows[0], cos_y, precision=high) - jnp.dot(rows[1], sin_y, precision=high)
    inv_im = jnp.dot(rows[1], cos_y, precision=high) + jnp.dot(rows[0], sin_y, precision=high)
    scattered = jnp.stack([inv_re, inv_im]) / count_y
    return lax.all_to_all(scattered, "gy", split_axis=3, concat_axis=1, tiled=True)


def general_device(incident, material, contrast, w_first, w_middle, w_last, z_kernel, spectral):
    high = lax.Precision.HIGHEST
    classes = contrast.shape[0]
    selector = (material[None] == jnp.arange(classes, dtype=jnp.int32)[:, None, None, None]).astype(
        jnp.float32
    )
    chi_re = jnp.einsum("k,kzxy->zxy", contrast[:, 0], selector, precision=high)
    chi_im = jnp.einsum("k,kzxy->zxy", contrast[:, 1], selector, precision=high)
    field = incident
    pol_re = chi_re * field[0] - chi_im * field[1]
    pol_im = chi_re * field[1] + chi_im * field[0]
    features = jnp.stack([field[0], field[1], pol_re, pol_im]).astype(jnp.bfloat16)
    padded = padded_2(features, (("gx", 2), ("gy", 3)), 3)
    hidden = activate(conv_layer(padded, w_first))
    hidden = activate(conv_layer(hidden, w_middle))
    correction = conv_layer(hidden, w_last)
    source = jnp.stack([pol_re, pol_im]) + correction
    field = incident + green_apply(source, z_kernel, spectral)
    return field


def split(values):
    high = values.astype(BF16)
    low = (values - high.astype(F32)).astype(BF16)
    return high, low


def cosine(steps, length):
    turn = 2.0 * math.pi / length
    angle = (length // 4 - jnp.minimum(steps, length - steps)).astype(F32) * turn
    square = angle * angle
    total = jnp.full_like(angle, 1.0 / math.factorial(13))
    for power in (11, 9, 7, 5, 3, 1):
        sign = 1.0 if power % 4 == 1 else -1.0
        total = total * square + sign / math.factorial(power)
    return total * angle


def dft_parts(rows, cols, length, axis, scale=1.0):
    steps = lax.rem(rows * cols, length)
    later = lax.rem(steps + 3 * length // 4, length)
    high, low = split(jnp.concatenate([cosine(steps, length), cosine(later, length)], axis=axis) * scale)
    return jnp.concatenate([high, high, low], axis=axis)


def left_split(values):
    high, low = split(values)
    return jnp.concatenate([high, low, high], axis=1)


def right_split(values):
    high, low = split(values)
    return jnp.concatenate([high, low, high], axis=0)


def mm(a, b):
    return jnp.dot(a, b, preferred_element_type=F32)


def iota(shape, dim):
    return lax.broadcasted_iota(jnp.int32, shape, dim)


def other_part(values, nz, sign):
    lanes = values.shape[1]
    real = (iota(values.shape, 1) // nz) % 2 == 0
    ahead = pltpu.roll(values, lanes - nz, 1)
    behind = pltpu.roll(values, nz, 1)
    return jnp.where(real, sign * ahead, -sign * behind)


def swap_blocks(ref, count):
    pieces = [ref[:, q, :] for q in range(count)]
    lanes = pieces[0].shape[1]
    inner = lanes // count
    block = iota(pieces[0].shape, 1) // inner
    rows = []
    for x in range(count):
        total = None
        for q in range(count):
            shift = ((q - x) * inner) % lanes
            moved = pltpu.roll(pieces[q], shift, 1) if shift else pieces[q]
            total = moved if total is None else jnp.where(block == q, moved, total)
        rows.append(total)
    return jnp.concatenate(rows, axis=0)


def spread_classes(con_ref, shape):
    return [
        [jnp.broadcast_to(con_ref[part : part + 1, k : k + 1], shape) for part in range(2)]
        for k in range(con_ref.shape[1])
    ]


def polarised(column, classes):
    re, im, cells = column
    chi_re = jnp.zeros_like(re)
    chi_im = jnp.zeros_like(re)
    for k, (class_re, class_im) in enumerate(classes):
        here = cells == float(k)
        chi_re = jnp.where(here, class_re, chi_re)
        chi_im = jnp.where(here, class_im, chi_im)
    return [re, im, chi_re * re - chi_im * im, chi_re * im + chi_im * re]


def pack_kernel(own_ref, planes_ref, whole_ref):
    for x in range(own_ref.shape[2]):
        for i in range(3):
            values = own_ref[i, :, x, :]
            high, low = split(values)
            planes_ref[3 * x + i] = values
            whole_ref[5 * x + i] = high
            if i < 2:
                whole_ref[5 * x + 3 + i] = low


def near_kernel(whole_ref, near_ref):
    near_ref[...] = whole_ref[whole_ref.shape[0] - near_ref.shape[0] :]


def table_kernel(xl, shift, dft_ref, fwd_ref, inv_ref):
    nx, ny = inv_ref.shape[0], dft_ref.shape[1]
    dft_ref[...] = dft_parts(iota((ny, ny), 0), iota((ny, ny), 1), ny, 0)
    first, second = iota((nx, nx), 0), iota((nx, nx), 1)
    inv_ref[...] = dft_parts(lax.rem(first + shift, nx), second, nx, 1, 1.0 / (nx * ny))
    count = nx // xl
    second = lax.rem(second, count) * xl + second // count
    fwd_ref[...] = dft_parts(first, second, nx, 1)


def features_of(column, ny):
    stack = jnp.concatenate([plane.astype(F32) for plane in column], axis=0)
    rolled = [pltpu.roll(stack, 1, 1), stack, pltpu.roll(stack, ny - 1, 1)]
    return jnp.concatenate(rolled, axis=0).astype(BF16)


def banded(spread, place, start):
    rows = jnp.zeros_like(spread[0])
    for a in range(3):
        rows = jnp.where(place == start + a, spread[a], rows)
    return rows.astype(BF16)


def weight_kernel(
    nz, con_ref, planes_ref, w1_ref, w2_ref, w3_ref, zk_ref, sp_ref, dft_ref,
    t1_ref, t2_ref, t2m_ref, t3_ref, z_ref, sr_ref, si_ref, feat_ref, hid_ref, pol_ref,
):
    hid = w2_ref.shape[3]
    half = nz // 2
    wide = half * hid
    pick = (iota((hid, wide), 0) == iota((hid, wide), 1) % hid).astype(BF16)
    place = iota((hid, wide), 1) // hid
    tall = (half - 1) * hid
    for b in range(3):
        for d in range(3):
            spread = [mm(w2_ref[a, b, d], pick) for a in range(3)]
            for r in range(half):
                block = banded(spread, place, r - 1)
                lanes = slice(b * wide, (b + 1) * wide)
                if r < half - 1:
                    t2_ref[0, d * tall + r * hid : d * tall + (r + 1) * hid, lanes] = block
                if r > 0:
                    t2_ref[1, d * tall + (r - 1) * hid : d * tall + r * hid, lanes] = block
                if 0 < r < 3:
                    top = (d * 2 + r - 1) * hid
                    t2m_ref[top : top + hid, b * 4 * hid : (b + 1) * 4 * hid] = block[:, : 4 * hid]
    channels = w1_ref.shape[3]
    taps, cols = 9 * channels, t1_ref.shape[1]
    pick = (iota((taps, cols), 0) == iota((taps, cols), 1) // nz).astype(BF16)
    spread = []
    for a in range(3):
        stack = jnp.concatenate(
            [w1_ref[a, b, d].astype(F32) for b in range(3) for d in range(3)], axis=0
        ).astype(BF16)
        spread.append(
            lax.dot_general(stack, pick, (((0,), (0,)), ((), ())), preferred_element_type=F32)
        )
    place = iota((hid, cols), 1) % nz
    for z in range(nz):
        t1_ref[z * hid : (z + 1) * hid, :] = banded(spread, place, z - 1)
    rows3, cols3 = t3_ref.shape
    taps = rows3 // nz
    pick = (iota((hid, cols3), 0) == iota((hid, cols3), 1) % hid).astype(BF16)
    offset = iota((nz, cols3), 1) // hid - iota((nz, cols3), 0)
    spread = []
    for a in range(3):
        stack = jnp.concatenate(
            [w3_ref[a, b, d].astype(F32) for b in range(3) for d in range(3)], axis=0
        ).astype(BF16)
        spread.append(mm(stack, pick))
    for r in range(taps):
        rows = [jnp.broadcast_to(spread[a][r : r + 1], (nz, cols3)) for a in range(3)]
        t3_ref[r * nz : (r + 1) * nz, :] = banded(rows, offset, -1)
    kr, ki = zk_ref[0], zk_ref[1]
    top = jnp.concatenate([kr, -ki], axis=1)
    bottom = jnp.concatenate([ki, kr], axis=1)
    high, low = split(jnp.concatenate([top, bottom, bottom, -top], axis=0))
    z_ref[...] = jnp.concatenate([high, high, low], axis=1)
    count, lanes = sp_ref.shape[1], sr_ref.shape[1]
    pick = (iota((count, lanes), 0) == iota((count, lanes), 1) // (lanes // count)).astype(F32)
    for part, ref in ((0, sr_ref), (1, si_ref)):
        ref[...] = lax.dot_general(
            sp_ref[part],
            pick,
            (((0,), (0,)), ((), ())),
            precision=lax.Precision.HIGHEST,
            preferred_element_type=F32,
        )
    ny = planes_ref.shape[2]
    depth = 12 * nz
    classes = spread_classes(con_ref, planes_ref.shape[1:])
    for x in range(planes_ref.shape[0] // 3):
        column = polarised([planes_ref[3 * x + i] for i in range(3)], classes)
        if x == 0:
            pol_ref[...] = jnp.concatenate(column[2:], axis=0)
        feat_ref[x * depth : (x + 1) * depth, :] = features_of(column, ny)
    window = [feat_ref[i * depth : (i + 3) * depth, :] for i in range(2)]
    hid_ref[...] = gelu(mm(t1_ref[...], jnp.concatenate(window, axis=1))).astype(BF16)


def gelu(values):
    return 0.5 * values * (1.0 + lax.erf(values * math.sqrt(0.5)))


def corrector_kernel(
    con_ref, first_ref, second_ref, own_feat, own_hid, own_pol, t1_ref, t2_ref, t2m_ref, t3_ref,
    z_ref, dft_ref, out_ref, feat, hid1, hid2,
):
    nz, ny = first_ref.shape[1:]
    xl = own_feat.shape[0] // (12 * nz)
    ahead = xl + 2
    depth = 12 * nz
    half = hid1.shape[0] // 2
    hid = 2 * half // nz
    tall = half - hid
    deep = 2 * nz
    classes = spread_classes(con_ref, (nz, ny))
    own = {}
    last = {}

    def features(place):
        ref, top = (second_ref, 5 * place) if place < 2 else (first_ref, 5 * (place - 2))
        high_re, high_im, cells, low_re, low_im = [ref[top + i].astype(F32) for i in range(5)]
        column = polarised([high_re + low_re, high_im + low_im, cells], classes)
        if place > 2:
            own[place - 3] = jnp.concatenate(column[2:], axis=0)
        column = [high_re, high_im] + column[2:]
        feat[place * depth : (place + 1) * depth, :] = features_of(column, ny)

    def feature_rows(place):
        if place < ahead:
            return feat[place * depth : (place + 1) * depth, :]
        return own_feat[(place - ahead) * depth : (place - ahead + 1) * depth, :]

    def first_layer(j):
        window = [jnp.concatenate([feature_rows(j + i + b) for b in range(3)], axis=0) for i in range(2)]
        return mm(t1_ref[...], jnp.concatenate(window, axis=1))

    def first_done(j, made):
        hid1[:, j * ny : (j + 2) * ny] = gelu(made).astype(BF16)

    def hidden(place, top, bottom):
        if place < ahead:
            return hid1[top:bottom, place * ny : (place + 1) * ny]
        return own_hid[top:bottom, (place - ahead) * ny : (place - ahead + 1) * ny]

    def tap_sum(weights, top, bottom, j):
        window = [
            jnp.concatenate([hidden(j + b + i, top, bottom) for i in range(2)], axis=1) for b in range(3)
        ]
        made = mm(weights, jnp.concatenate(window, axis=0))
        rows = weights.shape[0] // 3
        sides = []
        for i in range(2):
            lanes = slice(i * ny, (i + 1) * ny)
            sides.append(
                pltpu.roll(made[:rows, lanes], 1, 1)
                + made[rows : 2 * rows, lanes]
                + pltpu.roll(made[2 * rows :, lanes], ny - 1, 1)
            )
        return jnp.concatenate(sides, axis=1)

    def second_layer(j):
        return [
            tap_sum(t2_ref[0], 0, half, j),
            tap_sum(t2m_ref[...], half - 2 * hid, half + 2 * hid, j),
            tap_sum(t2_ref[1], half, 2 * half, j),
        ]

    def second_done(j, made):
        lanes = slice(j * ny, (j + 2) * ny)
        for top, part in zip((0, tall, tall + 2 * hid), made):
            hid2[top : top + part.shape[0], lanes] = gelu(part).astype(BF16)

    def third_layer(j):
        made = mm(t3_ref[...], hid2[:, j * ny : (j + 2) * ny])
        last[j], last[j + 1] = made[:, :ny], made[:, ny:]

    def source(x):
        parts = []
        for d in range(3):
            total = None
            for b in range(3):
                top = (b * 3 + d) * deep
                piece = last[x + b][top : top + deep]
                total = piece if total is None else total + piece
            parts.append(total)
        return own[x] + (pltpu.roll(parts[0], 1, 1) + parts[1] + pltpu.roll(parts[2], ny - 1, 1))

    def transformed(places):
        lifted = mm(z_ref[...], right_split(jnp.concatenate([source(x) for x in places], axis=1)))
        plain, turned = [], []
        for i in range(len(places)):
            plain.append(lifted[:deep, i * ny : (i + 1) * ny])
            turned.append(lifted[deep:, i * ny : (i + 1) * ny])
        both = [jnp.concatenate(plain, axis=0), jnp.concatenate(turned, axis=0)]
        return mm(left_split(jnp.concatenate(both, axis=1)), dft_ref[...])

    own[xl - 1] = own_pol[...]
    made1, made2 = {}, {}
    features(4)
    features(5)
    made1[4] = first_layer(4)
    features(2)
    features(3)
    made1[2] = first_layer(2)
    first_done(4, made1[4])
    made2[4] = second_layer(4)
    features(0)
    features(1)
    made1[0] = first_layer(0)
    first_done(2, made1[2])
    made2[2] = second_layer(2)
    first_done(0, made1[0])
    second_done(4, made2[4])
    third_layer(4)
    made2[0] = second_layer(0)
    second_done(2, made2[2])
    third_layer(2)
    later = transformed([2, 3])
    second_done(0, made2[0])
    third_layer(0)
    spectrum = jnp.concatenate([transformed([0, 1]), later], axis=0)
    out_ref[...] = jnp.transpose(spectrum).reshape(out_ref.shape)


def spectral_kernel(nz, in_ref, fwd_ref, inv_ref, sr_ref, si_ref, out_ref):
    values = swap_blocks(in_ref, in_ref.shape[1])
    both = jnp.concatenate([values, other_part(values, nz, 1.0)], axis=0)
    spectrum = mm(fwd_ref[...], right_split(both))
    scaled = sr_ref[...] * spectrum + si_ref[...] * other_part(spectrum, nz, -1.0)
    both = jnp.concatenate([scaled, other_part(scaled, nz, -1.0)], axis=0)
    out_ref[...] = mm(inv_ref[...], right_split(both)).reshape(out_ref.shape)


def finish_kernel(nz, in_ref, tab_ref, planes_ref, out_ref):
    values = swap_blocks(in_ref, in_ref.shape[1])
    both = jnp.concatenate([values, other_part(values, nz, -1.0)], axis=0)
    field = jnp.transpose(mm(tab_ref[...], right_split(both)))
    for x in range(out_ref.shape[2]):
        for part in range(2):
            first = (2 * x + part) * nz
            out_ref[part, :, x, :] = planes_ref[3 * x + part] + field[first : first + nz, :]


def call(kernel, out_shapes, args, scratch=(), flops=0):
    vmem = pl.BlockSpec(memory_space=pltpu.VMEM)
    single = not isinstance(out_shapes, list)
    return pl.pallas_call(
        kernel,
        out_shape=out_shapes,
        in_specs=[vmem] * len(args),
        out_specs=vmem if single else [vmem] * len(out_shapes),
        scratch_shapes=scratch,
        compiler_params=pltpu.CompilerParams(vmem_limit_bytes=VMEM_LIMIT),
        cost_estimate=pl.CostEstimate(flops=flops, bytes_accessed=4 * 1024 * 1024, transcendentals=0),
    )(*args)


def lane_device(incident, material, contrast, w_first, w_middle, w_last, z_kernel, spectral):
    count = lax.axis_size("gx")
    nz, xl, ny = material.shape
    hid = w_middle.shape[0]
    ql, nx = spectral.shape[1], spectral.shape[2]
    struct = jax.ShapeDtypeStruct
    still = ((0, 0),) * 3
    own = jnp.pad(material[None], ((2, 0),) + still).astype(F32) + jnp.pad(incident, ((0, 1),) + still)
    classes = jnp.transpose(contrast)
    planes, whole = call(
        pack_kernel,
        [struct((3 * xl, nz, ny), F32), struct((5 * xl, nz, ny), BF16)],
        (own,),
        flops=10**6,
    )
    near = call(near_kernel, struct((10, nz, ny), BF16), (whole,), flops=10**6)
    first = lax.ppermute(whole, "gx", [(i, (i + 1) % count) for i in range(count)])
    second = lax.ppermute(near, "gx", [(i, (i + 2) % count) for i in range(count)])
    lanes = 2 * nz * xl
    dft, fwd, inv = call(
        functools.partial(table_kernel, xl, 3),
        [struct((6 * ny, ny), BF16), struct((nx, 6 * nx), BF16), struct((nx, 6 * nx), BF16)],
        (),
        flops=10**9,
    )
    t1, t2, t2m, t3, zmat, sr, si, feat, hidden, pol = call(
        functools.partial(weight_kernel, nz),
        [
            struct((nz * hid, 36 * nz), BF16),
            struct((2, 3 * (nz // 2 - 1) * hid, 3 * nz // 2 * hid), BF16),
            struct((6 * hid, 12 * hid), BF16),
            struct((18 * nz, nz * hid), BF16),
            struct((4 * nz, 6 * nz), BF16),
            struct((nx, ql * 2 * nz), F32),
            struct((nx, ql * 2 * nz), F32),
            struct((xl * 12 * nz, ny), BF16),
            struct((nz * hid, 2 * ny), BF16),
            struct((2 * nz, ny), F32),
        ],
        (
            classes,
            planes,
            jnp.transpose(w_first, (2, 3, 4, 1, 0)),
            jnp.transpose(w_middle, (2, 3, 4, 0, 1)),
            jnp.transpose(w_last, (2, 3, 4, 0, 1)),
            z_kernel,
            spectral,
            dft,
        ),
        flops=10**9,
    )
    spectrum = call(
        corrector_kernel,
        struct((count, ql, lanes), F32),
        (classes, first, second, feat, hidden, pol, t1, t2, t2m, t3, zmat, dft),
        scratch=[
            pltpu.VMEM(((xl + 2) * 12 * nz, ny), BF16),
            pltpu.VMEM((nz * hid, (xl + 2) * ny), BF16),
            pltpu.VMEM((nz * hid, (xl + 2) * ny), BF16),
        ],
        flops=10**9,
    )
    piece = lax.all_to_all(spectrum, "gx", 0, 0, tiled=True)
    spread = call(
        functools.partial(spectral_kernel, nz),
        struct((count, xl, lanes), F32),
        (piece, fwd, inv, sr, si),
        flops=10**8,
    )
    rows = lax.all_to_all(spread, "gx", 0, 0, tiled=True)
    return call(
        functools.partial(finish_kernel, nz),
        struct(incident.shape, F32),
        (rows, fwd, planes),
        flops=10**8,
    )


def per_device(incident, material, contrast, w_first, w_middle, w_last, z_kernel, spectral):
    nz, xl, ny = material.shape
    ql, nx = spectral.shape[1], spectral.shape[2]
    lanes = (
        lax.axis_size("gy") == 1
        and ny == 128
        and nx == 128
        and xl == 4
        and ql == 4
        and 2 * nz * xl == 128
        and w_middle.shape[0] == 32
    )
    device = lane_device if lanes else general_device
    return device(incident, material, contrast, w_first, w_middle, w_last, z_kernel, spectral)


def solution(mesh):
    placed = (
        P("grp", None, "gx", "gy"),
        P("grp", "gx", "gy"),
        P("grp", None),
        P(),
        P(),
        P(),
        P("grp", None, None),
        P("grp", "gx", None),
    )
    return jax.shard_map(
        per_device,
        mesh=mesh,
        in_specs=placed,
        out_specs=P("grp", None, "gx", "gy"),
        check_vma=False,
    )
```

```python
import functools
import math

import jax
import jax.numpy as jnp
from jax import lax
from jax.experimental import pallas as pl
from jax.experimental.pallas import tpu as pltpu
from jax.sharding import PartitionSpec as P

F32 = jnp.float32
BF16 = jnp.bfloat16
VMEM_LIMIT = 48 * 1024 * 1024


def padded_2(x, sides, width):
    for axis, dim in sides:
        count, length = (lax.axis_size(axis), x.shape[dim])
        up = [(i, (i + 1) % count) for i in range(count)]
        down = [(j, i) for i, j in up]
        last = lax.slice_in_dim(x, length - width, length, axis=dim)
        leading = lax.slice_in_dim(x, 0, width, axis=dim)
        before = lax.ppermute(last, axis, up)
        after = lax.ppermute(leading, axis, down)
        x = jnp.concatenate([before, x, after], axis=dim)
    return x


def conv_layer(values, weights):
    return lax.conv_general_dilated(
        values[None],
        weights,
        (1, 1, 1),
        ((1, 1), (0, 0), (0, 0)),
        dimension_numbers=("NCDHW", "OIDHW", "NCDHW"),
        preferred_element_type=jnp.float32,
    )[0]


def activate(values):
    return jax.nn.gelu(values, approximate=False).astype(jnp.bfloat16)


def dft_tables(length):
    positions = jnp.arange(length, dtype=jnp.int32)
    product = positions[:, None] * positions[None, :] % length
    angle = product.astype(jnp.float32) * (2.0 * math.pi / length)
    return (jnp.cos(angle), jnp.sin(angle))


def green_apply(source, z_kernel, spectral):
    high = lax.Precision.HIGHEST
    kr, ki = (z_kernel[0], z_kernel[1])
    lre = jnp.einsum("zw,wxy->zxy", kr, source[0], precision=high) - jnp.einsum(
        "zw,wxy->zxy", ki, source[1], precision=high
    )
    lim = jnp.einsum("zw,wxy->zxy", kr, source[1], precision=high) + jnp.einsum(
        "zw,wxy->zxy", ki, source[0], precision=high
    )
    columns = lax.all_to_all(jnp.stack([lre, lim]), "gy", split_axis=1, concat_axis=3, tiled=True)
    count_y = columns.shape[3]
    cos_y, sin_y = dft_tables(count_y)
    fwd_re = jnp.dot(columns[0], cos_y, precision=high) + jnp.dot(columns[1], sin_y, precision=high)
    fwd_im = jnp.dot(columns[1], cos_y, precision=high) - jnp.dot(columns[0], sin_y, precision=high)
    count_x = columns.shape[2] * lax.axis_size("gx")
    cos_x, sin_x = dft_tables(count_x)
    piece = lax.all_to_all(
        jnp.stack([fwd_re, fwd_im]), "gx", split_axis=3, concat_axis=2, tiled=True
    )
    ar = jnp.einsum("zxk,xq->zkq", piece[0], cos_x, precision=high) + jnp.einsum(
        "zxk,xq->zkq", piece[1], sin_x, precision=high
    )
    ai = jnp.einsum("zxk,xq->zkq", piece[1], cos_x, precision=high) - jnp.einsum(
        "zxk,xq->zkq", piece[0], sin_x, precision=high
    )
    br = spectral[0] * ar - spectral[1] * ai
    bi = spectral[0] * ai + spectral[1] * ar
    gr = jnp.einsum("zkq,qx->zxk", br, cos_x, precision=high) - jnp.einsum(
        "zkq,qx->zxk", bi, sin_x, precision=high
    )
    gi = jnp.einsum("zkq,qx->zxk", bi, cos_x, precision=high) + jnp.einsum(
        "zkq,qx->zxk", br, sin_x, precision=high
    )
    spread = jnp.stack([gr, gi]) / count_x
    rows = lax.all_to_all(spread, "gx", split_axis=2, concat_axis=3, tiled=True)
    inv_re = jnp.dot(rows[0], cos_y, precision=high) - jnp.dot(rows[1], sin_y, precision=high)
    inv_im = jnp.dot(rows[1], cos_y, precision=high) + jnp.dot(rows[0], sin_y, precision=high)
    scattered = jnp.stack([inv_re, inv_im]) / count_y
    return lax.all_to_all(scattered, "gy", split_axis=3, concat_axis=1, tiled=True)


def general_device(incident, material, contrast, w_first, w_middle, w_last, z_kernel, spectral):
    high = lax.Precision.HIGHEST
    classes = contrast.shape[0]
    selector = (material[None] == jnp.arange(classes, dtype=jnp.int32)[:, None, None, None]).astype(
        jnp.float32
    )
    chi_re = jnp.einsum("k,kzxy->zxy", contrast[:, 0], selector, precision=high)
    chi_im = jnp.einsum("k,kzxy->zxy", contrast[:, 1], selector, precision=high)
    field = incident
    pol_re = chi_re * field[0] - chi_im * field[1]
    pol_im = chi_re * field[1] + chi_im * field[0]
    features = jnp.stack([field[0], field[1], pol_re, pol_im]).astype(jnp.bfloat16)
    padded = padded_2(features, (("gx", 2), ("gy", 3)), 3)
    hidden = activate(conv_layer(padded, w_first))
    hidden = activate(conv_layer(hidden, w_middle))
    correction = conv_layer(hidden, w_last)
    source = jnp.stack([pol_re, pol_im]) + correction
    field = incident + green_apply(source, z_kernel, spectral)
    return field


def split(values):
    high = values.astype(BF16)
    low = (values - high.astype(F32)).astype(BF16)
    return high, low


def cosine(steps, length):
    turn = 2.0 * math.pi / length
    angle = (length // 4 - jnp.minimum(steps, length - steps)).astype(F32) * turn
    square = angle * angle
    total = jnp.full_like(angle, 1.0 / math.factorial(13))
    for power in (11, 9, 7, 5, 3, 1):
        sign = 1.0 if power % 4 == 1 else -1.0
        total = total * square + sign / math.factorial(power)
    return total * angle


def dft_parts(rows, cols, length, axis, along, scale=1.0):
    steps = lax.rem(rows * cols, length)
    later = lax.rem(steps + 3 * length // 4, length)
    high, low = split(jnp.concatenate([cosine(steps, length), cosine(later, length)], axis=axis) * scale)
    return jnp.concatenate([high, high, low], axis=along)


def left_split(values):
    high, low = split(values)
    return jnp.concatenate([high, low, high], axis=1)


def right_split(values):
    high, low = split(values)
    return jnp.concatenate([high, low, high], axis=0)


def mm(a, b):
    return jnp.dot(a, b, preferred_element_type=F32)


def iota(shape, dim):
    return lax.broadcasted_iota(jnp.int32, shape, dim)


def turned(values, nz):
    real = (iota(values.shape, 1) // nz) % 2 == 0
    ahead = pltpu.roll(values, values.shape[1] - nz, 1)
    return jnp.where(real, -ahead, pltpu.roll(values, nz, 1))


def swap_blocks(ref, count):
    pieces = [ref[:, q, :] for q in range(count)]
    inner = pieces[0].shape[1] // count
    block = iota(pieces[0].shape, 1) // inner
    places = [block == q for q in range(count)]

    def chosen(options):
        total = options[0]
        for place, option in zip(places[1:], options[1:]):
            total = jnp.where(place, option, total)
        return total

    moved = []
    for step in range(count):
        total = chosen([pieces[(x + step) % count] for x in range(count)])
        moved.append(pltpu.roll(total, step * inner, 1) if step else total)
    rows = [chosen([moved[(q - x) % count] for q in range(count)]) for x in range(count)]
    return jnp.concatenate(rows, axis=0)


def spread_classes(con_ref, shape):
    return [
        [jnp.broadcast_to(con_ref[part : part + 1, k : k + 1], shape) for part in range(2)]
        for k in range(con_ref.shape[1])
    ]


def unpacked(ref, x, classes):
    high_re, high_im, cells, low_re, low_im = [ref[x, i].astype(F32) for i in range(5)]
    re, im = high_re + low_re, high_im + low_im
    chi_re = jnp.zeros_like(re)
    chi_im = jnp.zeros_like(re)
    for k, (class_re, class_im) in enumerate(classes):
        here = cells == float(k)
        chi_re = jnp.where(here, class_re, chi_re)
        chi_im = jnp.where(here, class_im, chi_im)
    return [high_re, high_im, chi_re * re - chi_im * im, chi_re * im + chi_im * re]


def pack_kernel(own_ref, whole_ref):
    for x in range(own_ref.shape[2]):
        for i in range(3):
            high, low = split(own_ref[i, :, x, :])
            whole_ref[x, i] = high
            if i < 2:
                whole_ref[x, i + 3] = low


def table_kernel(xl, shift, dft_ref, fwd_ref, inv_ref):
    nx, ny = inv_ref.shape[0], dft_ref.shape[1]
    dft_ref[...] = dft_parts(iota((ny, ny), 0), iota((ny, ny), 1), ny, 0, 0)
    first, second = iota((nx, nx), 0), iota((nx, nx), 1)
    inv_ref[...] = dft_parts(lax.rem(first + shift, nx), second, nx, 1, 1, 1.0 / (nx * ny))
    count = nx // xl
    second = lax.rem(second, count) * xl + second // count
    fwd_ref[...] = dft_parts(first, second, nx, 0, 1)


def features_of(column, ny):
    stack = jnp.concatenate([plane.astype(F32) for plane in column], axis=0)
    rolled = [pltpu.roll(stack, 1, 1), stack, pltpu.roll(stack, ny - 1, 1)]
    return jnp.concatenate(rolled, axis=0).astype(BF16)


def banded(spread, place, start):
    rows = jnp.zeros_like(spread[0])
    for a in range(3):
        rows = jnp.where(place == start + a, spread[a], rows)
    return rows.astype(BF16)


def weight_kernel(
    nz, con_ref, whole_ref, w1_ref, w2_ref, w3_ref, zk_ref, sp_ref, dft_ref,
    t1_ref, t2_ref, t2m_ref, t3_ref, z_ref, sr_ref, si_ref, feat_ref, hid_ref, pol_ref,
):
    hid = w2_ref.shape[3]
    half = nz // 2
    wide = half * hid
    pick = (iota((hid, wide), 0) == iota((hid, wide), 1) % hid).astype(BF16)
    place = iota((hid, wide), 1) // hid
    tall = (half - 1) * hid
    for b in range(3):
        for d in range(3):
            spread = [mm(w2_ref[a, b, d], pick) for a in range(3)]
            for r in range(half):
                block = banded(spread, place, r - 1)
                lanes = slice(b * wide, (b + 1) * wide)
                if r < half - 1:
                    t2_ref[0, d * tall + r * hid : d * tall + (r + 1) * hid, lanes] = block
                if r > 0:
                    t2_ref[1, d * tall + (r - 1) * hid : d * tall + r * hid, lanes] = block
                if 0 < r < 3:
                    top = (d * 2 + r - 1) * hid
                    t2m_ref[top : top + hid, b * 4 * hid : (b + 1) * 4 * hid] = block[:, : 4 * hid]
    channels = w1_ref.shape[3]
    taps, cols = 9 * channels, t1_ref.shape[1]
    pick = (iota((taps, cols), 0) == iota((taps, cols), 1) // nz).astype(BF16)
    spread = []
    for a in range(3):
        stack = jnp.concatenate(
            [w1_ref[a, b, d].astype(F32) for b in range(3) for d in range(3)], axis=0
        ).astype(BF16)
        spread.append(
            lax.dot_general(stack, pick, (((0,), (0,)), ((), ())), preferred_element_type=F32)
        )
    place = iota((hid, cols), 1) % nz
    for z in range(nz):
        t1_ref[z * hid : (z + 1) * hid, :] = banded(spread, place, z - 1)
    rows3, cols3 = t3_ref.shape
    taps = rows3 // nz
    pick = (iota((hid, cols3), 0) == iota((hid, cols3), 1) % hid).astype(BF16)
    offset = iota((nz, cols3), 1) // hid - iota((nz, cols3), 0)
    spread = []
    for a in range(3):
        stack = jnp.concatenate(
            [w3_ref[a, b, d].astype(F32) for b in range(3) for d in range(3)], axis=0
        ).astype(BF16)
        spread.append(mm(stack, pick))
    for r in range(taps):
        rows = [jnp.broadcast_to(spread[a][r : r + 1], (nz, cols3)) for a in range(3)]
        t3_ref[r * nz : (r + 1) * nz, :] = banded(rows, offset, -1)
    kr, ki = zk_ref[0], zk_ref[1]
    top = jnp.concatenate([kr, -ki], axis=1)
    bottom = jnp.concatenate([ki, kr], axis=1)
    high, low = split(jnp.concatenate([top, bottom, bottom, -top], axis=0))
    z_ref[...] = jnp.concatenate([high, high, low], axis=1)
    count, lanes = sp_ref.shape[1], sr_ref.shape[1]
    pick = (iota((count, lanes), 0) == iota((count, lanes), 1) // (lanes // count)).astype(F32)
    for part, ref in ((0, sr_ref), (1, si_ref)):
        ref[...] = lax.dot_general(
            sp_ref[part],
            pick,
            (((0,), (0,)), ((), ())),
            precision=lax.Precision.HIGHEST,
            preferred_element_type=F32,
        )
    ny = whole_ref.shape[3]
    depth = 12 * nz
    classes = spread_classes(con_ref, whole_ref.shape[2:])
    for x in range(whole_ref.shape[0]):
        column = unpacked(whole_ref, x, classes)
        if x == 0:
            pol_ref[...] = jnp.concatenate(column[2:], axis=0)
        feat_ref[x * depth : (x + 1) * depth, :] = features_of(column, ny)
    window = [feat_ref[i * depth : (i + 3) * depth, :] for i in range(2)]
    hid_ref[...] = gelu(mm(t1_ref[...], jnp.concatenate(window, axis=1))).astype(BF16)


def gelu(values):
    return 0.5 * values * (1.0 + lax.erf(values * math.sqrt(0.5)))


def corrector_kernel(
    con_ref, first_ref, second_ref, own_feat, own_hid, own_pol, t1_ref, t2_ref, t2m_ref, t3_ref,
    z_ref, dft_ref, out_ref, feat, hid1, hid2,
):
    nz, ny = first_ref.shape[2:]
    xl = own_feat.shape[0] // (12 * nz)
    ahead = xl + 2
    depth = 12 * nz
    half = hid1.shape[0] // 2
    hid = 2 * half // nz
    tall = half - hid
    deep = 2 * nz
    classes = spread_classes(con_ref, (nz, ny))
    own = {}
    last = {}

    def features(place):
        ref, x = (second_ref, place) if place < 2 else (first_ref, place - 2)
        column = unpacked(ref, x, classes)
        if place > 2:
            own[place - 3] = jnp.concatenate(column[2:], axis=0)
        feat[place * depth : (place + 1) * depth, :] = features_of(column, ny)

    def feature_rows(place):
        if place < ahead:
            return feat[place * depth : (place + 1) * depth, :]
        return own_feat[(place - ahead) * depth : (place - ahead + 1) * depth, :]

    def first_layer(j):
        window = [jnp.concatenate([feature_rows(j + i + b) for b in range(3)], axis=0) for i in range(2)]
        return mm(t1_ref[...], jnp.concatenate(window, axis=1))

    def first_done(j, made):
        hid1[:, j * ny : (j + 2) * ny] = gelu(made).astype(BF16)

    def hidden(place, top, bottom):
        if place < ahead:
            return hid1[top:bottom, place * ny : (place + 1) * ny]
        return own_hid[top:bottom, (place - ahead) * ny : (place - ahead + 1) * ny]

    def tap_sum(weights, top, bottom, j):
        window = [
            jnp.concatenate([hidden(j + b + i, top, bottom) for i in range(2)], axis=1) for b in range(3)
        ]
        made = mm(weights, jnp.concatenate(window, axis=0))
        rows = weights.shape[0] // 3
        sides = []
        for i in range(2):
            lanes = slice(i * ny, (i + 1) * ny)
            sides.append(
                pltpu.roll(made[:rows, lanes], 1, 1)
                + made[rows : 2 * rows, lanes]
                + pltpu.roll(made[2 * rows :, lanes], ny - 1, 1)
            )
        return jnp.concatenate(sides, axis=1)

    def second_layer(j):
        return [
            tap_sum(t2_ref[0], 0, half, j),
            tap_sum(t2m_ref[...], half - 2 * hid, half + 2 * hid, j),
            tap_sum(t2_ref[1], half, 2 * half, j),
        ]

    def second_done(j, made):
        lanes = slice(j * ny, (j + 2) * ny)
        for top, part in zip((0, tall, tall + 2 * hid), made):
            hid2[top : top + part.shape[0], lanes] = gelu(part).astype(BF16)

    def third_layer(j):
        made = mm(t3_ref[...], hid2[:, j * ny : (j + 2) * ny])
        last[j], last[j + 1] = made[:, :ny], made[:, ny:]

    def source(x):
        parts = []
        for d in range(3):
            total = None
            for b in range(3):
                top = (b * 3 + d) * deep
                piece = last[x + b][top : top + deep]
                total = piece if total is None else total + piece
            parts.append(total)
        return own[x] + (pltpu.roll(parts[0], 1, 1) + parts[1] + pltpu.roll(parts[2], ny - 1, 1))

    def transformed(places):
        lifted = mm(z_ref[...], right_split(jnp.concatenate([source(x) for x in places], axis=1)))
        plain, turned = [], []
        for i in range(len(places)):
            plain.append(lifted[:deep, i * ny : (i + 1) * ny])
            turned.append(lifted[deep:, i * ny : (i + 1) * ny])
        both = [jnp.concatenate(plain, axis=0), jnp.concatenate(turned, axis=0)]
        return mm(left_split(jnp.concatenate(both, axis=1)), dft_ref[...])

    own[xl - 1] = own_pol[...]
    made1, made2 = {}, {}
    features(4)
    features(5)
    made1[4] = first_layer(4)
    features(2)
    features(3)
    made1[2] = first_layer(2)
    first_done(4, made1[4])
    made2[4] = second_layer(4)
    features(0)
    features(1)
    made1[0] = first_layer(0)
    first_done(2, made1[2])
    made2[2] = second_layer(2)
    first_done(0, made1[0])
    second_done(4, made2[4])
    third_layer(4)
    made2[0] = second_layer(0)
    second_done(2, made2[2])
    third_layer(2)
    later = transformed([2, 3])
    second_done(0, made2[0])
    third_layer(0)
    spectrum = jnp.concatenate([transformed([0, 1]), later], axis=0)
    out_ref[...] = jnp.transpose(spectrum).reshape(out_ref.shape)


def spectral_kernel(nz, in_ref, fwd_ref, inv_ref, sr_ref, si_ref, out_ref):
    values = swap_blocks(in_ref, in_ref.shape[1])
    lanes = values.shape[1]
    made = mm(fwd_ref[...], right_split(jnp.concatenate([values, turned(values, nz)], axis=1)))
    nx = made.shape[0] // 2
    plain = made[:nx, :lanes] - made[nx:, lanes:]
    other = made[:nx, lanes:] + made[nx:, :lanes]
    scaled = [sr_ref[...] * plain + si_ref[...] * other, sr_ref[...] * other - si_ref[...] * plain]
    out_ref[...] = mm(inv_ref[...], right_split(jnp.concatenate(scaled, axis=0))).reshape(out_ref.shape)


def finish_kernel(nz, in_ref, tab_ref, inc_ref, out_ref):
    made = mm(tab_ref[...], right_split(swap_blocks(in_ref, in_ref.shape[1])))
    ny = made.shape[0] // 2
    field = jnp.transpose(made[:ny] + turned(made[ny:], nz))
    for x in range(out_ref.shape[2]):
        for part in range(2):
            first = (2 * x + part) * nz
            out_ref[part, :, x, :] = inc_ref[part, :, x, :] + field[first : first + nz, :]


def call(kernel, out_shapes, args, scratch=(), flops=0):
    vmem = pl.BlockSpec(memory_space=pltpu.VMEM)
    single = not isinstance(out_shapes, list)
    return pl.pallas_call(
        kernel,
        out_shape=out_shapes,
        in_specs=[vmem] * len(args),
        out_specs=vmem if single else [vmem] * len(out_shapes),
        scratch_shapes=scratch,
        compiler_params=pltpu.CompilerParams(vmem_limit_bytes=VMEM_LIMIT),
        cost_estimate=pl.CostEstimate(flops=flops, bytes_accessed=4 * 1024 * 1024, transcendentals=0),
    )(*args)


def lane_device(incident, material, contrast, w_first, w_middle, w_last, z_kernel, spectral):
    count = lax.axis_size("gx")
    nz, xl, ny = material.shape
    hid = w_middle.shape[0]
    ql, nx = spectral.shape[1], spectral.shape[2]
    struct = jax.ShapeDtypeStruct
    classes = jnp.transpose(contrast)
    still = ((0, 0),) * 3
    own = jnp.pad(material[None], ((2, 0),) + still).astype(F32) + jnp.pad(incident, ((0, 1),) + still)
    whole = call(pack_kernel, struct((xl, 5, nz, ny), BF16), (own,), flops=10**6)
    first = lax.ppermute(whole, "gx", [(i, (i + 1) % count) for i in range(count)])
    second = lax.ppermute(whole[xl - 2 :], "gx", [(i, (i + 2) % count) for i in range(count)])
    lanes = 2 * nz * xl
    dft, fwd, inv = call(
        functools.partial(table_kernel, xl, 3),
        [struct((6 * ny, ny), BF16), struct((2 * nx, 3 * nx), BF16), struct((nx, 6 * nx), BF16)],
        (),
        flops=10**9,
    )
    t1, t2, t2m, t3, zmat, sr, si, feat, hidden, pol = call(
        functools.partial(weight_kernel, nz),
        [
            struct((nz * hid, 36 * nz), BF16),
            struct((2, 3 * (nz // 2 - 1) * hid, 3 * nz // 2 * hid), BF16),
            struct((6 * hid, 12 * hid), BF16),
            struct((18 * nz, nz * hid), BF16),
            struct((4 * nz, 6 * nz), BF16),
            struct((nx, ql * 2 * nz), F32),
            struct((nx, ql * 2 * nz), F32),
            struct((xl * 12 * nz, ny), BF16),
            struct((nz * hid, 2 * ny), BF16),
            struct((2 * nz, ny), F32),
        ],
        (
            classes,
            whole,
            jnp.transpose(w_first, (2, 3, 4, 1, 0)),
            jnp.transpose(w_middle, (2, 3, 4, 0, 1)),
            jnp.transpose(w_last, (2, 3, 4, 0, 1)),
            z_kernel,
            spectral,
            dft,
        ),
        flops=10**9,
    )
    spectrum = call(
        corrector_kernel,
        struct((count, ql, lanes), F32),
        (classes, first, second, feat, hidden, pol, t1, t2, t2m, t3, zmat, dft),
        scratch=[
            pltpu.VMEM(((xl + 2) * 12 * nz, ny), BF16),
            pltpu.VMEM((nz * hid, (xl + 2) * ny), BF16),
            pltpu.VMEM((nz * hid, (xl + 2) * ny), BF16),
        ],
        flops=10**9,
    )
    piece = lax.all_to_all(spectrum, "gx", 0, 0, tiled=True)
    spread = call(
        functools.partial(spectral_kernel, nz),
        struct((count, xl, lanes), F32),
        (piece, fwd, inv, sr, si),
        flops=10**8,
    )
    rows = lax.all_to_all(spread, "gx", 0, 0, tiled=True)
    return call(
        functools.partial(finish_kernel, nz),
        struct(incident.shape, F32),
        (rows, fwd, incident),
        flops=10**8,
    )


def per_device(incident, material, contrast, w_first, w_middle, w_last, z_kernel, spectral):
    nz, xl, ny = material.shape
    ql, nx = spectral.shape[1], spectral.shape[2]
    lanes = (
        lax.axis_size("gy") == 1
        and ny == 128
        and nx == 128
        and xl == 4
        and ql == 4
        and 2 * nz * xl == 128
        and w_middle.shape[0] == 32
    )
    device = lane_device if lanes else general_device
    return device(incident, material, contrast, w_first, w_middle, w_last, z_kernel, spectral)


def solution(mesh):
    placed = (
        P("grp", None, "gx", "gy"),
        P("grp", "gx", "gy"),
        P("grp", None),
        P(),
        P(),
        P(),
        P("grp", None, None),
        P("grp", "gx", None),
    )
    return jax.shard_map(
        per_device,
        mesh=mesh,
        in_specs=placed,
        out_specs=P("grp", None, "gx", "gy"),
        check_vma=False,
    )
```

```python
import functools
import math

import jax
import jax.numpy as jnp
from jax import lax
from jax.experimental import pallas as pl
from jax.experimental.pallas import tpu as pltpu
from jax.sharding import PartitionSpec as P

F32 = jnp.float32
BF16 = jnp.bfloat16
VMEM_LIMIT = 48 * 1024 * 1024


def padded_2(x, sides, width):
    for axis, dim in sides:
        count, length = (lax.axis_size(axis), x.shape[dim])
        up = [(i, (i + 1) % count) for i in range(count)]
        down = [(j, i) for i, j in up]
        last = lax.slice_in_dim(x, length - width, length, axis=dim)
        leading = lax.slice_in_dim(x, 0, width, axis=dim)
        before = lax.ppermute(last, axis, up)
        after = lax.ppermute(leading, axis, down)
        x = jnp.concatenate([before, x, after], axis=dim)
    return x


def conv_layer(values, weights):
    return lax.conv_general_dilated(
        values[None],
        weights,
        (1, 1, 1),
        ((1, 1), (0, 0), (0, 0)),
        dimension_numbers=("NCDHW", "OIDHW", "NCDHW"),
        preferred_element_type=jnp.float32,
    )[0]


def activate(values):
    return jax.nn.gelu(values, approximate=False).astype(jnp.bfloat16)


def dft_tables(length):
    positions = jnp.arange(length, dtype=jnp.int32)
    product = positions[:, None] * positions[None, :] % length
    angle = product.astype(jnp.float32) * (2.0 * math.pi / length)
    return (jnp.cos(angle), jnp.sin(angle))


def green_apply(source, z_kernel, spectral):
    high = lax.Precision.HIGHEST
    kr, ki = (z_kernel[0], z_kernel[1])
    lre = jnp.einsum("zw,wxy->zxy", kr, source[0], precision=high) - jnp.einsum(
        "zw,wxy->zxy", ki, source[1], precision=high
    )
    lim = jnp.einsum("zw,wxy->zxy", kr, source[1], precision=high) + jnp.einsum(
        "zw,wxy->zxy", ki, source[0], precision=high
    )
    columns = lax.all_to_all(jnp.stack([lre, lim]), "gy", split_axis=1, concat_axis=3, tiled=True)
    count_y = columns.shape[3]
    cos_y, sin_y = dft_tables(count_y)
    fwd_re = jnp.dot(columns[0], cos_y, precision=high) + jnp.dot(columns[1], sin_y, precision=high)
    fwd_im = jnp.dot(columns[1], cos_y, precision=high) - jnp.dot(columns[0], sin_y, precision=high)
    count_x = columns.shape[2] * lax.axis_size("gx")
    cos_x, sin_x = dft_tables(count_x)
    piece = lax.all_to_all(
        jnp.stack([fwd_re, fwd_im]), "gx", split_axis=3, concat_axis=2, tiled=True
    )
    ar = jnp.einsum("zxk,xq->zkq", piece[0], cos_x, precision=high) + jnp.einsum(
        "zxk,xq->zkq", piece[1], sin_x, precision=high
    )
    ai = jnp.einsum("zxk,xq->zkq", piece[1], cos_x, precision=high) - jnp.einsum(
        "zxk,xq->zkq", piece[0], sin_x, precision=high
    )
    br = spectral[0] * ar - spectral[1] * ai
    bi = spectral[0] * ai + spectral[1] * ar
    gr = jnp.einsum("zkq,qx->zxk", br, cos_x, precision=high) - jnp.einsum(
        "zkq,qx->zxk", bi, sin_x, precision=high
    )
    gi = jnp.einsum("zkq,qx->zxk", bi, cos_x, precision=high) + jnp.einsum(
        "zkq,qx->zxk", br, sin_x, precision=high
    )
    spread = jnp.stack([gr, gi]) / count_x
    rows = lax.all_to_all(spread, "gx", split_axis=2, concat_axis=3, tiled=True)
    inv_re = jnp.dot(rows[0], cos_y, precision=high) - jnp.dot(rows[1], sin_y, precision=high)
    inv_im = jnp.dot(rows[1], cos_y, precision=high) + jnp.dot(rows[0], sin_y, precision=high)
    scattered = jnp.stack([inv_re, inv_im]) / count_y
    return lax.all_to_all(scattered, "gy", split_axis=3, concat_axis=1, tiled=True)


def general_device(incident, material, contrast, w_first, w_middle, w_last, z_kernel, spectral):
    high = lax.Precision.HIGHEST
    classes = contrast.shape[0]
    selector = (material[None] == jnp.arange(classes, dtype=jnp.int32)[:, None, None, None]).astype(
        jnp.float32
    )
    chi_re = jnp.einsum("k,kzxy->zxy", contrast[:, 0], selector, precision=high)
    chi_im = jnp.einsum("k,kzxy->zxy", contrast[:, 1], selector, precision=high)
    field = incident
    pol_re = chi_re * field[0] - chi_im * field[1]
    pol_im = chi_re * field[1] + chi_im * field[0]
    features = jnp.stack([field[0], field[1], pol_re, pol_im]).astype(jnp.bfloat16)
    padded = padded_2(features, (("gx", 2), ("gy", 3)), 3)
    hidden = activate(conv_layer(padded, w_first))
    hidden = activate(conv_layer(hidden, w_middle))
    correction = conv_layer(hidden, w_last)
    source = jnp.stack([pol_re, pol_im]) + correction
    field = incident + green_apply(source, z_kernel, spectral)
    return field


def split(values):
    high = values.astype(BF16)
    low = (values - high.astype(F32)).astype(BF16)
    return high, low


def cosine(steps, length):
    turn = 2.0 * math.pi / length
    angle = (length // 4 - jnp.minimum(steps, length - steps)).astype(F32) * turn
    square = angle * angle
    total = jnp.full_like(angle, 1.0 / math.factorial(13))
    for power in (11, 9, 7, 5, 3, 1):
        sign = 1.0 if power % 4 == 1 else -1.0
        total = total * square + sign / math.factorial(power)
    return total * angle


def dft_parts(rows, cols, length, axis, along, scale=1.0):
    steps = lax.rem(rows * cols, length)
    later = lax.rem(steps + 3 * length // 4, length)
    high, low = split(jnp.concatenate([cosine(steps, length), cosine(later, length)], axis=axis) * scale)
    return jnp.concatenate([high, high, low], axis=along)


def left_split(values):
    high, low = split(values)
    return jnp.concatenate([high, low, high], axis=1)


def right_split(values):
    high, low = split(values)
    return jnp.concatenate([high, low, high], axis=0)


def mm(a, b):
    return jnp.dot(a, b, preferred_element_type=F32)


def iota(shape, dim):
    return lax.broadcasted_iota(jnp.int32, shape, dim)


def turned(values, nz):
    real = (iota(values.shape, 1) // nz) % 2 == 0
    ahead = pltpu.roll(values, values.shape[1] - nz, 1)
    return jnp.where(real, -ahead, pltpu.roll(values, nz, 1))


def swap_blocks(ref, count):
    pieces = [ref[:, q, :] for q in range(count)]
    inner = pieces[0].shape[1] // count
    block = iota(pieces[0].shape, 1) // inner
    places = [block == q for q in range(count)]

    def chosen(options):
        total = options[0]
        for place, option in zip(places[1:], options[1:]):
            total = jnp.where(place, option, total)
        return total

    moved = []
    for step in range(count):
        total = chosen([pieces[(x + step) % count] for x in range(count)])
        moved.append(pltpu.roll(total, step * inner, 1) if step else total)
    rows = [chosen([moved[(q - x) % count] for q in range(count)]) for x in range(count)]
    return jnp.concatenate(rows, axis=0)


def spread_classes(con_ref, shape):
    return [
        [jnp.broadcast_to(con_ref[part : part + 1, k : k + 1], shape) for part in range(2)]
        for k in range(con_ref.shape[1])
    ]


def unpacked(ref, x, classes):
    high_re, high_im, cells, low_re, low_im = [ref[x, i].astype(F32) for i in range(5)]
    re, im = high_re + low_re, high_im + low_im
    chi_re = jnp.zeros_like(re)
    chi_im = jnp.zeros_like(re)
    for k, (class_re, class_im) in enumerate(classes):
        here = cells == float(k)
        chi_re = jnp.where(here, class_re, chi_re)
        chi_im = jnp.where(here, class_im, chi_im)
    return [high_re, high_im, chi_re * re - chi_im * im, chi_re * im + chi_im * re]


def pack_kernel(own_ref, whole_ref):
    for x in range(own_ref.shape[2]):
        for i in range(3):
            high, low = split(own_ref[i, :, x, :])
            whole_ref[x, i] = high
            if i < 2:
                whole_ref[x, i + 3] = low


def table_kernel(xl, shift, dft_ref, fwd_ref, inv_ref):
    nx, ny = inv_ref.shape[0], dft_ref.shape[1]
    dft_ref[...] = dft_parts(iota((ny, ny), 0), iota((ny, ny), 1), ny, 0, 0)
    first, second = iota((nx, nx), 0), iota((nx, nx), 1)
    inv_ref[...] = dft_parts(lax.rem(first + shift, nx), second, nx, 1, 1, 1.0 / (nx * ny))
    count = nx // xl
    second = lax.rem(second, count) * xl + second // count
    fwd_ref[...] = dft_parts(first, second, nx, 0, 1)


def features_of(column, ny):
    planes = [plane.astype(F32) for plane in column]
    half = planes[0].shape[0] // 2
    lower = jnp.concatenate([plane[:half] for plane in planes], axis=0)
    upper = jnp.concatenate([plane[half:] for plane in planes], axis=0)
    rows = [plane[half : half + 1] for plane in planes] + [plane[half - 1 : half] for plane in planes]
    edge = jnp.concatenate(rows, axis=0)
    made = []
    for part in (lower, upper, edge):
        made += [pltpu.roll(part, 1, 1), part, pltpu.roll(part, ny - 1, 1)]
    return jnp.concatenate(made + [jnp.zeros_like(edge)], axis=0).astype(BF16)


def first_product(t1_ref, rows_of, places):
    made = []
    depth = t1_ref.shape[2] // 3
    for part in range(2):
        pieces = []
        for place in places:
            taps = []
            for b in range(3):
                rows = rows_of(place + b)
                edge = 2 * depth - rows.shape[0]
                main = depth - edge
                taps += [rows[part * main : (part + 1) * main], rows[2 * main :]]
            pieces.append(jnp.concatenate(taps, axis=0))
        made.append(mm(t1_ref[part], jnp.concatenate(pieces, axis=1)))
    return jnp.concatenate(made, axis=0)


def banded(spread, place, start):
    rows = jnp.zeros_like(spread[0])
    for a in range(3):
        rows = jnp.where(place == start + a, spread[a], rows)
    return rows.astype(BF16)


def weight_kernel(
    nz, con_ref, whole_ref, w1_ref, w2_ref, w3_ref, zk_ref, sp_ref, dft_ref,
    t1_ref, t2_ref, t2m_ref, t3_ref, z_ref, sr_ref, si_ref, feat_ref, hid_ref, pol_ref,
):
    hid = w2_ref.shape[3]
    half = nz // 2
    wide = half * hid
    pick = (iota((hid, wide), 0) == iota((hid, wide), 1) % hid).astype(BF16)
    place = iota((hid, wide), 1) // hid
    tall = (half - 1) * hid
    for b in range(3):
        for d in range(3):
            spread = [mm(w2_ref[a, b, d], pick) for a in range(3)]
            for r in range(half):
                block = banded(spread, place, r - 1)
                lanes = slice(b * wide, (b + 1) * wide)
                if r < half - 1:
                    t2_ref[0, d * tall + r * hid : d * tall + (r + 1) * hid, lanes] = block
                if r > 0:
                    t2_ref[1, d * tall + (r - 1) * hid : d * tall + r * hid, lanes] = block
                if 0 < r < 3:
                    top = (d * 2 + r - 1) * hid
                    t2m_ref[top : top + hid, b * 4 * hid : (b + 1) * 4 * hid] = block[:, : 4 * hid]
    channels = w1_ref.shape[3]
    taps, cols = 9 * channels, t1_ref.shape[2]
    depth = cols // 3
    main = 3 * channels * half
    row = iota((1, cols), 1) % depth
    beyond = row - main
    spot = jnp.where(beyond < 0, row // half, beyond // (2 * channels) * channels + beyond % channels)
    tap = iota((1, cols), 1) // depth * 3 * channels + spot
    pick = (iota((taps, cols), 0) == tap).astype(BF16)
    spread = []
    for a in range(3):
        stack = jnp.concatenate(
            [w1_ref[a, b, d].astype(F32) for b in range(3) for d in range(3)], axis=0
        ).astype(BF16)
        spread.append(
            lax.dot_general(stack, pick, (((0,), (0,)), ((), ())), preferred_element_type=F32)
        )
    outer = beyond % (2 * channels) // channels
    for part, cell in ((0, half), (1, -1)):
        place = jnp.where((outer == part) & (spot < 3 * channels), cell, -9)
        place = jnp.broadcast_to(jnp.where(beyond < 0, row % half, place), (hid, cols))
        for z in range(half):
            t1_ref[part, z * hid : (z + 1) * hid, :] = banded(spread, place, z - 1)
    rows3, cols3 = t3_ref.shape
    taps = rows3 // nz
    pick = (iota((hid, cols3), 0) == iota((hid, cols3), 1) % hid).astype(BF16)
    offset = iota((nz, cols3), 1) // hid - iota((nz, cols3), 0)
    spread = []
    for a in range(3):
        stack = jnp.concatenate(
            [w3_ref[a, b, d].astype(F32) for b in range(3) for d in range(3)], axis=0
        ).astype(BF16)
        spread.append(mm(stack, pick))
    for r in range(taps):
        rows = [jnp.broadcast_to(spread[a][r : r + 1], (nz, cols3)) for a in range(3)]
        t3_ref[r * nz : (r + 1) * nz, :] = banded(rows, offset, -1)
    kr, ki = zk_ref[0], zk_ref[1]
    top = jnp.concatenate([kr, -ki], axis=1)
    bottom = jnp.concatenate([ki, kr], axis=1)
    high, low = split(jnp.concatenate([top, bottom, bottom, -top], axis=0))
    z_ref[...] = jnp.concatenate([high, high, low], axis=1)
    count, lanes = sp_ref.shape[1], sr_ref.shape[1]
    pick = (iota((count, lanes), 0) == iota((count, lanes), 1) // (lanes // count)).astype(F32)
    for part, ref in ((0, sr_ref), (1, si_ref)):
        ref[...] = lax.dot_general(
            sp_ref[part],
            pick,
            (((0,), (0,)), ((), ())),
            precision=lax.Precision.HIGHEST,
            preferred_element_type=F32,
        )
    ny = whole_ref.shape[3]
    deep = feat_ref.shape[0] // whole_ref.shape[0]
    classes = spread_classes(con_ref, whole_ref.shape[2:])
    for x in range(whole_ref.shape[0]):
        column = unpacked(whole_ref, x, classes)
        if x == 0:
            pol_ref[...] = jnp.concatenate(column[2:], axis=0)
        feat_ref[x * deep : (x + 1) * deep, :] = features_of(column, ny)
    made = first_product(t1_ref, lambda x: feat_ref[x * deep : (x + 1) * deep, :], (0, 1))
    hid_ref[...] = gelu(made).astype(BF16)


def gelu(values):
    return 0.5 * values * (1.0 + lax.erf(values * math.sqrt(0.5)))


def corrector_kernel(
    con_ref, first_ref, second_ref, own_feat, own_hid, own_pol, t1_ref, t2_ref, t2m_ref, t3_ref,
    z_ref, dft_ref, out_ref, feat, hid1, hid2,
):
    nz, ny = first_ref.shape[2:]
    ahead = first_ref.shape[0] + second_ref.shape[0]
    xl = first_ref.shape[0]
    depth = feat.shape[0] // ahead
    half = hid1.shape[0] // 2
    hid = 2 * half // nz
    tall = half - hid
    deep = 2 * nz
    classes = spread_classes(con_ref, (nz, ny))
    own = {}
    last = {}

    def features(place):
        ref, x = (second_ref, place) if place < 2 else (first_ref, place - 2)
        column = unpacked(ref, x, classes)
        if place > 2:
            own[place - 3] = jnp.concatenate(column[2:], axis=0)
        feat[place * depth : (place + 1) * depth, :] = features_of(column, ny)

    def feature_rows(place):
        if place < ahead:
            return feat[place * depth : (place + 1) * depth, :]
        return own_feat[(place - ahead) * depth : (place - ahead + 1) * depth, :]

    def first_layer(j):
        return first_product(t1_ref, feature_rows, (j, j + 1))

    def first_done(j, made):
        hid1[:, j * ny : (j + 2) * ny] = gelu(made).astype(BF16)

    def hidden(place, top, bottom):
        if place < ahead:
            return hid1[top:bottom, place * ny : (place + 1) * ny]
        return own_hid[top:bottom, (place - ahead) * ny : (place - ahead + 1) * ny]

    def tap_sum(weights, top, bottom, j):
        window = [
            jnp.concatenate([hidden(j + b + i, top, bottom) for i in range(2)], axis=1) for b in range(3)
        ]
        made = mm(weights, jnp.concatenate(window, axis=0))
        rows = weights.shape[0] // 3
        sides = []
        for i in range(2):
            lanes = slice(i * ny, (i + 1) * ny)
            sides.append(
                pltpu.roll(made[:rows, lanes], 1, 1)
                + made[rows : 2 * rows, lanes]
                + pltpu.roll(made[2 * rows :, lanes], ny - 1, 1)
            )
        return jnp.concatenate(sides, axis=1)

    def second_layer(j):
        return [
            tap_sum(t2_ref[0], 0, half, j),
            tap_sum(t2m_ref[...], half - 2 * hid, half + 2 * hid, j),
            tap_sum(t2_ref[1], half, 2 * half, j),
        ]

    def second_done(j, made):
        lanes = slice(j * ny, (j + 2) * ny)
        for top, part in zip((0, tall, tall + 2 * hid), made):
            hid2[top : top + part.shape[0], lanes] = gelu(part).astype(BF16)

    def third_layer(j):
        made = mm(t3_ref[...], hid2[:, j * ny : (j + 2) * ny])
        last[j], last[j + 1] = made[:, :ny], made[:, ny:]

    def source(x):
        parts = []
        for d in range(3):
            total = None
            for b in range(3):
                top = (b * 3 + d) * deep
                piece = last[x + b][top : top + deep]
                total = piece if total is None else total + piece
            parts.append(total)
        return own[x] + (pltpu.roll(parts[0], 1, 1) + parts[1] + pltpu.roll(parts[2], ny - 1, 1))

    def transformed(places):
        lifted = mm(z_ref[...], right_split(jnp.concatenate([source(x) for x in places], axis=1)))
        plain, turned = [], []
        for i in range(len(places)):
            plain.append(lifted[:deep, i * ny : (i + 1) * ny])
            turned.append(lifted[deep:, i * ny : (i + 1) * ny])
        both = [jnp.concatenate(plain, axis=0), jnp.concatenate(turned, axis=0)]
        return mm(left_split(jnp.concatenate(both, axis=1)), dft_ref[...])

    own[xl - 1] = own_pol[...]
    made1, made2 = {}, {}
    features(4)
    features(5)
    made1[4] = first_layer(4)
    features(2)
    features(3)
    made1[2] = first_layer(2)
    first_done(4, made1[4])
    made2[4] = second_layer(4)
    features(0)
    features(1)
    made1[0] = first_layer(0)
    first_done(2, made1[2])
    made2[2] = second_layer(2)
    first_done(0, made1[0])
    second_done(4, made2[4])
    third_layer(4)
    made2[0] = second_layer(0)
    second_done(2, made2[2])
    third_layer(2)
    later = transformed([2, 3])
    second_done(0, made2[0])
    third_layer(0)
    spectrum = jnp.concatenate([transformed([0, 1]), later], axis=0)
    out_ref[...] = jnp.transpose(spectrum).reshape(out_ref.shape)


def spectral_kernel(nz, in_ref, fwd_ref, inv_ref, sr_ref, si_ref, out_ref):
    values = swap_blocks(in_ref, in_ref.shape[1])
    lanes = values.shape[1]
    made = mm(fwd_ref[...], right_split(jnp.concatenate([values, turned(values, nz)], axis=1)))
    nx = made.shape[0] // 2
    plain = made[:nx, :lanes] - made[nx:, lanes:]
    other = made[:nx, lanes:] + made[nx:, :lanes]
    scaled = [sr_ref[...] * plain + si_ref[...] * other, sr_ref[...] * other - si_ref[...] * plain]
    out_ref[...] = mm(inv_ref[...], right_split(jnp.concatenate(scaled, axis=0))).reshape(out_ref.shape)


def finish_kernel(nz, in_ref, tab_ref, inc_ref, out_ref):
    made = mm(tab_ref[...], right_split(swap_blocks(in_ref, in_ref.shape[1])))
    ny = made.shape[0] // 2
    field = jnp.transpose(made[:ny] + turned(made[ny:], nz))
    for x in range(out_ref.shape[2]):
        for part in range(2):
            first = (2 * x + part) * nz
            out_ref[part, :, x, :] = inc_ref[part, :, x, :] + field[first : first + nz, :]


def call(kernel, out_shapes, args, scratch=(), flops=0):
    vmem = pl.BlockSpec(memory_space=pltpu.VMEM)
    single = not isinstance(out_shapes, list)
    return pl.pallas_call(
        kernel,
        out_shape=out_shapes,
        in_specs=[vmem] * len(args),
        out_specs=vmem if single else [vmem] * len(out_shapes),
        scratch_shapes=scratch,
        compiler_params=pltpu.CompilerParams(vmem_limit_bytes=VMEM_LIMIT),
        cost_estimate=pl.CostEstimate(flops=flops, bytes_accessed=4 * 1024 * 1024, transcendentals=0),
    )(*args)


def lane_device(incident, material, contrast, w_first, w_middle, w_last, z_kernel, spectral):
    count = lax.axis_size("gx")
    nz, xl, ny = material.shape
    hid = w_middle.shape[0]
    ql, nx = spectral.shape[1], spectral.shape[2]
    struct = jax.ShapeDtypeStruct
    classes = jnp.transpose(contrast)
    still = ((0, 0),) * 3
    own = jnp.pad(material[None], ((2, 0),) + still).astype(F32) + jnp.pad(incident, ((0, 1),) + still)
    whole = call(pack_kernel, struct((xl, 5, nz, ny), BF16), (own,), flops=10**6)
    first = lax.ppermute(whole, "gx", [(i, (i + 1) % count) for i in range(count)])
    second = lax.ppermute(whole[xl - 2 :], "gx", [(i, (i + 2) % count) for i in range(count)])
    lanes = 2 * nz * xl
    depth, deep = 6 * nz + 32, 12 * nz + 32
    dft, fwd, inv = call(
        functools.partial(table_kernel, xl, 3),
        [struct((6 * ny, ny), BF16), struct((2 * nx, 3 * nx), BF16), struct((nx, 6 * nx), BF16)],
        (),
        flops=10**9,
    )
    t1, t2, t2m, t3, zmat, sr, si, feat, hidden, pol = call(
        functools.partial(weight_kernel, nz),
        [
            struct((2, nz // 2 * hid, 3 * depth), BF16),
            struct((2, 3 * (nz // 2 - 1) * hid, 3 * nz // 2 * hid), BF16),
            struct((6 * hid, 12 * hid), BF16),
            struct((18 * nz, nz * hid), BF16),
            struct((4 * nz, 6 * nz), BF16),
            struct((nx, ql * 2 * nz), F32),
            struct((nx, ql * 2 * nz), F32),
            struct((xl * deep, ny), BF16),
            struct((nz * hid, 2 * ny), BF16),
            struct((2 * nz, ny), F32),
        ],
        (
            classes,
            whole,
            jnp.transpose(w_first, (2, 3, 4, 1, 0)),
            jnp.transpose(w_middle, (2, 3, 4, 0, 1)),
            jnp.transpose(w_last, (2, 3, 4, 0, 1)),
            z_kernel,
            spectral,
            dft,
        ),
        flops=10**9,
    )
    spectrum = call(
        corrector_kernel,
        struct((count, ql, lanes), F32),
        (classes, first, second, feat, hidden, pol, t1, t2, t2m, t3, zmat, dft),
        scratch=[
            pltpu.VMEM(((xl + 2) * deep, ny), BF16),
            pltpu.VMEM((nz * hid, (xl + 2) * ny), BF16),
            pltpu.VMEM((nz * hid, (xl + 2) * ny), BF16),
        ],
        flops=10**9,
    )
    piece = lax.all_to_all(spectrum, "gx", 0, 0, tiled=True)
    spread = call(
        functools.partial(spectral_kernel, nz),
        struct((count, xl, lanes), F32),
        (piece, fwd, inv, sr, si),
        flops=10**8,
    )
    rows = lax.all_to_all(spread, "gx", 0, 0, tiled=True)
    return call(
        functools.partial(finish_kernel, nz),
        struct(incident.shape, F32),
        (rows, fwd, incident),
        flops=10**8,
    )


def per_device(incident, material, contrast, w_first, w_middle, w_last, z_kernel, spectral):
    nz, xl, ny = material.shape
    ql, nx = spectral.shape[1], spectral.shape[2]
    lanes = (
        lax.axis_size("gy") == 1
        and ny == 128
        and nx == 128
        and xl == 4
        and ql == 4
        and 2 * nz * xl == 128
        and w_middle.shape[0] == 32
    )
    device = lane_device if lanes else general_device
    return device(incident, material, contrast, w_first, w_middle, w_last, z_kernel, spectral)


def solution(mesh):
    placed = (
        P("grp", None, "gx", "gy"),
        P("grp", "gx", "gy"),
        P("grp", None),
        P(),
        P(),
        P(),
        P("grp", None, None),
        P("grp", "gx", None),
    )
    return jax.shard_map(
        per_device,
        mesh=mesh,
        in_specs=placed,
        out_specs=P("grp", None, "gx", "gy"),
        check_vma=False,
    )
```

```python
import functools
import math

import jax
import jax.numpy as jnp
from jax import lax
from jax.experimental import pallas as pl
from jax.experimental.pallas import tpu as pltpu
from jax.sharding import PartitionSpec as P

F32 = jnp.float32
BF16 = jnp.bfloat16
VMEM_LIMIT = 48 * 1024 * 1024


def padded_2(x, sides, width):
    for axis, dim in sides:
        count, length = (lax.axis_size(axis), x.shape[dim])
        up = [(i, (i + 1) % count) for i in range(count)]
        down = [(j, i) for i, j in up]
        last = lax.slice_in_dim(x, length - width, length, axis=dim)
        leading = lax.slice_in_dim(x, 0, width, axis=dim)
        before = lax.ppermute(last, axis, up)
        after = lax.ppermute(leading, axis, down)
        x = jnp.concatenate([before, x, after], axis=dim)
    return x


def conv_layer(values, weights):
    return lax.conv_general_dilated(
        values[None],
        weights,
        (1, 1, 1),
        ((1, 1), (0, 0), (0, 0)),
        dimension_numbers=("NCDHW", "OIDHW", "NCDHW"),
        preferred_element_type=jnp.float32,
    )[0]


def activate(values):
    return jax.nn.gelu(values, approximate=False).astype(jnp.bfloat16)


def dft_tables(length):
    positions = jnp.arange(length, dtype=jnp.int32)
    product = positions[:, None] * positions[None, :] % length
    angle = product.astype(jnp.float32) * (2.0 * math.pi / length)
    return (jnp.cos(angle), jnp.sin(angle))


def green_apply(source, z_kernel, spectral):
    high = lax.Precision.HIGHEST
    kr, ki = (z_kernel[0], z_kernel[1])
    lre = jnp.einsum("zw,wxy->zxy", kr, source[0], precision=high) - jnp.einsum(
        "zw,wxy->zxy", ki, source[1], precision=high
    )
    lim = jnp.einsum("zw,wxy->zxy", kr, source[1], precision=high) + jnp.einsum(
        "zw,wxy->zxy", ki, source[0], precision=high
    )
    columns = lax.all_to_all(jnp.stack([lre, lim]), "gy", split_axis=1, concat_axis=3, tiled=True)
    count_y = columns.shape[3]
    cos_y, sin_y = dft_tables(count_y)
    fwd_re = jnp.dot(columns[0], cos_y, precision=high) + jnp.dot(columns[1], sin_y, precision=high)
    fwd_im = jnp.dot(columns[1], cos_y, precision=high) - jnp.dot(columns[0], sin_y, precision=high)
    count_x = columns.shape[2] * lax.axis_size("gx")
    cos_x, sin_x = dft_tables(count_x)
    piece = lax.all_to_all(
        jnp.stack([fwd_re, fwd_im]), "gx", split_axis=3, concat_axis=2, tiled=True
    )
    ar = jnp.einsum("zxk,xq->zkq", piece[0], cos_x, precision=high) + jnp.einsum(
        "zxk,xq->zkq", piece[1], sin_x, precision=high
    )
    ai = jnp.einsum("zxk,xq->zkq", piece[1], cos_x, precision=high) - jnp.einsum(
        "zxk,xq->zkq", piece[0], sin_x, precision=high
    )
    br = spectral[0] * ar - spectral[1] * ai
    bi = spectral[0] * ai + spectral[1] * ar
    gr = jnp.einsum("zkq,qx->zxk", br, cos_x, precision=high) - jnp.einsum(
        "zkq,qx->zxk", bi, sin_x, precision=high
    )
    gi = jnp.einsum("zkq,qx->zxk", bi, cos_x, precision=high) + jnp.einsum(
        "zkq,qx->zxk", br, sin_x, precision=high
    )
    spread = jnp.stack([gr, gi]) / count_x
    rows = lax.all_to_all(spread, "gx", split_axis=2, concat_axis=3, tiled=True)
    inv_re = jnp.dot(rows[0], cos_y, precision=high) - jnp.dot(rows[1], sin_y, precision=high)
    inv_im = jnp.dot(rows[1], cos_y, precision=high) + jnp.dot(rows[0], sin_y, precision=high)
    scattered = jnp.stack([inv_re, inv_im]) / count_y
    return lax.all_to_all(scattered, "gy", split_axis=3, concat_axis=1, tiled=True)


def general_device(incident, material, contrast, w_first, w_middle, w_last, z_kernel, spectral):
    high = lax.Precision.HIGHEST
    classes = contrast.shape[0]
    selector = (material[None] == jnp.arange(classes, dtype=jnp.int32)[:, None, None, None]).astype(
        jnp.float32
    )
    chi_re = jnp.einsum("k,kzxy->zxy", contrast[:, 0], selector, precision=high)
    chi_im = jnp.einsum("k,kzxy->zxy", contrast[:, 1], selector, precision=high)
    field = incident
    pol_re = chi_re * field[0] - chi_im * field[1]
    pol_im = chi_re * field[1] + chi_im * field[0]
    features = jnp.stack([field[0], field[1], pol_re, pol_im]).astype(jnp.bfloat16)
    padded = padded_2(features, (("gx", 2), ("gy", 3)), 3)
    hidden = activate(conv_layer(padded, w_first))
    hidden = activate(conv_layer(hidden, w_middle))
    correction = conv_layer(hidden, w_last)
    source = jnp.stack([pol_re, pol_im]) + correction
    field = incident + green_apply(source, z_kernel, spectral)
    return field


def split(values):
    high = values.astype(BF16)
    low = (values - high.astype(F32)).astype(BF16)
    return high, low


def cosine(steps, length):
    turn = 2.0 * math.pi / length
    angle = (length // 4 - jnp.minimum(steps, length - steps)).astype(F32) * turn
    square = angle * angle
    total = jnp.full_like(angle, 1.0 / math.factorial(13))
    for power in (11, 9, 7, 5, 3, 1):
        sign = 1.0 if power % 4 == 1 else -1.0
        total = total * square + sign / math.factorial(power)
    return total * angle


def dft_parts(rows, cols, length, axis, along, scale=1.0):
    steps = lax.rem(rows * cols, length)
    later = lax.rem(steps + 3 * length // 4, length)
    high, low = split(jnp.concatenate([cosine(steps, length), cosine(later, length)], axis=axis) * scale)
    return jnp.concatenate([high, high, low], axis=along)


def left_split(values):
    high, low = split(values)
    return jnp.concatenate([high, low, high], axis=1)


def right_split(values):
    high, low = split(values)
    return jnp.concatenate([high, low, high], axis=0)


def mm(a, b):
    return jnp.dot(a, b, preferred_element_type=F32)


def iota(shape, dim):
    return lax.broadcasted_iota(jnp.int32, shape, dim)


def turned(values, nz):
    real = (iota(values.shape, 1) // nz) % 2 == 0
    ahead = pltpu.roll(values, values.shape[1] - nz, 1)
    return jnp.where(real, -ahead, pltpu.roll(values, nz, 1))


def swap_blocks(ref, count):
    pieces = [ref[:, q, :] for q in range(count)]
    inner = pieces[0].shape[1] // count
    block = iota(pieces[0].shape, 1) // inner
    places = [block == q for q in range(count)]

    def chosen(options):
        total = options[0]
        for place, option in zip(places[1:], options[1:]):
            total = jnp.where(place, option, total)
        return total

    moved = []
    for step in range(count):
        total = chosen([pieces[(x + step) % count] for x in range(count)])
        moved.append(pltpu.roll(total, step * inner, 1) if step else total)
    rows = [chosen([moved[(q - x) % count] for q in range(count)]) for x in range(count)]
    return jnp.concatenate(rows, axis=0)


def spread_classes(con_ref, shape):
    return [
        [jnp.broadcast_to(con_ref[part : part + 1, k : k + 1], shape) for part in range(2)]
        for k in range(con_ref.shape[1])
    ]


def unpacked(ref, x, classes):
    high_re, high_im, cells, low_re, low_im = [ref[x, i].astype(F32) for i in range(5)]
    re, im = high_re + low_re, high_im + low_im
    chi_re = jnp.zeros_like(re)
    chi_im = jnp.zeros_like(re)
    for k, (class_re, class_im) in enumerate(classes):
        here = cells == float(k)
        chi_re = jnp.where(here, class_re, chi_re)
        chi_im = jnp.where(here, class_im, chi_im)
    return [high_re, high_im, chi_re * re - chi_im * im, chi_re * im + chi_im * re]


def pack_kernel(own_ref, whole_ref):
    for x in range(own_ref.shape[2]):
        for i in range(3):
            high, low = split(own_ref[i, :, x, :])
            whole_ref[x, i] = high
            if i < 2:
                whole_ref[x, i + 3] = low


def table_kernel(xl, shift, dft_ref, fwd_ref, inv_ref):
    nx, ny = inv_ref.shape[0], dft_ref.shape[1]
    dft_ref[...] = dft_parts(iota((ny, ny), 0), iota((ny, ny), 1), ny, 0, 0)
    first, second = iota((nx, nx), 0), iota((nx, nx), 1)
    inv_ref[...] = dft_parts(lax.rem(first + shift, nx), second, nx, 1, 1, 1.0 / (nx * ny))
    count = nx // xl
    second = lax.rem(second, count) * xl + second // count
    fwd_ref[...] = dft_parts(first, second, nx, 0, 1)


def features_of(column, ny):
    planes = [plane.astype(F32) for plane in column]
    half = planes[0].shape[0] // 2
    lower = jnp.concatenate([plane[:half] for plane in planes], axis=0)
    upper = jnp.concatenate([plane[half:] for plane in planes], axis=0)
    rows = [plane[half : half + 1] for plane in planes] + [plane[half - 1 : half] for plane in planes]
    edge = jnp.concatenate(rows, axis=0)
    made = []
    for part in (lower, upper, edge):
        made += [pltpu.roll(part, 1, 1), part, pltpu.roll(part, ny - 1, 1)]
    return jnp.concatenate(made + [jnp.zeros_like(edge)], axis=0).astype(BF16)


def first_product(t1_ref, rows_of, places):
    made = []
    depth = t1_ref.shape[2] // 3
    for part in range(2):
        pieces = []
        for place in places:
            taps = []
            for b in range(3):
                rows = rows_of(place + b)
                edge = 2 * depth - rows.shape[0]
                main = depth - edge
                taps += [rows[part * main : (part + 1) * main], rows[2 * main :]]
            pieces.append(jnp.concatenate(taps, axis=0))
        made.append(mm(t1_ref[part], jnp.concatenate(pieces, axis=1)))
    return jnp.concatenate(made, axis=0)


def banded(spread, place, start):
    rows = jnp.zeros_like(spread[0])
    for a in range(3):
        rows = jnp.where(place == start + a, spread[a], rows)
    return rows.astype(BF16)


def weight_kernel(
    nz, con_ref, whole_ref, w1_ref, w2_ref, w3_ref, zk_ref, sp_ref, dft_ref,
    t1_ref, t2_ref, t2m_ref, t3_ref, z_ref, sr_ref, si_ref, feat_ref, hid_ref, pol_ref,
):
    hid = w2_ref.shape[3]
    half = nz // 2
    wide = half * hid
    pick = (iota((hid, wide), 0) == iota((hid, wide), 1) % hid).astype(BF16)
    place = iota((hid, wide), 1) // hid
    tall = (half - 1) * hid
    for b in range(3):
        for d in range(3):
            spread = [mm(w2_ref[a, b, d], pick) for a in range(3)]
            for r in range(half):
                block = banded(spread, place, r - 1)
                lanes = slice(b * wide, (b + 1) * wide)
                if r < half - 1:
                    t2_ref[0, d * tall + r * hid : d * tall + (r + 1) * hid, lanes] = block
                if r > 0:
                    t2_ref[1, d * tall + (r - 1) * hid : d * tall + r * hid, lanes] = block
                if 0 < r < 3:
                    top = (d * 2 + r - 1) * hid
                    t2m_ref[top : top + hid, b * 4 * hid : (b + 1) * 4 * hid] = block[:, : 4 * hid]
    channels = w1_ref.shape[3]
    taps, cols = 9 * channels, t1_ref.shape[2]
    depth = cols // 3
    main = 3 * channels * half
    row = iota((1, cols), 1) % depth
    beyond = row - main
    spot = jnp.where(beyond < 0, row // half, beyond // (2 * channels) * channels + beyond % channels)
    tap = iota((1, cols), 1) // depth * 3 * channels + spot
    pick = (iota((taps, cols), 0) == tap).astype(BF16)
    spread = []
    for a in range(3):
        stack = jnp.concatenate(
            [w1_ref[a, b, d].astype(F32) for b in range(3) for d in range(3)], axis=0
        ).astype(BF16)
        spread.append(
            lax.dot_general(stack, pick, (((0,), (0,)), ((), ())), preferred_element_type=F32)
        )
    outer = beyond % (2 * channels) // channels
    for part, cell in ((0, half), (1, -1)):
        place = jnp.where((outer == part) & (spot < 3 * channels), cell, -9)
        place = jnp.broadcast_to(jnp.where(beyond < 0, row % half, place), (hid, cols))
        for z in range(half):
            t1_ref[part, z * hid : (z + 1) * hid, :] = banded(spread, place, z - 1)
    rows3, cols3 = t3_ref.shape
    taps = rows3 // nz
    pick = (iota((hid, cols3), 0) == iota((hid, cols3), 1) % hid).astype(BF16)
    offset = iota((nz, cols3), 1) // hid - iota((nz, cols3), 0)
    spread = []
    for a in range(3):
        stack = jnp.concatenate(
            [w3_ref[a, b, d].astype(F32) for b in range(3) for d in range(3)], axis=0
        ).astype(BF16)
        spread.append(mm(stack, pick))
    for r in range(taps):
        rows = [jnp.broadcast_to(spread[a][r : r + 1], (nz, cols3)) for a in range(3)]
        t3_ref[r * nz : (r + 1) * nz, :] = banded(rows, offset, -1)
    kr, ki = zk_ref[0], zk_ref[1]
    top = jnp.concatenate([kr, -ki], axis=1)
    bottom = jnp.concatenate([ki, kr], axis=1)
    high, low = split(jnp.concatenate([top, bottom, bottom, -top], axis=0))
    z_ref[...] = jnp.concatenate([high, high, low], axis=1)
    count, lanes = sp_ref.shape[1], sr_ref.shape[1]
    pick = (iota((count, lanes), 0) == iota((count, lanes), 1) // (lanes // count)).astype(F32)
    for part, ref in ((0, sr_ref), (1, si_ref)):
        ref[...] = lax.dot_general(
            sp_ref[part],
            pick,
            (((0,), (0,)), ((), ())),
            precision=lax.Precision.HIGHEST,
            preferred_element_type=F32,
        )
    ny = whole_ref.shape[3]
    deep = feat_ref.shape[0] // whole_ref.shape[0]
    classes = spread_classes(con_ref, whole_ref.shape[2:])
    for x in range(whole_ref.shape[0]):
        column = unpacked(whole_ref, x, classes)
        if x == 0:
            pol_ref[...] = jnp.concatenate(column[2:], axis=0)
        feat_ref[x * deep : (x + 1) * deep, :] = features_of(column, ny)
    made = first_product(t1_ref, lambda x: feat_ref[x * deep : (x + 1) * deep, :], (0, 1))
    hid_ref[...] = gelu(made).astype(BF16)


def gelu(values):
    half = 0.5 * values
    return half + half * lax.erf(values * math.sqrt(0.5))


def corrector_kernel(
    con_ref, first_ref, second_ref, own_feat, own_hid, own_pol, t1_ref, t2_ref, t2m_ref, t3_ref,
    z_ref, dft_ref, out_ref, feat, hid1, hid2,
):
    nz, ny = first_ref.shape[2:]
    ahead = first_ref.shape[0] + second_ref.shape[0]
    xl = first_ref.shape[0]
    depth = feat.shape[0] // ahead
    half = hid1.shape[0] // 2
    hid = 2 * half // nz
    tall = half - hid
    deep = 2 * nz
    classes = spread_classes(con_ref, (nz, ny))
    own = {}
    last = {}

    def features(place):
        ref, x = (second_ref, place) if place < 2 else (first_ref, place - 2)
        column = unpacked(ref, x, classes)
        if place > 2:
            own[place - 3] = jnp.concatenate(column[2:], axis=0)
        feat[place * depth : (place + 1) * depth, :] = features_of(column, ny)

    def feature_rows(place):
        if place < ahead:
            return feat[place * depth : (place + 1) * depth, :]
        return own_feat[(place - ahead) * depth : (place - ahead + 1) * depth, :]

    def first_layer(j):
        return first_product(t1_ref, feature_rows, (j, j + 1))

    def first_done(j, made):
        hid1[:, j * ny : (j + 2) * ny] = gelu(made).astype(BF16)

    def hidden(place, top, bottom):
        if place < ahead:
            return hid1[top:bottom, place * ny : (place + 1) * ny]
        return own_hid[top:bottom, (place - ahead) * ny : (place - ahead + 1) * ny]

    def tap_sum(weights, top, bottom, j):
        window = [
            jnp.concatenate([hidden(j + b + i, top, bottom) for i in range(2)], axis=1) for b in range(3)
        ]
        made = mm(weights, jnp.concatenate(window, axis=0))
        rows = weights.shape[0] // 3
        sides = []
        for i in range(2):
            lanes = slice(i * ny, (i + 1) * ny)
            sides.append(
                pltpu.roll(made[:rows, lanes], 1, 1)
                + made[rows : 2 * rows, lanes]
                + pltpu.roll(made[2 * rows :, lanes], ny - 1, 1)
            )
        return jnp.concatenate(sides, axis=1)

    def second_layer(j):
        return [
            tap_sum(t2_ref[0], 0, half, j),
            tap_sum(t2m_ref[...], half - 2 * hid, half + 2 * hid, j),
            tap_sum(t2_ref[1], half, 2 * half, j),
        ]

    def second_done(j, made):
        lanes = slice(j * ny, (j + 2) * ny)
        for top, part in zip((0, tall, tall + 2 * hid), made):
            hid2[top : top + part.shape[0], lanes] = gelu(part).astype(BF16)

    def third_layer(j):
        made = mm(t3_ref[...], hid2[:, j * ny : (j + 2) * ny])
        last[j], last[j + 1] = made[:, :ny], made[:, ny:]

    def source(x):
        parts = []
        for d in range(3):
            total = None
            for b in range(3):
                top = (b * 3 + d) * deep
                piece = last[x + b][top : top + deep]
                total = piece if total is None else total + piece
            parts.append(total)
        return own[x] + (pltpu.roll(parts[0], 1, 1) + parts[1] + pltpu.roll(parts[2], ny - 1, 1))

    def transformed(places):
        lifted = mm(z_ref[...], right_split(jnp.concatenate([source(x) for x in places], axis=1)))
        plain, turned = [], []
        for i in range(len(places)):
            plain.append(lifted[:deep, i * ny : (i + 1) * ny])
            turned.append(lifted[deep:, i * ny : (i + 1) * ny])
        both = [jnp.concatenate(plain, axis=0), jnp.concatenate(turned, axis=0)]
        return mm(left_split(jnp.concatenate(both, axis=1)), dft_ref[...])

    own[xl - 1] = own_pol[...]
    pairs = range(ahead - 2, -1, -2)
    for j in pairs:
        features(j)
        features(j + 1)
    for j in pairs:
        first_done(j, first_layer(j))
    for j in pairs:
        second_done(j, second_layer(j))
    for j in pairs:
        third_layer(j)
    out_ref[...] = jnp.transpose(transformed(range(xl))).reshape(out_ref.shape)


def spectral_kernel(nz, in_ref, fwd_ref, inv_ref, sr_ref, si_ref, out_ref):
    values = swap_blocks(in_ref, in_ref.shape[1])
    lanes = values.shape[1]
    made = mm(fwd_ref[...], right_split(jnp.concatenate([values, turned(values, nz)], axis=1)))
    nx = made.shape[0] // 2
    plain = made[:nx, :lanes] - made[nx:, lanes:]
    other = made[:nx, lanes:] + made[nx:, :lanes]
    scaled = [sr_ref[...] * plain + si_ref[...] * other, sr_ref[...] * other - si_ref[...] * plain]
    out_ref[...] = mm(inv_ref[...], right_split(jnp.concatenate(scaled, axis=0))).reshape(out_ref.shape)


def finish_kernel(nz, in_ref, tab_ref, inc_ref, out_ref):
    made = mm(tab_ref[...], right_split(swap_blocks(in_ref, in_ref.shape[1])))
    ny = made.shape[0] // 2
    field = jnp.transpose(made[:ny] + turned(made[ny:], nz))
    for x in range(out_ref.shape[2]):
        for part in range(2):
            first = (2 * x + part) * nz
            out_ref[part, :, x, :] = inc_ref[part, :, x, :] + field[first : first + nz, :]


def call(kernel, out_shapes, args, scratch=(), flops=0):
    vmem = pl.BlockSpec(memory_space=pltpu.VMEM)
    single = not isinstance(out_shapes, list)
    return pl.pallas_call(
        kernel,
        out_shape=out_shapes,
        in_specs=[vmem] * len(args),
        out_specs=vmem if single else [vmem] * len(out_shapes),
        scratch_shapes=scratch,
        compiler_params=pltpu.CompilerParams(vmem_limit_bytes=VMEM_LIMIT),
        cost_estimate=pl.CostEstimate(flops=flops, bytes_accessed=4 * 1024 * 1024, transcendentals=0),
    )(*args)


def lane_device(incident, material, contrast, w_first, w_middle, w_last, z_kernel, spectral):
    count = lax.axis_size("gx")
    nz, xl, ny = material.shape
    hid = w_middle.shape[0]
    ql, nx = spectral.shape[1], spectral.shape[2]
    struct = jax.ShapeDtypeStruct
    classes = jnp.transpose(contrast)
    still = ((0, 0),) * 3
    own = jnp.pad(material[None], ((2, 0),) + still).astype(F32) + jnp.pad(incident, ((0, 1),) + still)
    whole = call(pack_kernel, struct((xl, 5, nz, ny), BF16), (own,), flops=10**6)
    first = lax.ppermute(whole, "gx", [(i, (i + 1) % count) for i in range(count)])
    second = lax.ppermute(whole[xl - 2 :], "gx", [(i, (i + 2) % count) for i in range(count)])
    lanes = 2 * nz * xl
    depth, deep = 6 * nz + 32, 12 * nz + 32
    dft, fwd, inv = call(
        functools.partial(table_kernel, xl, 3),
        [struct((6 * ny, ny), BF16), struct((2 * nx, 3 * nx), BF16), struct((nx, 6 * nx), BF16)],
        (),
        flops=10**9,
    )
    t1, t2, t2m, t3, zmat, sr, si, feat, hidden, pol = call(
        functools.partial(weight_kernel, nz),
        [
            struct((2, nz // 2 * hid, 3 * depth), BF16),
            struct((2, 3 * (nz // 2 - 1) * hid, 3 * nz // 2 * hid), BF16),
            struct((6 * hid, 12 * hid), BF16),
            struct((18 * nz, nz * hid), BF16),
            struct((4 * nz, 6 * nz), BF16),
            struct((nx, ql * 2 * nz), F32),
            struct((nx, ql * 2 * nz), F32),
            struct((xl * deep, ny), BF16),
            struct((nz * hid, 2 * ny), BF16),
            struct((2 * nz, ny), F32),
        ],
        (
            classes,
            whole,
            jnp.transpose(w_first, (2, 3, 4, 1, 0)),
            jnp.transpose(w_middle, (2, 3, 4, 0, 1)),
            jnp.transpose(w_last, (2, 3, 4, 0, 1)),
            z_kernel,
            spectral,
            dft,
        ),
        flops=10**9,
    )
    spectrum = call(
        corrector_kernel,
        struct((count, ql, lanes), F32),
        (classes, first, second, feat, hidden, pol, t1, t2, t2m, t3, zmat, dft),
        scratch=[
            pltpu.VMEM(((xl + 2) * deep, ny), BF16),
            pltpu.VMEM((nz * hid, (xl + 2) * ny), BF16),
            pltpu.VMEM((nz * hid, (xl + 2) * ny), BF16),
        ],
        flops=10**9,
    )
    piece = lax.all_to_all(spectrum, "gx", 0, 0, tiled=True)
    spread = call(
        functools.partial(spectral_kernel, nz),
        struct((count, xl, lanes), F32),
        (piece, fwd, inv, sr, si),
        flops=10**8,
    )
    rows = lax.all_to_all(spread, "gx", 0, 0, tiled=True)
    return call(
        functools.partial(finish_kernel, nz),
        struct(incident.shape, F32),
        (rows, fwd, incident),
        flops=10**8,
    )


def per_device(incident, material, contrast, w_first, w_middle, w_last, z_kernel, spectral):
    nz, xl, ny = material.shape
    ql, nx = spectral.shape[1], spectral.shape[2]
    lanes = (
        lax.axis_size("gy") == 1
        and ny == 128
        and nx == 128
        and xl == 4
        and ql == 4
        and 2 * nz * xl == 128
        and w_middle.shape[0] == 32
    )
    device = lane_device if lanes else general_device
    return device(incident, material, contrast, w_first, w_middle, w_last, z_kernel, spectral)


def solution(mesh):
    placed = (
        P("grp", None, "gx", "gy"),
        P("grp", "gx", "gy"),
        P("grp", None),
        P(),
        P(),
        P(),
        P("grp", None, None),
        P("grp", "gx", None),
    )
    return jax.shard_map(
        per_device,
        mesh=mesh,
        in_specs=placed,
        out_specs=P("grp", None, "gx", "gy"),
        check_vma=False,
    )
```

```python
import functools
import math

import jax
import jax.numpy as jnp
from jax import lax
from jax.experimental import pallas as pl
from jax.experimental.pallas import tpu as pltpu
from jax.sharding import PartitionSpec as P

F32 = jnp.float32
BF16 = jnp.bfloat16
VMEM_LIMIT = 48 * 1024 * 1024


def padded_2(x, sides, width):
    for axis, dim in sides:
        count, length = (lax.axis_size(axis), x.shape[dim])
        up = [(i, (i + 1) % count) for i in range(count)]
        down = [(j, i) for i, j in up]
        last = lax.slice_in_dim(x, length - width, length, axis=dim)
        leading = lax.slice_in_dim(x, 0, width, axis=dim)
        before = lax.ppermute(last, axis, up)
        after = lax.ppermute(leading, axis, down)
        x = jnp.concatenate([before, x, after], axis=dim)
    return x


def conv_layer(values, weights):
    return lax.conv_general_dilated(
        values[None],
        weights,
        (1, 1, 1),
        ((1, 1), (0, 0), (0, 0)),
        dimension_numbers=("NCDHW", "OIDHW", "NCDHW"),
        preferred_element_type=jnp.float32,
    )[0]


def activate(values):
    return jax.nn.gelu(values, approximate=False).astype(jnp.bfloat16)


def dft_tables(length):
    positions = jnp.arange(length, dtype=jnp.int32)
    product = positions[:, None] * positions[None, :] % length
    angle = product.astype(jnp.float32) * (2.0 * math.pi / length)
    return (jnp.cos(angle), jnp.sin(angle))


def green_apply(source, z_kernel, spectral):
    high = lax.Precision.HIGHEST
    kr, ki = (z_kernel[0], z_kernel[1])
    lre = jnp.einsum("zw,wxy->zxy", kr, source[0], precision=high) - jnp.einsum(
        "zw,wxy->zxy", ki, source[1], precision=high
    )
    lim = jnp.einsum("zw,wxy->zxy", kr, source[1], precision=high) + jnp.einsum(
        "zw,wxy->zxy", ki, source[0], precision=high
    )
    columns = lax.all_to_all(jnp.stack([lre, lim]), "gy", split_axis=1, concat_axis=3, tiled=True)
    count_y = columns.shape[3]
    cos_y, sin_y = dft_tables(count_y)
    fwd_re = jnp.dot(columns[0], cos_y, precision=high) + jnp.dot(columns[1], sin_y, precision=high)
    fwd_im = jnp.dot(columns[1], cos_y, precision=high) - jnp.dot(columns[0], sin_y, precision=high)
    count_x = columns.shape[2] * lax.axis_size("gx")
    cos_x, sin_x = dft_tables(count_x)
    piece = lax.all_to_all(
        jnp.stack([fwd_re, fwd_im]), "gx", split_axis=3, concat_axis=2, tiled=True
    )
    ar = jnp.einsum("zxk,xq->zkq", piece[0], cos_x, precision=high) + jnp.einsum(
        "zxk,xq->zkq", piece[1], sin_x, precision=high
    )
    ai = jnp.einsum("zxk,xq->zkq", piece[1], cos_x, precision=high) - jnp.einsum(
        "zxk,xq->zkq", piece[0], sin_x, precision=high
    )
    br = spectral[0] * ar - spectral[1] * ai
    bi = spectral[0] * ai + spectral[1] * ar
    gr = jnp.einsum("zkq,qx->zxk", br, cos_x, precision=high) - jnp.einsum(
        "zkq,qx->zxk", bi, sin_x, precision=high
    )
    gi = jnp.einsum("zkq,qx->zxk", bi, cos_x, precision=high) + jnp.einsum(
        "zkq,qx->zxk", br, sin_x, precision=high
    )
    spread = jnp.stack([gr, gi]) / count_x
    rows = lax.all_to_all(spread, "gx", split_axis=2, concat_axis=3, tiled=True)
    inv_re = jnp.dot(rows[0], cos_y, precision=high) - jnp.dot(rows[1], sin_y, precision=high)
    inv_im = jnp.dot(rows[1], cos_y, precision=high) + jnp.dot(rows[0], sin_y, precision=high)
    scattered = jnp.stack([inv_re, inv_im]) / count_y
    return lax.all_to_all(scattered, "gy", split_axis=3, concat_axis=1, tiled=True)


def general_device(incident, material, contrast, w_first, w_middle, w_last, z_kernel, spectral):
    high = lax.Precision.HIGHEST
    classes = contrast.shape[0]
    selector = (material[None] == jnp.arange(classes, dtype=jnp.int32)[:, None, None, None]).astype(
        jnp.float32
    )
    chi_re = jnp.einsum("k,kzxy->zxy", contrast[:, 0], selector, precision=high)
    chi_im = jnp.einsum("k,kzxy->zxy", contrast[:, 1], selector, precision=high)
    field = incident
    pol_re = chi_re * field[0] - chi_im * field[1]
    pol_im = chi_re * field[1] + chi_im * field[0]
    features = jnp.stack([field[0], field[1], pol_re, pol_im]).astype(jnp.bfloat16)
    padded = padded_2(features, (("gx", 2), ("gy", 3)), 3)
    hidden = activate(conv_layer(padded, w_first))
    hidden = activate(conv_layer(hidden, w_middle))
    correction = conv_layer(hidden, w_last)
    source = jnp.stack([pol_re, pol_im]) + correction
    field = incident + green_apply(source, z_kernel, spectral)
    return field


def split(values):
    high = values.astype(BF16)
    low = (values - high.astype(F32)).astype(BF16)
    return high, low


def cosine(steps, length):
    turn = 2.0 * math.pi / length
    angle = (length // 4 - jnp.minimum(steps, length - steps)).astype(F32) * turn
    square = angle * angle
    total = jnp.full_like(angle, 1.0 / math.factorial(13))
    for power in (11, 9, 7, 5, 3, 1):
        sign = 1.0 if power % 4 == 1 else -1.0
        total = total * square + sign / math.factorial(power)
    return total * angle


def dft_parts(rows, cols, length, axis, along, scale=1.0):
    steps = lax.rem(rows * cols, length)
    later = lax.rem(steps + 3 * length // 4, length)
    high, low = split(jnp.concatenate([cosine(steps, length), cosine(later, length)], axis=axis) * scale)
    return jnp.concatenate([high, high, low], axis=along)


def left_split(values):
    high, low = split(values)
    return jnp.concatenate([high, low, high], axis=1)


def right_split(values):
    high, low = split(values)
    return jnp.concatenate([high, low, high], axis=0)


def mm(a, b):
    return jnp.dot(a, b, preferred_element_type=F32)


def iota(shape, dim):
    return lax.broadcasted_iota(jnp.int32, shape, dim)


def turned(values, nz):
    real = (iota(values.shape, 1) // nz) % 2 == 0
    ahead = pltpu.roll(values, values.shape[1] - nz, 1)
    return jnp.where(real, -ahead, pltpu.roll(values, nz, 1))


def swap_blocks(ref, count):
    pieces = [ref[:, q, :] for q in range(count)]
    inner = pieces[0].shape[1] // count
    block = iota(pieces[0].shape, 1) // inner
    places = [block == q for q in range(count)]

    def chosen(options):
        total = options[0]
        for place, option in zip(places[1:], options[1:]):
            total = jnp.where(place, option, total)
        return total

    moved = []
    for step in range(count):
        total = chosen([pieces[(x + step) % count] for x in range(count)])
        moved.append(pltpu.roll(total, step * inner, 1) if step else total)
    rows = [chosen([moved[(q - x) % count] for q in range(count)]) for x in range(count)]
    return jnp.concatenate(rows, axis=0)


def spread_classes(con_ref, shape):
    return [
        [jnp.broadcast_to(con_ref[part : part + 1, k : k + 1], shape) for part in range(2)]
        for k in range(con_ref.shape[1])
    ]


def unpacked(ref, x, classes):
    high_re, high_im, cells, low_re, low_im = [ref[x, i].astype(F32) for i in range(5)]
    re, im = high_re + low_re, high_im + low_im
    chi_re = jnp.zeros_like(re)
    chi_im = jnp.zeros_like(re)
    for k, (class_re, class_im) in enumerate(classes):
        here = cells == float(k)
        chi_re = jnp.where(here, class_re, chi_re)
        chi_im = jnp.where(here, class_im, chi_im)
    return [high_re, high_im, chi_re * re - chi_im * im, chi_re * im + chi_im * re]


def pack_kernel(own_ref, whole_ref):
    for x in range(own_ref.shape[2]):
        for i in range(3):
            high, low = split(own_ref[i, :, x, :])
            whole_ref[x, i] = high
            if i < 2:
                whole_ref[x, i + 3] = low


def near_kernel(class_count, own_ref, whole_ref, near_ref):
    xl, _, nz, ny = whole_ref.shape
    classes = [
        [jnp.broadcast_to(own_ref[3, 0, part : part + 1, k : k + 1], (nz, ny)) for part in range(2)]
        for k in range(class_count)
    ]
    for x in range(2):
        for i, plane in enumerate(unpacked(whole_ref, xl - 2 + x, classes)):
            near_ref[x, i] = plane.astype(BF16)


def table_kernel(xl, shift, dft_ref, fwd_ref, inv_ref):
    nx, ny = inv_ref.shape[0], dft_ref.shape[1]
    dft_ref[...] = dft_parts(iota((ny, ny), 0), iota((ny, ny), 1), ny, 0, 0)
    first, second = iota((nx, nx), 0), iota((nx, nx), 1)
    inv_ref[...] = dft_parts(lax.rem(first + shift, nx), second, nx, 1, 1, 1.0 / (nx * ny))
    count = nx // xl
    second = lax.rem(second, count) * xl + second // count
    fwd_ref[...] = dft_parts(first, second, nx, 0, 1)


def features_of(column, ny):
    planes = [plane.astype(F32) for plane in column]
    half = planes[0].shape[0] // 2
    lower = jnp.concatenate([plane[:half] for plane in planes], axis=0)
    upper = jnp.concatenate([plane[half:] for plane in planes], axis=0)
    rows = [plane[half : half + 1] for plane in planes] + [plane[half - 1 : half] for plane in planes]
    edge = jnp.concatenate(rows, axis=0)
    made = []
    for part in (lower, upper, edge):
        made += [pltpu.roll(part, 1, 1), part, pltpu.roll(part, ny - 1, 1)]
    return jnp.concatenate(made + [jnp.zeros_like(edge)], axis=0).astype(BF16)


def first_product(t1_ref, rows_of, places):
    made = []
    depth = t1_ref.shape[2] // 3
    for part in range(2):
        pieces = []
        for place in places:
            taps = []
            for b in range(3):
                rows = rows_of(place + b)
                edge = 2 * depth - rows.shape[0]
                main = depth - edge
                taps += [rows[part * main : (part + 1) * main], rows[2 * main :]]
            pieces.append(jnp.concatenate(taps, axis=0))
        made.append(mm(t1_ref[part], jnp.concatenate(pieces, axis=1)))
    return jnp.concatenate(made, axis=0)


def banded(spread, place, start):
    rows = jnp.zeros_like(spread[0])
    for a in range(3):
        rows = jnp.where(place == start + a, spread[a], rows)
    return rows.astype(BF16)


def weight_kernel(
    nz, con_ref, whole_ref, w1_ref, w2_ref, w3_ref, zk_ref, sp_ref, dft_ref,
    t1_ref, t2_ref, t2m_ref, t3_ref, z_ref, sr_ref, si_ref, feat_ref, hid_ref, pol_ref,
):
    hid = w2_ref.shape[3]
    half = nz // 2
    wide = half * hid
    pick = (iota((hid, wide), 0) == iota((hid, wide), 1) % hid).astype(BF16)
    place = iota((hid, wide), 1) // hid
    tall = (half - 1) * hid
    for b in range(3):
        for d in range(3):
            spread = [mm(w2_ref[a, b, d], pick) for a in range(3)]
            for r in range(half):
                block = banded(spread, place, r - 1)
                lanes = slice(b * wide, (b + 1) * wide)
                if r < half - 1:
                    t2_ref[0, d * tall + r * hid : d * tall + (r + 1) * hid, lanes] = block
                if r > 0:
                    t2_ref[1, d * tall + (r - 1) * hid : d * tall + r * hid, lanes] = block
                if 0 < r < 3:
                    top = (d * 2 + r - 1) * hid
                    t2m_ref[top : top + hid, b * 4 * hid : (b + 1) * 4 * hid] = block[:, : 4 * hid]
    channels = w1_ref.shape[3]
    taps, cols = 9 * channels, t1_ref.shape[2]
    depth = cols // 3
    main = 3 * channels * half
    row = iota((1, cols), 1) % depth
    beyond = row - main
    spot = jnp.where(beyond < 0, row // half, beyond // (2 * channels) * channels + beyond % channels)
    tap = iota((1, cols), 1) // depth * 3 * channels + spot
    pick = (iota((taps, cols), 0) == tap).astype(BF16)
    spread = []
    for a in range(3):
        stack = jnp.concatenate(
            [w1_ref[a, b, d].astype(F32) for b in range(3) for d in range(3)], axis=0
        ).astype(BF16)
        spread.append(
            lax.dot_general(stack, pick, (((0,), (0,)), ((), ())), preferred_element_type=F32)
        )
    outer = beyond % (2 * channels) // channels
    for part, cell in ((0, half), (1, -1)):
        place = jnp.where((outer == part) & (spot < 3 * channels), cell, -9)
        place = jnp.broadcast_to(jnp.where(beyond < 0, row % half, place), (hid, cols))
        for z in range(half):
            t1_ref[part, z * hid : (z + 1) * hid, :] = banded(spread, place, z - 1)
    rows3, cols3 = t3_ref.shape
    taps = rows3 // nz
    pick = (iota((hid, cols3), 0) == iota((hid, cols3), 1) % hid).astype(BF16)
    offset = iota((nz, cols3), 1) // hid - iota((nz, cols3), 0)
    spread = []
    for a in range(3):
        stack = jnp.concatenate(
            [w3_ref[a, b, d].astype(F32) for b in range(3) for d in range(3)], axis=0
        ).astype(BF16)
        spread.append(mm(stack, pick))
    for r in range(taps):
        rows = [jnp.broadcast_to(spread[a][r : r + 1], (nz, cols3)) for a in range(3)]
        t3_ref[r * nz : (r + 1) * nz, :] = banded(rows, offset, -1)
    kr, ki = zk_ref[0], zk_ref[1]
    top = jnp.concatenate([kr, -ki], axis=1)
    bottom = jnp.concatenate([ki, kr], axis=1)
    high, low = split(jnp.concatenate([top, bottom, bottom, -top], axis=0))
    z_ref[...] = jnp.concatenate([high, high, low], axis=1)
    count, lanes = sp_ref.shape[1], sr_ref.shape[1]
    pick = (iota((count, lanes), 0) == iota((count, lanes), 1) // (lanes // count)).astype(F32)
    for part, ref in ((0, sr_ref), (1, si_ref)):
        ref[...] = lax.dot_general(
            sp_ref[part],
            pick,
            (((0,), (0,)), ((), ())),
            precision=lax.Precision.HIGHEST,
            preferred_element_type=F32,
        )
    ny = whole_ref.shape[3]
    deep = feat_ref.shape[0] // whole_ref.shape[0]
    classes = spread_classes(con_ref, whole_ref.shape[2:])
    for x in range(whole_ref.shape[0]):
        column = unpacked(whole_ref, x, classes)
        if x == 0:
            pol_ref[...] = jnp.concatenate(column[2:], axis=0)
        feat_ref[x * deep : (x + 1) * deep, :] = features_of(column, ny)
    made = first_product(t1_ref, lambda x: feat_ref[x * deep : (x + 1) * deep, :], (0, 1))
    hid_ref[...] = gelu(made).astype(BF16)


def gelu(values):
    half = 0.5 * values
    return half + half * lax.erf(values * math.sqrt(0.5))


def corrector_kernel(
    con_ref, first_ref, second_ref, own_feat, own_hid, own_pol, t1_ref, t2_ref, t2m_ref, t3_ref,
    z_ref, dft_ref, green_ref, out_ref, feat, hid1, hid2,
):
    nz, ny = first_ref.shape[2:]
    ahead = first_ref.shape[0] + second_ref.shape[0]
    xl = first_ref.shape[0]
    depth = feat.shape[0] // ahead
    half = hid1.shape[0] // 2
    hid = 2 * half // nz
    tall = half - hid
    deep = 2 * nz
    classes = spread_classes(con_ref, (nz, ny))
    own = {}
    last = {}

    def features(place):
        if place < 2:
            column = [second_ref[place, i] for i in range(4)]
        else:
            column = unpacked(first_ref, place - 2, classes)
        if place > 2:
            own[place - 3] = jnp.concatenate(column[2:], axis=0)
        feat[place * depth : (place + 1) * depth, :] = features_of(column, ny)

    def feature_rows(place):
        if place < ahead:
            return feat[place * depth : (place + 1) * depth, :]
        return own_feat[(place - ahead) * depth : (place - ahead + 1) * depth, :]

    def first_layer(j):
        return first_product(t1_ref, feature_rows, (j, j + 1))

    def first_done(j, made):
        hid1[:, j * ny : (j + 2) * ny] = gelu(made).astype(BF16)

    def hidden(place, top, bottom):
        if place < ahead:
            return hid1[top:bottom, place * ny : (place + 1) * ny]
        return own_hid[top:bottom, (place - ahead) * ny : (place - ahead + 1) * ny]

    def tap_sum(weights, top, bottom, j):
        window = [
            jnp.concatenate([hidden(j + b + i, top, bottom) for i in range(2)], axis=1) for b in range(3)
        ]
        made = mm(weights, jnp.concatenate(window, axis=0))
        rows = weights.shape[0] // 3
        sides = []
        for i in range(2):
            lanes = slice(i * ny, (i + 1) * ny)
            sides.append(
                pltpu.roll(made[:rows, lanes], 1, 1)
                + made[rows : 2 * rows, lanes]
                + pltpu.roll(made[2 * rows :, lanes], ny - 1, 1)
            )
        return jnp.concatenate(sides, axis=1)

    def second_layer(j):
        return [
            tap_sum(t2_ref[0], 0, half, j),
            tap_sum(t2m_ref[...], half - 2 * hid, half + 2 * hid, j),
            tap_sum(t2_ref[1], half, 2 * half, j),
        ]

    def second_done(j, made):
        lanes = slice(j * ny, (j + 2) * ny)
        for top, part in zip((0, tall, tall + 2 * hid), made):
            hid2[top : top + part.shape[0], lanes] = gelu(part).astype(BF16)

    def third_layer(j):
        made = mm(t3_ref[...], hid2[:, j * ny : (j + 2) * ny])
        last[j], last[j + 1] = made[:, :ny], made[:, ny:]

    def source(x):
        parts = []
        for d in range(3):
            total = None
            for b in range(3):
                top = (b * 3 + d) * deep
                piece = last[x + b][top : top + deep]
                total = piece if total is None else total + piece
            parts.append(total)
        return own[x] + (pltpu.roll(parts[0], 1, 1) + parts[1] + pltpu.roll(parts[2], ny - 1, 1))

    def transformed(places):
        lifted = mm(z_ref[...], right_split(jnp.concatenate([source(x) for x in places], axis=1)))
        plain, turned = [], []
        for i in range(len(places)):
            plain.append(lifted[:deep, i * ny : (i + 1) * ny])
            turned.append(lifted[deep:, i * ny : (i + 1) * ny])
        both = [jnp.concatenate(plain, axis=0), jnp.concatenate(turned, axis=0)]
        return mm(left_split(jnp.concatenate(both, axis=1)), dft_ref[...])

    own[xl - 1] = own_pol[...]
    pairs = range(ahead - 2, -1, -2)
    for j in pairs:
        features(j)
        features(j + 1)
    for j in pairs:
        first_done(j, first_layer(j))
    for j in pairs:
        second_done(j, second_layer(j))
    for j in pairs:
        third_layer(j)
    out_ref[...] = jnp.transpose(transformed(range(xl))).reshape(out_ref.shape)


def green_kernel(fwd_ref, inv_ref, sr_ref, si_ref, green_ref):
    nx = inv_ref.shape[0]
    table = fwd_ref[:, :nx].astype(F32) + fwd_ref[:, 2 * nx :].astype(F32)
    cos, sin = table[:nx], table[nx:]
    count = green_ref.shape[0] // nx
    inner = sr_ref.shape[1] // count
    for q in range(count):
        re, im = sr_ref[:, q * inner : q * inner + 1], si_ref[:, q * inner : q * inner + 1]
        same, cross = re * cos + im * sin, re * sin - im * cos
        top = jnp.concatenate([same, -cross], axis=1)
        bottom = jnp.concatenate([cross, same], axis=1)
        high, low = split(mm(inv_ref[...], right_split(jnp.concatenate([top, bottom], axis=0))))
        green_ref[q * nx : (q + 1) * nx, :] = jnp.concatenate([high, high, low], axis=1)


def spectral_kernel(nz, in_ref, green_ref, out_ref):
    values = swap_blocks(in_ref, in_ref.shape[1])
    both = jnp.concatenate([values, turned(values, nz)], axis=0)
    made = mm(green_ref[...], right_split(both))
    nx, lanes = values.shape
    count = made.shape[0] // nx
    block = iota((nx, lanes), 1) // (lanes // count)
    total = made[:nx]
    for q in range(1, count):
        total = jnp.where(block == q, made[q * nx : (q + 1) * nx], total)
    out_ref[...] = total.reshape(out_ref.shape)


def finish_kernel(nz, in_ref, tab_ref, inc_ref, out_ref):
    made = mm(tab_ref[...], right_split(swap_blocks(in_ref, in_ref.shape[1])))
    ny = made.shape[0] // 2
    field = jnp.transpose(made[:ny] + turned(made[ny:], nz))
    for x in range(out_ref.shape[2]):
        for part in range(2):
            first = (2 * x + part) * nz
            out_ref[part, :, x, :] = inc_ref[part, :, x, :] + field[first : first + nz, :]


def call(kernel, out_shapes, args, scratch=(), flops=0):
    vmem = pl.BlockSpec(memory_space=pltpu.VMEM)
    single = not isinstance(out_shapes, list)
    return pl.pallas_call(
        kernel,
        out_shape=out_shapes,
        in_specs=[vmem] * len(args),
        out_specs=vmem if single else [vmem] * len(out_shapes),
        scratch_shapes=scratch,
        compiler_params=pltpu.CompilerParams(vmem_limit_bytes=VMEM_LIMIT),
        cost_estimate=pl.CostEstimate(flops=flops, bytes_accessed=4 * 1024 * 1024, transcendentals=0),
    )(*args)


def lane_device(incident, material, contrast, w_first, w_middle, w_last, z_kernel, spectral):
    count = lax.axis_size("gx")
    nz, xl, ny = material.shape
    hid = w_middle.shape[0]
    ql, nx = spectral.shape[1], spectral.shape[2]
    struct = jax.ShapeDtypeStruct
    classes = jnp.transpose(contrast)
    still = ((0, 0),) * 3
    own = jnp.pad(material[None], ((2, 1),) + still).astype(F32) + jnp.pad(incident, ((0, 2),) + still)
    parts, kinds = classes.shape
    own += jnp.pad(classes[None, None], ((3, 0), (0, nz - 1), (0, xl - parts), (0, ny - kinds)))
    whole = call(pack_kernel, struct((xl, 5, nz, ny), BF16), (own,), flops=10**6)
    first = lax.ppermute(whole, "gx", [(i, (i + 1) % count) for i in range(count)])
    near = call(
        functools.partial(near_kernel, kinds), struct((2, 4, nz, ny), BF16), (own, whole), flops=10**6
    )
    second = lax.ppermute(near, "gx", [(i, (i + 2) % count) for i in range(count)])
    lanes = 2 * nz * xl
    depth, deep = 6 * nz + 32, 12 * nz + 32
    dft, fwd, inv = call(
        functools.partial(table_kernel, xl, 3),
        [struct((6 * ny, ny), BF16), struct((2 * nx, 3 * nx), BF16), struct((nx, 6 * nx), BF16)],
        (),
        flops=10**9,
    )
    t1, t2, t2m, t3, zmat, sr, si, feat, hidden, pol = call(
        functools.partial(weight_kernel, nz),
        [
            struct((2, nz // 2 * hid, 3 * depth), BF16),
            struct((2, 3 * (nz // 2 - 1) * hid, 3 * nz // 2 * hid), BF16),
            struct((6 * hid, 12 * hid), BF16),
            struct((18 * nz, nz * hid), BF16),
            struct((4 * nz, 6 * nz), BF16),
            struct((nx, ql * 2 * nz), F32),
            struct((nx, ql * 2 * nz), F32),
            struct((xl * deep, ny), BF16),
            struct((nz * hid, 2 * ny), BF16),
            struct((2 * nz, ny), F32),
        ],
        (
            classes,
            whole,
            jnp.transpose(w_first, (2, 3, 4, 1, 0)),
            jnp.transpose(w_middle, (2, 3, 4, 0, 1)),
            jnp.transpose(w_last, (2, 3, 4, 0, 1)),
            z_kernel,
            spectral,
            dft,
        ),
        flops=10**9,
    )
    green = call(
        green_kernel, struct((ql * nx, 6 * nx), BF16), (fwd, inv, sr, si), flops=10**9
    )
    spectrum = call(
        corrector_kernel,
        struct((count, ql, lanes), F32),
        (classes, first, second, feat, hidden, pol, t1, t2, t2m, t3, zmat, dft, green),
        scratch=[
            pltpu.VMEM(((xl + 2) * deep, ny), BF16),
            pltpu.VMEM((nz * hid, (xl + 2) * ny), BF16),
            pltpu.VMEM((nz * hid, (xl + 2) * ny), BF16),
        ],
        flops=10**9,
    )
    piece = lax.all_to_all(spectrum, "gx", 0, 0, tiled=True)
    spread = call(
        functools.partial(spectral_kernel, nz),
        struct((count, xl, lanes), F32),
        (piece, green),
        flops=10**8,
    )
    rows = lax.all_to_all(spread, "gx", 0, 0, tiled=True)
    return call(
        functools.partial(finish_kernel, nz),
        struct(incident.shape, F32),
        (rows, fwd, incident),
        flops=10**8,
    )


def per_device(incident, material, contrast, w_first, w_middle, w_last, z_kernel, spectral):
    nz, xl, ny = material.shape
    ql, nx = spectral.shape[1], spectral.shape[2]
    lanes = (
        lax.axis_size("gy") == 1
        and ny == 128
        and nx == 128
        and xl == 4
        and ql == 4
        and 2 * nz * xl == 128
        and w_middle.shape[0] == 32
    )
    device = lane_device if lanes else general_device
    return device(incident, material, contrast, w_first, w_middle, w_last, z_kernel, spectral)


def solution(mesh):
    placed = (
        P("grp", None, "gx", "gy"),
        P("grp", "gx", "gy"),
        P("grp", None),
        P(),
        P(),
        P(),
        P("grp", None, None),
        P("grp", "gx", None),
    )
    return jax.shard_map(
        per_device,
        mesh=mesh,
        in_specs=placed,
        out_specs=P("grp", None, "gx", "gy"),
        check_vma=False,
    )
```

```python
import functools
import math

import jax
import jax.numpy as jnp
from jax import lax
from jax.experimental import pallas as pl
from jax.experimental.pallas import tpu as pltpu
from jax.sharding import PartitionSpec as P

F32 = jnp.float32
BF16 = jnp.bfloat16
VMEM_LIMIT = 48 * 1024 * 1024


def padded_2(x, sides, width):
    for axis, dim in sides:
        count, length = (lax.axis_size(axis), x.shape[dim])
        up = [(i, (i + 1) % count) for i in range(count)]
        down = [(j, i) for i, j in up]
        last = lax.slice_in_dim(x, length - width, length, axis=dim)
        leading = lax.slice_in_dim(x, 0, width, axis=dim)
        before = lax.ppermute(last, axis, up)
        after = lax.ppermute(leading, axis, down)
        x = jnp.concatenate([before, x, after], axis=dim)
    return x


def conv_layer(values, weights):
    return lax.conv_general_dilated(
        values[None],
        weights,
        (1, 1, 1),
        ((1, 1), (0, 0), (0, 0)),
        dimension_numbers=("NCDHW", "OIDHW", "NCDHW"),
        preferred_element_type=jnp.float32,
    )[0]


def activate(values):
    return jax.nn.gelu(values, approximate=False).astype(jnp.bfloat16)


def dft_tables(length):
    positions = jnp.arange(length, dtype=jnp.int32)
    product = positions[:, None] * positions[None, :] % length
    angle = product.astype(jnp.float32) * (2.0 * math.pi / length)
    return (jnp.cos(angle), jnp.sin(angle))


def green_apply(source, z_kernel, spectral):
    high = lax.Precision.HIGHEST
    kr, ki = (z_kernel[0], z_kernel[1])
    lre = jnp.einsum("zw,wxy->zxy", kr, source[0], precision=high) - jnp.einsum(
        "zw,wxy->zxy", ki, source[1], precision=high
    )
    lim = jnp.einsum("zw,wxy->zxy", kr, source[1], precision=high) + jnp.einsum(
        "zw,wxy->zxy", ki, source[0], precision=high
    )
    columns = lax.all_to_all(jnp.stack([lre, lim]), "gy", split_axis=1, concat_axis=3, tiled=True)
    count_y = columns.shape[3]
    cos_y, sin_y = dft_tables(count_y)
    fwd_re = jnp.dot(columns[0], cos_y, precision=high) + jnp.dot(columns[1], sin_y, precision=high)
    fwd_im = jnp.dot(columns[1], cos_y, precision=high) - jnp.dot(columns[0], sin_y, precision=high)
    count_x = columns.shape[2] * lax.axis_size("gx")
    cos_x, sin_x = dft_tables(count_x)
    piece = lax.all_to_all(
        jnp.stack([fwd_re, fwd_im]), "gx", split_axis=3, concat_axis=2, tiled=True
    )
    ar = jnp.einsum("zxk,xq->zkq", piece[0], cos_x, precision=high) + jnp.einsum(
        "zxk,xq->zkq", piece[1], sin_x, precision=high
    )
    ai = jnp.einsum("zxk,xq->zkq", piece[1], cos_x, precision=high) - jnp.einsum(
        "zxk,xq->zkq", piece[0], sin_x, precision=high
    )
    br = spectral[0] * ar - spectral[1] * ai
    bi = spectral[0] * ai + spectral[1] * ar
    gr = jnp.einsum("zkq,qx->zxk", br, cos_x, precision=high) - jnp.einsum(
        "zkq,qx->zxk", bi, sin_x, precision=high
    )
    gi = jnp.einsum("zkq,qx->zxk", bi, cos_x, precision=high) + jnp.einsum(
        "zkq,qx->zxk", br, sin_x, precision=high
    )
    spread = jnp.stack([gr, gi]) / count_x
    rows = lax.all_to_all(spread, "gx", split_axis=2, concat_axis=3, tiled=True)
    inv_re = jnp.dot(rows[0], cos_y, precision=high) - jnp.dot(rows[1], sin_y, precision=high)
    inv_im = jnp.dot(rows[1], cos_y, precision=high) + jnp.dot(rows[0], sin_y, precision=high)
    scattered = jnp.stack([inv_re, inv_im]) / count_y
    return lax.all_to_all(scattered, "gy", split_axis=3, concat_axis=1, tiled=True)


def general_device(incident, material, contrast, w_first, w_middle, w_last, z_kernel, spectral):
    high = lax.Precision.HIGHEST
    classes = contrast.shape[0]
    selector = (material[None] == jnp.arange(classes, dtype=jnp.int32)[:, None, None, None]).astype(
        jnp.float32
    )
    chi_re = jnp.einsum("k,kzxy->zxy", contrast[:, 0], selector, precision=high)
    chi_im = jnp.einsum("k,kzxy->zxy", contrast[:, 1], selector, precision=high)
    field = incident
    pol_re = chi_re * field[0] - chi_im * field[1]
    pol_im = chi_re * field[1] + chi_im * field[0]
    features = jnp.stack([field[0], field[1], pol_re, pol_im]).astype(jnp.bfloat16)
    padded = padded_2(features, (("gx", 2), ("gy", 3)), 3)
    hidden = activate(conv_layer(padded, w_first))
    hidden = activate(conv_layer(hidden, w_middle))
    correction = conv_layer(hidden, w_last)
    source = jnp.stack([pol_re, pol_im]) + correction
    field = incident + green_apply(source, z_kernel, spectral)
    return field


def split(values):
    high = values.astype(BF16)
    low = (values - high.astype(F32)).astype(BF16)
    return high, low


def cosine(steps, length):
    turn = 2.0 * math.pi / length
    angle = (length // 4 - jnp.minimum(steps, length - steps)).astype(F32) * turn
    square = angle * angle
    total = jnp.full_like(angle, 1.0 / math.factorial(13))
    for power in (11, 9, 7, 5, 3, 1):
        sign = 1.0 if power % 4 == 1 else -1.0
        total = total * square + sign / math.factorial(power)
    return total * angle


def dft_parts(rows, cols, length, axis, along, scale=1.0):
    steps = lax.rem(rows * cols, length)
    later = lax.rem(steps + 3 * length // 4, length)
    high, low = split(jnp.concatenate([cosine(steps, length), cosine(later, length)], axis=axis) * scale)
    return jnp.concatenate([high, high, low], axis=along)


def left_split(values):
    high, low = split(values)
    return jnp.concatenate([high, low, high], axis=1)


def right_split(values):
    high, low = split(values)
    return jnp.concatenate([high, low, high], axis=0)


def mm(a, b):
    return jnp.dot(a, b, preferred_element_type=F32)


def iota(shape, dim):
    return lax.broadcasted_iota(jnp.int32, shape, dim)


def turned(values, nz):
    real = (iota(values.shape, 1) // nz) % 2 == 0
    ahead = pltpu.roll(values, values.shape[1] - nz, 1)
    return jnp.where(real, -ahead, pltpu.roll(values, nz, 1))


def mixed(made, nz, sign):
    half = made.shape[1] // 2
    blocks = []
    for top in range(0, made.shape[0], 2 * nz):
        re, im = made[top : top + nz], made[top + nz : top + 2 * nz]
        blocks.append(re[:, :half] + sign * im[:, half:])
        blocks.append(im[:, :half] - sign * re[:, half:])
    return blocks


def swap_blocks(ref, count):
    pieces = [ref[:, q, :] for q in range(count)]
    inner = pieces[0].shape[1] // count
    block = iota(pieces[0].shape, 1) // inner
    places = [block == q for q in range(count)]

    def chosen(options):
        total = options[0]
        for place, option in zip(places[1:], options[1:]):
            total = jnp.where(place, option, total)
        return total

    moved = []
    for step in range(count):
        total = chosen([pieces[(x + step) % count] for x in range(count)])
        moved.append(pltpu.roll(total, step * inner, 1) if step else total)
    rows = [chosen([moved[(q - x) % count] for q in range(count)]) for x in range(count)]
    return jnp.concatenate(rows, axis=0)


def spread_classes(con_ref, shape):
    return [
        [jnp.broadcast_to(con_ref[part : part + 1, k : k + 1], shape) for part in range(2)]
        for k in range(con_ref.shape[1])
    ]


def unpacked(ref, x, classes):
    high_re, high_im, cells, low_re, low_im = [ref[x, i].astype(F32) for i in range(5)]
    re, im = high_re + low_re, high_im + low_im
    chi_re = jnp.zeros_like(re)
    chi_im = jnp.zeros_like(re)
    for k, (class_re, class_im) in enumerate(classes):
        here = cells == float(k)
        chi_re = jnp.where(here, class_re, chi_re)
        chi_im = jnp.where(here, class_im, chi_im)
    return [high_re, high_im, chi_re * re - chi_im * im, chi_re * im + chi_im * re]


def pack_kernel(own_ref, whole_ref):
    for x in range(own_ref.shape[2]):
        for i in range(3):
            high, low = split(own_ref[i, :, x, :])
            whole_ref[x, i] = high
            if i < 2:
                whole_ref[x, i + 3] = low


def near_kernel(class_count, own_ref, whole_ref, near_ref):
    xl, _, nz, ny = whole_ref.shape
    classes = [
        [jnp.broadcast_to(own_ref[3, 0, part : part + 1, k : k + 1], (nz, ny)) for part in range(2)]
        for k in range(class_count)
    ]
    for x in range(2):
        for i, plane in enumerate(unpacked(whole_ref, xl - 2 + x, classes)):
            near_ref[x, i] = plane.astype(BF16)


def table_kernel(xl, shift, dft_ref, fwd_ref, inv_ref, back_ref):
    nx, ny = inv_ref.shape[0], dft_ref.shape[1] // 2
    dft_ref[...] = dft_parts(iota((ny, ny), 0), iota((ny, ny), 1), ny, 1, 0)
    first, second = iota((nx, nx), 0), iota((nx, nx), 1)
    inv_ref[...] = dft_parts(lax.rem(first + shift, nx), second, nx, 1, 1, 1.0 / (nx * ny))
    count = nx // xl
    second = lax.rem(second, count) * xl + second // count
    fwd_ref[...] = dft_parts(first, second, nx, 0, 1)
    first, second = iota((ny, ny), 0), iota((ny, ny), 1)
    count = ny // xl
    back_ref[...] = dft_parts(lax.rem(first, count) * xl + first // count, second, ny, 1, 0)


def features_of(column, ny):
    planes = [plane.astype(F32) for plane in column]
    half = planes[0].shape[0] // 2
    lower = jnp.concatenate([plane[:half] for plane in planes], axis=0)
    upper = jnp.concatenate([plane[half:] for plane in planes], axis=0)
    rows = [plane[half : half + 1] for plane in planes] + [plane[half - 1 : half] for plane in planes]
    edge = jnp.concatenate(rows, axis=0)
    made = []
    for part in (lower, upper, edge):
        made += [pltpu.roll(part, 1, 1), part, pltpu.roll(part, ny - 1, 1)]
    return jnp.concatenate(made + [jnp.zeros_like(edge)], axis=0).astype(BF16)


def first_product(t1_ref, rows_of, places):
    made = []
    depth = t1_ref.shape[2] // 3
    for part in range(2):
        pieces = []
        for place in places:
            taps = []
            for b in range(3):
                rows = rows_of(place + b)
                edge = 2 * depth - rows.shape[0]
                main = depth - edge
                taps += [rows[part * main : (part + 1) * main], rows[2 * main :]]
            pieces.append(jnp.concatenate(taps, axis=0))
        made.append(mm(t1_ref[part], jnp.concatenate(pieces, axis=1)))
    return jnp.concatenate(made, axis=0)


def banded(spread, place, start):
    rows = jnp.zeros_like(spread[0])
    for a in range(3):
        rows = jnp.where(place == start + a, spread[a], rows)
    return rows.astype(BF16)


def weight_kernel(
    nz, con_ref, whole_ref, w1_ref, w2_ref, w3_ref, zk_ref, sp_ref, dft_ref,
    t1_ref, t2_ref, t2m_ref, t3_ref, z_ref, sr_ref, si_ref, feat_ref, hid_ref, pol_ref,
):
    hid = w2_ref.shape[3]
    half = nz // 2
    wide = half * hid
    pick = (iota((hid, wide), 0) == iota((hid, wide), 1) % hid).astype(BF16)
    place = iota((hid, wide), 1) // hid
    tall = (half - 1) * hid
    for b in range(3):
        for d in range(3):
            spread = [mm(w2_ref[a, b, d], pick) for a in range(3)]
            for r in range(half):
                block = banded(spread, place, r - 1)
                lanes = slice(b * wide, (b + 1) * wide)
                if r < half - 1:
                    t2_ref[0, d * tall + r * hid : d * tall + (r + 1) * hid, lanes] = block
                if r > 0:
                    t2_ref[1, d * tall + (r - 1) * hid : d * tall + r * hid, lanes] = block
                if 0 < r < 3:
                    top = (d * 2 + r - 1) * hid
                    t2m_ref[top : top + hid, b * 4 * hid : (b + 1) * 4 * hid] = block[:, : 4 * hid]
    channels = w1_ref.shape[3]
    taps, cols = 9 * channels, t1_ref.shape[2]
    depth = cols // 3
    main = 3 * channels * half
    row = iota((1, cols), 1) % depth
    beyond = row - main
    spot = jnp.where(beyond < 0, row // half, beyond // (2 * channels) * channels + beyond % channels)
    tap = iota((1, cols), 1) // depth * 3 * channels + spot
    pick = (iota((taps, cols), 0) == tap).astype(BF16)
    spread = []
    for a in range(3):
        stack = jnp.concatenate(
            [w1_ref[a, b, d].astype(F32) for b in range(3) for d in range(3)], axis=0
        ).astype(BF16)
        spread.append(
            lax.dot_general(stack, pick, (((0,), (0,)), ((), ())), preferred_element_type=F32)
        )
    outer = beyond % (2 * channels) // channels
    for part, cell in ((0, half), (1, -1)):
        place = jnp.where((outer == part) & (spot < 3 * channels), cell, -9)
        place = jnp.broadcast_to(jnp.where(beyond < 0, row % half, place), (hid, cols))
        for z in range(half):
            t1_ref[part, z * hid : (z + 1) * hid, :] = banded(spread, place, z - 1)
    rows3, cols3 = t3_ref.shape
    taps = rows3 // nz
    pick = (iota((hid, cols3), 0) == iota((hid, cols3), 1) % hid).astype(BF16)
    offset = iota((nz, cols3), 1) // hid - iota((nz, cols3), 0)
    spread = []
    for a in range(3):
        stack = jnp.concatenate(
            [w3_ref[a, b, d].astype(F32) for b in range(3) for d in range(3)], axis=0
        ).astype(BF16)
        spread.append(mm(stack, pick))
    for r in range(taps):
        rows = [jnp.broadcast_to(spread[a][r : r + 1], (nz, cols3)) for a in range(3)]
        t3_ref[r * nz : (r + 1) * nz, :] = banded(rows, offset, -1)
    kr, ki = zk_ref[0], zk_ref[1]
    top = jnp.concatenate([kr, -ki], axis=1)
    bottom = jnp.concatenate([ki, kr], axis=1)
    high, low = split(jnp.concatenate([top, bottom], axis=0))
    z_ref[...] = jnp.concatenate([high, high, low], axis=1)
    count, lanes = sp_ref.shape[1], sr_ref.shape[1]
    pick = (iota((count, lanes), 0) == iota((count, lanes), 1) // (lanes // count)).astype(F32)
    for part, ref in ((0, sr_ref), (1, si_ref)):
        ref[...] = lax.dot_general(
            sp_ref[part],
            pick,
            (((0,), (0,)), ((), ())),
            precision=lax.Precision.HIGHEST,
            preferred_element_type=F32,
        )
    ny = whole_ref.shape[3]
    deep = feat_ref.shape[0] // whole_ref.shape[0]
    classes = spread_classes(con_ref, whole_ref.shape[2:])
    for x in range(whole_ref.shape[0]):
        column = unpacked(whole_ref, x, classes)
        if x == 0:
            pol_ref[...] = jnp.concatenate(column[2:], axis=0)
        feat_ref[x * deep : (x + 1) * deep, :] = features_of(column, ny)
    made = first_product(t1_ref, lambda x: feat_ref[x * deep : (x + 1) * deep, :], (0, 1))
    hid_ref[...] = gelu(made).astype(BF16)


def gelu(values):
    half = 0.5 * values
    return half + half * lax.erf(values * math.sqrt(0.5))


def corrector_kernel(
    con_ref, first_ref, second_ref, own_feat, own_hid, own_pol, t1_ref, t2_ref, t2m_ref, t3_ref,
    z_ref, dft_ref, green_ref, out_ref, feat, hid1, hid2,
):
    nz, ny = first_ref.shape[2:]
    ahead = first_ref.shape[0] + second_ref.shape[0]
    xl = first_ref.shape[0]
    depth = feat.shape[0] // ahead
    half = hid1.shape[0] // 2
    hid = 2 * half // nz
    tall = half - hid
    deep = 2 * nz
    classes = spread_classes(con_ref, (nz, ny))
    own = {}
    last = {}

    def features(place):
        if place < 2:
            column = [second_ref[place, i] for i in range(4)]
        else:
            column = unpacked(first_ref, place - 2, classes)
        if place > 2:
            own[place - 3] = jnp.concatenate(column[2:], axis=0)
        feat[place * depth : (place + 1) * depth, :] = features_of(column, ny)

    def feature_rows(place):
        if place < ahead:
            return feat[place * depth : (place + 1) * depth, :]
        return own_feat[(place - ahead) * depth : (place - ahead + 1) * depth, :]

    def first_layer(j):
        return first_product(t1_ref, feature_rows, (j, j + 1))

    def first_done(j, made):
        hid1[:, j * ny : (j + 2) * ny] = gelu(made).astype(BF16)

    def hidden(place, top, bottom):
        if place < ahead:
            return hid1[top:bottom, place * ny : (place + 1) * ny]
        return own_hid[top:bottom, (place - ahead) * ny : (place - ahead + 1) * ny]

    def tap_sum(weights, top, bottom, j):
        window = [
            jnp.concatenate([hidden(j + b + i, top, bottom) for i in range(2)], axis=1) for b in range(3)
        ]
        made = mm(weights, jnp.concatenate(window, axis=0))
        rows = weights.shape[0] // 3
        sides = []
        for i in range(2):
            lanes = slice(i * ny, (i + 1) * ny)
            sides.append(
                pltpu.roll(made[:rows, lanes], 1, 1)
                + made[rows : 2 * rows, lanes]
                + pltpu.roll(made[2 * rows :, lanes], ny - 1, 1)
            )
        return jnp.concatenate(sides, axis=1)

    def second_layer(j):
        return [
            tap_sum(t2_ref[0], 0, half, j),
            tap_sum(t2m_ref[...], half - 2 * hid, half + 2 * hid, j),
            tap_sum(t2_ref[1], half, 2 * half, j),
        ]

    def second_done(j, made):
        lanes = slice(j * ny, (j + 2) * ny)
        for top, part in zip((0, tall, tall + 2 * hid), made):
            hid2[top : top + part.shape[0], lanes] = gelu(part).astype(BF16)

    def third_layer(j):
        made = mm(t3_ref[...], hid2[:, j * ny : (j + 2) * ny])
        last[j], last[j + 1] = made[:, :ny], made[:, ny:]

    def source(x):
        parts = []
        for d in range(3):
            total = None
            for b in range(3):
                top = (b * 3 + d) * deep
                piece = last[x + b][top : top + deep]
                total = piece if total is None else total + piece
            parts.append(total)
        return own[x] + (pltpu.roll(parts[0], 1, 1) + parts[1] + pltpu.roll(parts[2], ny - 1, 1))

    def transformed(places):
        lifted = mm(z_ref[...], right_split(jnp.concatenate([source(x) for x in places], axis=1)))
        rows = [lifted[:, i * ny : (i + 1) * ny] for i in range(len(places))]
        made = mm(left_split(jnp.concatenate(rows, axis=0)), dft_ref[...])
        return jnp.concatenate(mixed(made, nz, 1.0), axis=0)

    own[xl - 1] = own_pol[...]
    pairs = range(ahead - 2, -1, -2)
    for j in pairs:
        features(j)
        features(j + 1)
    for j in pairs:
        first_done(j, first_layer(j))
    for j in pairs:
        second_done(j, second_layer(j))
    for j in pairs:
        third_layer(j)
    out_ref[...] = jnp.transpose(transformed(range(xl))).reshape(out_ref.shape)


def green_kernel(fwd_ref, inv_ref, sr_ref, si_ref, green_ref):
    nx = inv_ref.shape[0]
    table = fwd_ref[:, :nx].astype(F32) + fwd_ref[:, 2 * nx :].astype(F32)
    cos, sin = table[:nx], table[nx:]
    count = green_ref.shape[0] // nx
    inner = sr_ref.shape[1] // count
    for q in range(count):
        re, im = sr_ref[:, q * inner : q * inner + 1], si_ref[:, q * inner : q * inner + 1]
        same, cross = re * cos + im * sin, re * sin - im * cos
        top = jnp.concatenate([same, -cross], axis=1)
        bottom = jnp.concatenate([cross, same], axis=1)
        high, low = split(mm(inv_ref[...], right_split(jnp.concatenate([top, bottom], axis=0))))
        green_ref[q * nx : (q + 1) * nx, :] = jnp.concatenate([high, high, low], axis=1)


def spectral_kernel(nz, in_ref, green_ref, out_ref):
    values = swap_blocks(in_ref, in_ref.shape[1])
    both = jnp.concatenate([values, turned(values, nz)], axis=0)
    made = mm(green_ref[...], right_split(both))
    nx, lanes = values.shape
    count = made.shape[0] // nx
    block = iota((nx, lanes), 1) // (lanes // count)
    total = made[:nx]
    for q in range(1, count):
        total = jnp.where(block == q, made[q * nx : (q + 1) * nx], total)
    out_ref[...] = total.reshape(out_ref.shape)


def finish_kernel(nz, in_ref, back_ref, inc_ref, out_ref):
    values = jnp.transpose(swap_blocks(in_ref, in_ref.shape[1]))
    blocks = mixed(mm(left_split(values), back_ref[...]), nz, -1.0)
    for x in range(inc_ref.shape[2]):
        for part in range(2):
            out_ref[part, :, x, :] = inc_ref[part, :, x, :] + blocks[2 * x + part]


def call(kernel, out_shapes, args, scratch=(), flops=0):
    vmem = pl.BlockSpec(memory_space=pltpu.VMEM)
    single = not isinstance(out_shapes, list)
    return pl.pallas_call(
        kernel,
        out_shape=out_shapes,
        in_specs=[vmem] * len(args),
        out_specs=vmem if single else [vmem] * len(out_shapes),
        scratch_shapes=scratch,
        compiler_params=pltpu.CompilerParams(vmem_limit_bytes=VMEM_LIMIT),
        cost_estimate=pl.CostEstimate(flops=flops, bytes_accessed=4 * 1024 * 1024, transcendentals=0),
    )(*args)


def lane_device(incident, material, contrast, w_first, w_middle, w_last, z_kernel, spectral):
    count = lax.axis_size("gx")
    nz, xl, ny = material.shape
    hid = w_middle.shape[0]
    ql, nx = spectral.shape[1], spectral.shape[2]
    struct = jax.ShapeDtypeStruct
    classes = jnp.transpose(contrast)
    still = ((0, 0),) * 3
    own = jnp.pad(material[None], ((2, 1),) + still).astype(F32) + jnp.pad(incident, ((0, 2),) + still)
    parts, kinds = classes.shape
    own += jnp.pad(classes[None, None], ((3, 0), (0, nz - 1), (0, xl - parts), (0, ny - kinds)))
    whole = call(pack_kernel, struct((xl, 5, nz, ny), BF16), (own,), flops=10**6)
    first = lax.ppermute(whole, "gx", [(i, (i + 1) % count) for i in range(count)])
    near = call(
        functools.partial(near_kernel, kinds), struct((2, 4, nz, ny), BF16), (own, whole), flops=10**6
    )
    second = lax.ppermute(near, "gx", [(i, (i + 2) % count) for i in range(count)])
    lanes = 2 * nz * xl
    depth, deep = 6 * nz + 32, 12 * nz + 32
    dft, fwd, inv, back = call(
        functools.partial(table_kernel, xl, 3),
        [
            struct((3 * ny, 2 * ny), BF16),
            struct((2 * nx, 3 * nx), BF16),
            struct((nx, 6 * nx), BF16),
            struct((3 * ny, 2 * ny), BF16),
        ],
        (),
        flops=10**9,
    )
    t1, t2, t2m, t3, zmat, sr, si, feat, hidden, pol = call(
        functools.partial(weight_kernel, nz),
        [
            struct((2, nz // 2 * hid, 3 * depth), BF16),
            struct((2, 3 * (nz // 2 - 1) * hid, 3 * nz // 2 * hid), BF16),
            struct((6 * hid, 12 * hid), BF16),
            struct((18 * nz, nz * hid), BF16),
            struct((2 * nz, 6 * nz), BF16),
            struct((nx, ql * 2 * nz), F32),
            struct((nx, ql * 2 * nz), F32),
            struct((xl * deep, ny), BF16),
            struct((nz * hid, 2 * ny), BF16),
            struct((2 * nz, ny), F32),
        ],
        (
            classes,
            whole,
            jnp.transpose(w_first, (2, 3, 4, 1, 0)),
            jnp.transpose(w_middle, (2, 3, 4, 0, 1)),
            jnp.transpose(w_last, (2, 3, 4, 0, 1)),
            z_kernel,
            spectral,
            dft,
        ),
        flops=10**9,
    )
    green = call(
        green_kernel, struct((ql * nx, 6 * nx), BF16), (fwd, inv, sr, si), flops=10**9
    )
    spectrum = call(
        corrector_kernel,
        struct((count, ql, lanes), F32),
        (classes, first, second, feat, hidden, pol, t1, t2, t2m, t3, zmat, dft, green),
        scratch=[
            pltpu.VMEM(((xl + 2) * deep, ny), BF16),
            pltpu.VMEM((nz * hid, (xl + 2) * ny), BF16),
            pltpu.VMEM((nz * hid, (xl + 2) * ny), BF16),
        ],
        flops=10**9,
    )
    piece = lax.all_to_all(spectrum, "gx", 0, 0, tiled=True)
    spread = call(
        functools.partial(spectral_kernel, nz),
        struct((count, xl, lanes), F32),
        (piece, green),
        flops=10**8,
    )
    rows = lax.all_to_all(spread, "gx", 0, 0, tiled=True)
    return call(
        functools.partial(finish_kernel, nz),
        struct(incident.shape, F32),
        (rows, back, incident),
        flops=10**8,
    )


def per_device(incident, material, contrast, w_first, w_middle, w_last, z_kernel, spectral):
    nz, xl, ny = material.shape
    ql, nx = spectral.shape[1], spectral.shape[2]
    lanes = (
        lax.axis_size("gy") == 1
        and ny == 128
        and nx == 128
        and xl == 4
        and ql == 4
        and 2 * nz * xl == 128
        and w_middle.shape[0] == 32
    )
    device = lane_device if lanes else general_device
    return device(incident, material, contrast, w_first, w_middle, w_last, z_kernel, spectral)


def solution(mesh):
    placed = (
        P("grp", None, "gx", "gy"),
        P("grp", "gx", "gy"),
        P("grp", None),
        P(),
        P(),
        P(),
        P("grp", None, None),
        P("grp", "gx", None),
    )
    return jax.shard_map(
        per_device,
        mesh=mesh,
        in_specs=placed,
        out_specs=P("grp", None, "gx", "gy"),
        check_vma=False,
    )
```

```python
import functools
import math

import jax
import jax.numpy as jnp
from jax import lax
from jax.experimental import pallas as pl
from jax.experimental.pallas import tpu as pltpu
from jax.sharding import PartitionSpec as P

F32 = jnp.float32
BF16 = jnp.bfloat16
VMEM_LIMIT = 48 * 1024 * 1024


def padded_2(x, sides, width):
    for axis, dim in sides:
        count, length = (lax.axis_size(axis), x.shape[dim])
        up = [(i, (i + 1) % count) for i in range(count)]
        down = [(j, i) for i, j in up]
        last = lax.slice_in_dim(x, length - width, length, axis=dim)
        leading = lax.slice_in_dim(x, 0, width, axis=dim)
        before = lax.ppermute(last, axis, up)
        after = lax.ppermute(leading, axis, down)
        x = jnp.concatenate([before, x, after], axis=dim)
    return x


def conv_layer(values, weights):
    return lax.conv_general_dilated(
        values[None],
        weights,
        (1, 1, 1),
        ((1, 1), (0, 0), (0, 0)),
        dimension_numbers=("NCDHW", "OIDHW", "NCDHW"),
        preferred_element_type=jnp.float32,
    )[0]


def activate(values):
    return jax.nn.gelu(values, approximate=False).astype(jnp.bfloat16)


def dft_tables(length):
    positions = jnp.arange(length, dtype=jnp.int32)
    product = positions[:, None] * positions[None, :] % length
    angle = product.astype(jnp.float32) * (2.0 * math.pi / length)
    return (jnp.cos(angle), jnp.sin(angle))


def green_apply(source, z_kernel, spectral):
    high = lax.Precision.HIGHEST
    kr, ki = (z_kernel[0], z_kernel[1])
    lre = jnp.einsum("zw,wxy->zxy", kr, source[0], precision=high) - jnp.einsum(
        "zw,wxy->zxy", ki, source[1], precision=high
    )
    lim = jnp.einsum("zw,wxy->zxy", kr, source[1], precision=high) + jnp.einsum(
        "zw,wxy->zxy", ki, source[0], precision=high
    )
    columns = lax.all_to_all(jnp.stack([lre, lim]), "gy", split_axis=1, concat_axis=3, tiled=True)
    count_y = columns.shape[3]
    cos_y, sin_y = dft_tables(count_y)
    fwd_re = jnp.dot(columns[0], cos_y, precision=high) + jnp.dot(columns[1], sin_y, precision=high)
    fwd_im = jnp.dot(columns[1], cos_y, precision=high) - jnp.dot(columns[0], sin_y, precision=high)
    count_x = columns.shape[2] * lax.axis_size("gx")
    cos_x, sin_x = dft_tables(count_x)
    piece = lax.all_to_all(
        jnp.stack([fwd_re, fwd_im]), "gx", split_axis=3, concat_axis=2, tiled=True
    )
    ar = jnp.einsum("zxk,xq->zkq", piece[0], cos_x, precision=high) + jnp.einsum(
        "zxk,xq->zkq", piece[1], sin_x, precision=high
    )
    ai = jnp.einsum("zxk,xq->zkq", piece[1], cos_x, precision=high) - jnp.einsum(
        "zxk,xq->zkq", piece[0], sin_x, precision=high
    )
    br = spectral[0] * ar - spectral[1] * ai
    bi = spectral[0] * ai + spectral[1] * ar
    gr = jnp.einsum("zkq,qx->zxk", br, cos_x, precision=high) - jnp.einsum(
        "zkq,qx->zxk", bi, sin_x, precision=high
    )
    gi = jnp.einsum("zkq,qx->zxk", bi, cos_x, precision=high) + jnp.einsum(
        "zkq,qx->zxk", br, sin_x, precision=high
    )
    spread = jnp.stack([gr, gi]) / count_x
    rows = lax.all_to_all(spread, "gx", split_axis=2, concat_axis=3, tiled=True)
    inv_re = jnp.dot(rows[0], cos_y, precision=high) - jnp.dot(rows[1], sin_y, precision=high)
    inv_im = jnp.dot(rows[1], cos_y, precision=high) + jnp.dot(rows[0], sin_y, precision=high)
    scattered = jnp.stack([inv_re, inv_im]) / count_y
    return lax.all_to_all(scattered, "gy", split_axis=3, concat_axis=1, tiled=True)


def general_device(incident, material, contrast, w_first, w_middle, w_last, z_kernel, spectral):
    high = lax.Precision.HIGHEST
    classes = contrast.shape[0]
    selector = (material[None] == jnp.arange(classes, dtype=jnp.int32)[:, None, None, None]).astype(
        jnp.float32
    )
    chi_re = jnp.einsum("k,kzxy->zxy", contrast[:, 0], selector, precision=high)
    chi_im = jnp.einsum("k,kzxy->zxy", contrast[:, 1], selector, precision=high)
    field = incident
    pol_re = chi_re * field[0] - chi_im * field[1]
    pol_im = chi_re * field[1] + chi_im * field[0]
    features = jnp.stack([field[0], field[1], pol_re, pol_im]).astype(jnp.bfloat16)
    padded = padded_2(features, (("gx", 2), ("gy", 3)), 3)
    hidden = activate(conv_layer(padded, w_first))
    hidden = activate(conv_layer(hidden, w_middle))
    correction = conv_layer(hidden, w_last)
    source = jnp.stack([pol_re, pol_im]) + correction
    field = incident + green_apply(source, z_kernel, spectral)
    return field


def split(values):
    high = values.astype(BF16)
    low = (values - high.astype(F32)).astype(BF16)
    return high, low


def cosine(steps, length):
    turn = 2.0 * math.pi / length
    angle = (length // 4 - jnp.minimum(steps, length - steps)).astype(F32) * turn
    square = angle * angle
    total = jnp.full_like(angle, 1.0 / math.factorial(13))
    for power in (11, 9, 7, 5, 3, 1):
        sign = 1.0 if power % 4 == 1 else -1.0
        total = total * square + sign / math.factorial(power)
    return total * angle


def dft_parts(rows, cols, length, axis, along, scale=1.0):
    steps = lax.rem(rows * cols, length)
    later = lax.rem(steps + 3 * length // 4, length)
    high, low = split(jnp.concatenate([cosine(steps, length), cosine(later, length)], axis=axis) * scale)
    return jnp.concatenate([high, high, low], axis=along)


def left_split(values):
    high, low = split(values)
    return jnp.concatenate([high, low, high], axis=1)


def right_split(values):
    high, low = split(values)
    return jnp.concatenate([high, low, high], axis=0)


def mm(a, b):
    return jnp.dot(a, b, preferred_element_type=F32)


def iota(shape, dim):
    return lax.broadcasted_iota(jnp.int32, shape, dim)


def turned(values, nz):
    real = (iota(values.shape, 1) // nz) % 2 == 0
    ahead = pltpu.roll(values, values.shape[1] - nz, 1)
    return jnp.where(real, -ahead, pltpu.roll(values, nz, 1))


def mixed(made, nz, sign):
    half = made.shape[1] // 2
    blocks = []
    for top in range(0, made.shape[0], 2 * nz):
        re, im = made[top : top + nz], made[top + nz : top + 2 * nz]
        blocks.append(re[:, :half] + sign * im[:, half:])
        blocks.append(im[:, :half] - sign * re[:, half:])
    return blocks


def swap_blocks(ref, count):
    pieces = [ref[:, q, :] for q in range(count)]
    inner = pieces[0].shape[1] // count
    block = iota(pieces[0].shape, 1) // inner
    places = [block == q for q in range(count)]

    def chosen(options):
        total = options[0]
        for place, option in zip(places[1:], options[1:]):
            total = jnp.where(place, option, total)
        return total

    moved = []
    for step in range(count):
        total = chosen([pieces[(x + step) % count] for x in range(count)])
        moved.append(pltpu.roll(total, step * inner, 1) if step else total)
    rows = [chosen([moved[(q - x) % count] for q in range(count)]) for x in range(count)]
    return jnp.concatenate(rows, axis=0)


def spread_classes(con_ref, shape):
    return [
        [jnp.broadcast_to(con_ref[part : part + 1, k : k + 1], shape) for part in range(2)]
        for k in range(con_ref.shape[1])
    ]


def unpacked(ref, x, classes):
    high_re, high_im, cells, low_re, low_im = [ref[x, i].astype(F32) for i in range(5)]
    re, im = high_re + low_re, high_im + low_im
    chi_re = jnp.zeros_like(re)
    chi_im = jnp.zeros_like(re)
    for k, (class_re, class_im) in enumerate(classes):
        here = cells == float(k)
        chi_re = jnp.where(here, class_re, chi_re)
        chi_im = jnp.where(here, class_im, chi_im)
    return [high_re, high_im, chi_re * re - chi_im * im, chi_re * im + chi_im * re]


def near_kernel(class_count, own_ref, whole_ref, near_ref):
    xl, _, nz, ny = whole_ref.shape
    classes = [
        [jnp.broadcast_to(own_ref[3, 0, part : part + 1, k : k + 1], (nz, ny)) for part in range(2)]
        for k in range(class_count)
    ]
    for x in range(2):
        for i, plane in enumerate(unpacked(whole_ref, xl - 2 + x, classes)):
            near_ref[x, i] = plane.astype(BF16)


def table_kernel(xl, shift, dft_ref, fwd_ref, inv_ref, back_ref):
    nx, ny = inv_ref.shape[0], dft_ref.shape[1] // 2
    dft_ref[...] = dft_parts(iota((ny, ny), 0), iota((ny, ny), 1), ny, 1, 0)
    first, second = iota((nx, nx), 0), iota((nx, nx), 1)
    inv_ref[...] = dft_parts(lax.rem(first + shift, nx), second, nx, 1, 1, 1.0 / (nx * ny))
    count = nx // xl
    second = lax.rem(second, count) * xl + second // count
    fwd_ref[...] = dft_parts(first, second, nx, 0, 1)
    first, second = iota((ny, ny), 0), iota((ny, ny), 1)
    count = ny // xl
    back_ref[...] = dft_parts(lax.rem(first, count) * xl + first // count, second, ny, 1, 0)


def features_of(column, ny):
    planes = [plane.astype(F32) for plane in column]
    half = planes[0].shape[0] // 2
    lower = jnp.concatenate([plane[:half] for plane in planes], axis=0)
    upper = jnp.concatenate([plane[half:] for plane in planes], axis=0)
    rows = [plane[half : half + 1] for plane in planes] + [plane[half - 1 : half] for plane in planes]
    edge = jnp.concatenate(rows, axis=0)
    made = []
    for part in (lower, upper, edge):
        made += [pltpu.roll(part, 1, 1), part, pltpu.roll(part, ny - 1, 1)]
    return jnp.concatenate(made + [jnp.zeros_like(edge)], axis=0).astype(BF16)


def first_product(t1_ref, rows_of, places):
    made = []
    depth = t1_ref.shape[2] // 3
    for part in range(2):
        pieces = []
        for place in places:
            taps = []
            for b in range(3):
                rows = rows_of(place + b)
                edge = 2 * depth - rows.shape[0]
                main = depth - edge
                taps += [rows[part * main : (part + 1) * main], rows[2 * main :]]
            pieces.append(jnp.concatenate(taps, axis=0))
        made.append(mm(t1_ref[part], jnp.concatenate(pieces, axis=1)))
    return jnp.concatenate(made, axis=0)


def banded(spread, place, start):
    rows = jnp.zeros_like(spread[0])
    for a in range(3):
        rows = jnp.where(place == start + a, spread[a], rows)
    return rows.astype(BF16)


def weight_kernel(
    nz, con_ref, whole_ref, w1_ref, w2_ref, w3_ref, zk_ref, sp_ref, dft_ref,
    t1_ref, t2_ref, t2m_ref, t3_ref, z_ref, sr_ref, si_ref, feat_ref, hid_ref, pol_ref,
):
    hid = w2_ref.shape[3]
    half = nz // 2
    wide = half * hid
    pick = (iota((hid, wide), 0) == iota((hid, wide), 1) % hid).astype(BF16)
    place = iota((hid, wide), 1) // hid
    tall = (half - 1) * hid
    for b in range(3):
        for d in range(3):
            spread = [mm(w2_ref[a, b, d], pick) for a in range(3)]
            for r in range(half):
                block = banded(spread, place, r - 1)
                lanes = slice(b * wide, (b + 1) * wide)
                if r < half - 1:
                    t2_ref[0, d * tall + r * hid : d * tall + (r + 1) * hid, lanes] = block
                if r > 0:
                    t2_ref[1, d * tall + (r - 1) * hid : d * tall + r * hid, lanes] = block
                if 0 < r < 3:
                    top = (d * 2 + r - 1) * hid
                    t2m_ref[top : top + hid, b * 4 * hid : (b + 1) * 4 * hid] = block[:, : 4 * hid]
    channels = w1_ref.shape[3]
    taps, cols = 9 * channels, t1_ref.shape[2]
    depth = cols // 3
    main = 3 * channels * half
    row = iota((1, cols), 1) % depth
    beyond = row - main
    spot = jnp.where(beyond < 0, row // half, beyond // (2 * channels) * channels + beyond % channels)
    tap = iota((1, cols), 1) // depth * 3 * channels + spot
    pick = (iota((taps, cols), 0) == tap).astype(BF16)
    spread = []
    for a in range(3):
        stack = jnp.concatenate(
            [w1_ref[a, b, d].astype(F32) for b in range(3) for d in range(3)], axis=0
        ).astype(BF16)
        spread.append(
            lax.dot_general(stack, pick, (((0,), (0,)), ((), ())), preferred_element_type=F32)
        )
    outer = beyond % (2 * channels) // channels
    for part, cell in ((0, half), (1, -1)):
        place = jnp.where((outer == part) & (spot < 3 * channels), cell, -9)
        place = jnp.broadcast_to(jnp.where(beyond < 0, row % half, place), (hid, cols))
        for z in range(half):
            t1_ref[part, z * hid : (z + 1) * hid, :] = banded(spread, place, z - 1)
    rows3, cols3 = t3_ref.shape
    taps = rows3 // nz
    pick = (iota((hid, cols3), 0) == iota((hid, cols3), 1) % hid).astype(BF16)
    offset = iota((nz, cols3), 1) // hid - iota((nz, cols3), 0)
    spread = []
    for a in range(3):
        stack = jnp.concatenate(
            [w3_ref[a, b, d].astype(F32) for b in range(3) for d in range(3)], axis=0
        ).astype(BF16)
        spread.append(mm(stack, pick))
    for r in range(taps):
        rows = [jnp.broadcast_to(spread[a][r : r + 1], (nz, cols3)) for a in range(3)]
        t3_ref[r * nz : (r + 1) * nz, :] = banded(rows, offset, -1)
    kr, ki = zk_ref[0], zk_ref[1]
    top = jnp.concatenate([kr, -ki], axis=1)
    bottom = jnp.concatenate([ki, kr], axis=1)
    high, low = split(jnp.concatenate([top, bottom], axis=0))
    z_ref[...] = jnp.concatenate([high, high, low], axis=1)
    count, lanes = sp_ref.shape[1], sr_ref.shape[1]
    pick = (iota((count, lanes), 0) == iota((count, lanes), 1) // (lanes // count)).astype(F32)
    for part, ref in ((0, sr_ref), (1, si_ref)):
        ref[...] = lax.dot_general(
            sp_ref[part],
            pick,
            (((0,), (0,)), ((), ())),
            precision=lax.Precision.HIGHEST,
            preferred_element_type=F32,
        )
    ny = whole_ref.shape[3]
    deep = feat_ref.shape[0] // whole_ref.shape[0]
    classes = spread_classes(con_ref, whole_ref.shape[2:])
    for x in range(whole_ref.shape[0]):
        column = unpacked(whole_ref, x, classes)
        if x == 0:
            pol_ref[...] = jnp.concatenate(column[2:], axis=0)
        feat_ref[x * deep : (x + 1) * deep, :] = features_of(column, ny)
    made = first_product(t1_ref, lambda x: feat_ref[x * deep : (x + 1) * deep, :], (0, 1))
    hid_ref[...] = gelu(made).astype(BF16)


def gelu(values):
    half = 0.5 * values
    return half + half * lax.erf(values * math.sqrt(0.5))


def corrector_kernel(
    con_ref, first_ref, second_ref, own_feat, own_hid, own_pol, t1_ref, t2_ref, t2m_ref, t3_ref,
    z_ref, dft_ref, green_ref, out_ref, feat, hid1, hid2,
):
    nz, ny = first_ref.shape[2:]
    ahead = first_ref.shape[0] + second_ref.shape[0]
    xl = first_ref.shape[0]
    depth = feat.shape[0] // ahead
    half = hid1.shape[0] // 2
    hid = 2 * half // nz
    tall = half - hid
    deep = 2 * nz
    classes = spread_classes(con_ref, (nz, ny))
    own = {}
    last = {}

    def features(place):
        if place < 2:
            column = [second_ref[place, i] for i in range(4)]
        else:
            column = unpacked(first_ref, place - 2, classes)
        if place > 2:
            own[place - 3] = jnp.concatenate(column[2:], axis=0)
        feat[place * depth : (place + 1) * depth, :] = features_of(column, ny)

    def feature_rows(place):
        if place < ahead:
            return feat[place * depth : (place + 1) * depth, :]
        return own_feat[(place - ahead) * depth : (place - ahead + 1) * depth, :]

    def first_layer(j):
        return first_product(t1_ref, feature_rows, (j, j + 1))

    def first_done(j, made):
        hid1[:, j * ny : (j + 2) * ny] = gelu(made).astype(BF16)

    def hidden(place, top, bottom):
        if place < ahead:
            return hid1[top:bottom, place * ny : (place + 1) * ny]
        return own_hid[top:bottom, (place - ahead) * ny : (place - ahead + 1) * ny]

    def tap_sum(weights, top, bottom, j):
        window = [
            jnp.concatenate([hidden(j + b + i, top, bottom) for i in range(2)], axis=1) for b in range(3)
        ]
        made = mm(weights, jnp.concatenate(window, axis=0))
        rows = weights.shape[0] // 3
        sides = []
        for i in range(2):
            lanes = slice(i * ny, (i + 1) * ny)
            sides.append(
                pltpu.roll(made[:rows, lanes], 1, 1)
                + made[rows : 2 * rows, lanes]
                + pltpu.roll(made[2 * rows :, lanes], ny - 1, 1)
            )
        return jnp.concatenate(sides, axis=1)

    def second_layer(j):
        return [
            tap_sum(t2_ref[0], 0, half, j),
            tap_sum(t2m_ref[...], half - 2 * hid, half + 2 * hid, j),
            tap_sum(t2_ref[1], half, 2 * half, j),
        ]

    def second_done(j, made):
        lanes = slice(j * ny, (j + 2) * ny)
        for top, part in zip((0, tall, tall + 2 * hid), made):
            hid2[top : top + part.shape[0], lanes] = gelu(part).astype(BF16)

    def third_layer(j):
        made = mm(t3_ref[...], hid2[:, j * ny : (j + 2) * ny])
        last[j], last[j + 1] = made[:, :ny], made[:, ny:]

    def source(x):
        parts = []
        for d in range(3):
            total = None
            for b in range(3):
                top = (b * 3 + d) * deep
                piece = last[x + b][top : top + deep]
                total = piece if total is None else total + piece
            parts.append(total)
        return own[x] + (pltpu.roll(parts[0], 1, 1) + parts[1] + pltpu.roll(parts[2], ny - 1, 1))

    def transformed(places):
        lifted = mm(z_ref[...], right_split(jnp.concatenate([source(x) for x in places], axis=1)))
        rows = [lifted[:, i * ny : (i + 1) * ny] for i in range(len(places))]
        made = mm(left_split(jnp.concatenate(rows, axis=0)), dft_ref[...])
        return jnp.concatenate(mixed(made, nz, 1.0), axis=0)

    own[xl - 1] = own_pol[...]
    pairs = range(ahead - 2, -1, -2)
    for j in pairs:
        features(j)
        features(j + 1)
    for j in pairs:
        first_done(j, first_layer(j))
    for j in pairs:
        second_done(j, second_layer(j))
    for j in pairs:
        third_layer(j)
    out_ref[...] = jnp.transpose(transformed(range(xl))).reshape(out_ref.shape)


def green_kernel(fwd_ref, inv_ref, sr_ref, si_ref, green_ref):
    nx = inv_ref.shape[0]
    table = fwd_ref[:, :nx].astype(F32) + fwd_ref[:, 2 * nx :].astype(F32)
    cos, sin = table[:nx], table[nx:]
    count = green_ref.shape[0] // nx
    inner = sr_ref.shape[1] // count
    for q in range(count):
        re, im = sr_ref[:, q * inner : q * inner + 1], si_ref[:, q * inner : q * inner + 1]
        same, cross = re * cos + im * sin, re * sin - im * cos
        top = jnp.concatenate([same, -cross], axis=1)
        bottom = jnp.concatenate([cross, same], axis=1)
        high, low = split(mm(inv_ref[...], right_split(jnp.concatenate([top, bottom], axis=0))))
        green_ref[q * nx : (q + 1) * nx, :] = jnp.concatenate([high, high, low], axis=1)


def spectral_kernel(nz, in_ref, green_ref, out_ref):
    values = swap_blocks(in_ref, in_ref.shape[1])
    both = jnp.concatenate([values, turned(values, nz)], axis=0)
    made = mm(green_ref[...], right_split(both))
    nx, lanes = values.shape
    count = made.shape[0] // nx
    block = iota((nx, lanes), 1) // (lanes // count)
    total = made[:nx]
    for q in range(1, count):
        total = jnp.where(block == q, made[q * nx : (q + 1) * nx], total)
    out_ref[...] = total.reshape(out_ref.shape)


def finish_kernel(nz, in_ref, back_ref, inc_ref, out_ref):
    values = jnp.transpose(swap_blocks(in_ref, in_ref.shape[1]))
    blocks = mixed(mm(left_split(values), back_ref[...]), nz, -1.0)
    for x in range(out_ref.shape[2]):
        for part in range(2):
            out_ref[part, :, x, :] = inc_ref[part, :, x, :] + blocks[2 * x + part]


def call(kernel, out_shapes, args, scratch=(), flops=0):
    vmem = pl.BlockSpec(memory_space=pltpu.VMEM)
    single = not isinstance(out_shapes, list)
    return pl.pallas_call(
        kernel,
        out_shape=out_shapes,
        in_specs=[vmem] * len(args),
        out_specs=vmem if single else [vmem] * len(out_shapes),
        scratch_shapes=scratch,
        compiler_params=pltpu.CompilerParams(vmem_limit_bytes=VMEM_LIMIT),
        cost_estimate=pl.CostEstimate(flops=flops, bytes_accessed=4 * 1024 * 1024, transcendentals=0),
    )(*args)


def lane_device(incident, material, contrast, w_first, w_middle, w_last, z_kernel, spectral):
    count = lax.axis_size("gx")
    nz, xl, ny = material.shape
    hid = w_middle.shape[0]
    ql, nx = spectral.shape[1], spectral.shape[2]
    struct = jax.ShapeDtypeStruct
    classes = jnp.transpose(contrast)
    still = ((0, 0),) * 3
    own = jnp.pad(material[None], ((2, 1),) + still).astype(F32) + jnp.pad(incident, ((0, 2),) + still)
    parts, kinds = classes.shape
    own += jnp.pad(classes[None, None], ((3, 0), (0, nz - 1), (0, xl - parts), (0, ny - kinds)))
    planes = jnp.transpose(own, (2, 0, 1, 3))[:, :3]
    again = jnp.pad(planes, ((0, 0), (0, 2), (0, 0), (0, 0)))
    again += jnp.pad(planes[:, :2], ((0, 0), (3, 0), (0, 0), (0, 0)))
    high = lax.reduce_precision(again, 8, 7)
    later = lax.broadcasted_iota(jnp.int32, (1, 5, 1, 1), 1) > 2
    whole = jnp.where(later, again - high, high).astype(BF16)
    first = lax.ppermute(whole, "gx", [(i, (i + 1) % count) for i in range(count)])
    near = call(
        functools.partial(near_kernel, kinds), struct((2, 4, nz, ny), BF16), (own, whole), flops=10**6
    )
    second = lax.ppermute(near, "gx", [(i, (i + 2) % count) for i in range(count)])
    lanes = 2 * nz * xl
    depth, deep = 6 * nz + 32, 12 * nz + 32
    dft, fwd, inv, back = call(
        functools.partial(table_kernel, xl, 3),
        [
            struct((3 * ny, 2 * ny), BF16),
            struct((2 * nx, 3 * nx), BF16),
            struct((nx, 6 * nx), BF16),
            struct((3 * ny, 2 * ny), BF16),
        ],
        (),
        flops=10**9,
    )
    t1, t2, t2m, t3, zmat, sr, si, feat, hidden, pol = call(
        functools.partial(weight_kernel, nz),
        [
            struct((2, nz // 2 * hid, 3 * depth), BF16),
            struct((2, 3 * (nz // 2 - 1) * hid, 3 * nz // 2 * hid), BF16),
            struct((6 * hid, 12 * hid), BF16),
            struct((18 * nz, nz * hid), BF16),
            struct((2 * nz, 6 * nz), BF16),
            struct((nx, ql * 2 * nz), F32),
            struct((nx, ql * 2 * nz), F32),
            struct((xl * deep, ny), BF16),
            struct((nz * hid, 2 * ny), BF16),
            struct((2 * nz, ny), F32),
        ],
        (
            classes,
            whole,
            jnp.transpose(w_first, (2, 3, 4, 1, 0)),
            jnp.transpose(w_middle, (2, 3, 4, 0, 1)),
            jnp.transpose(w_last, (2, 3, 4, 0, 1)),
            z_kernel,
            spectral,
            dft,
        ),
        flops=10**9,
    )
    green = call(
        green_kernel, struct((ql * nx, 6 * nx), BF16), (fwd, inv, sr, si), flops=10**9
    )
    spectrum = call(
        corrector_kernel,
        struct((count, ql, lanes), F32),
        (classes, first, second, feat, hidden, pol, t1, t2, t2m, t3, zmat, dft, green),
        scratch=[
            pltpu.VMEM(((xl + 2) * deep, ny), BF16),
            pltpu.VMEM((nz * hid, (xl + 2) * ny), BF16),
            pltpu.VMEM((nz * hid, (xl + 2) * ny), BF16),
        ],
        flops=10**9,
    )
    piece = lax.all_to_all(spectrum, "gx", 0, 0, tiled=True)
    spread = call(
        functools.partial(spectral_kernel, nz),
        struct((count, xl, lanes), F32),
        (piece, green),
        flops=10**8,
    )
    rows = lax.all_to_all(spread, "gx", 0, 0, tiled=True)
    return call(
        functools.partial(finish_kernel, nz),
        struct(incident.shape, F32),
        (rows, back, own),
        flops=10**8,
    )


def per_device(incident, material, contrast, w_first, w_middle, w_last, z_kernel, spectral):
    nz, xl, ny = material.shape
    ql, nx = spectral.shape[1], spectral.shape[2]
    lanes = (
        lax.axis_size("gy") == 1
        and ny == 128
        and nx == 128
        and xl == 4
        and ql == 4
        and 2 * nz * xl == 128
        and w_middle.shape[0] == 32
    )
    device = lane_device if lanes else general_device
    return device(incident, material, contrast, w_first, w_middle, w_last, z_kernel, spectral)


def solution(mesh):
    placed = (
        P("grp", None, "gx", "gy"),
        P("grp", "gx", "gy"),
        P("grp", None),
        P(),
        P(),
        P(),
        P("grp", None, None),
        P("grp", "gx", None),
    )
    return jax.shard_map(
        per_device,
        mesh=mesh,
        in_specs=placed,
        out_specs=P("grp", None, "gx", "gy"),
        check_vma=False,
    )
```

```python
import functools
import math

import jax
import jax.numpy as jnp
from jax import lax
from jax.experimental import pallas as pl
from jax.experimental.pallas import tpu as pltpu
from jax.sharding import PartitionSpec as P

F32 = jnp.float32
BF16 = jnp.bfloat16
VMEM_LIMIT = 48 * 1024 * 1024


def padded_2(x, sides, width):
    for axis, dim in sides:
        count, length = (lax.axis_size(axis), x.shape[dim])
        up = [(i, (i + 1) % count) for i in range(count)]
        down = [(j, i) for i, j in up]
        last = lax.slice_in_dim(x, length - width, length, axis=dim)
        leading = lax.slice_in_dim(x, 0, width, axis=dim)
        before = lax.ppermute(last, axis, up)
        after = lax.ppermute(leading, axis, down)
        x = jnp.concatenate([before, x, after], axis=dim)
    return x


def conv_layer(values, weights):
    return lax.conv_general_dilated(
        values[None],
        weights,
        (1, 1, 1),
        ((1, 1), (0, 0), (0, 0)),
        dimension_numbers=("NCDHW", "OIDHW", "NCDHW"),
        preferred_element_type=jnp.float32,
    )[0]


def activate(values):
    return jax.nn.gelu(values, approximate=False).astype(jnp.bfloat16)


def dft_tables(length):
    positions = jnp.arange(length, dtype=jnp.int32)
    product = positions[:, None] * positions[None, :] % length
    angle = product.astype(jnp.float32) * (2.0 * math.pi / length)
    return (jnp.cos(angle), jnp.sin(angle))


def green_apply(source, z_kernel, spectral):
    high = lax.Precision.HIGHEST
    kr, ki = (z_kernel[0], z_kernel[1])
    lre = jnp.einsum("zw,wxy->zxy", kr, source[0], precision=high) - jnp.einsum(
        "zw,wxy->zxy", ki, source[1], precision=high
    )
    lim = jnp.einsum("zw,wxy->zxy", kr, source[1], precision=high) + jnp.einsum(
        "zw,wxy->zxy", ki, source[0], precision=high
    )
    columns = lax.all_to_all(jnp.stack([lre, lim]), "gy", split_axis=1, concat_axis=3, tiled=True)
    count_y = columns.shape[3]
    cos_y, sin_y = dft_tables(count_y)
    fwd_re = jnp.dot(columns[0], cos_y, precision=high) + jnp.dot(columns[1], sin_y, precision=high)
    fwd_im = jnp.dot(columns[1], cos_y, precision=high) - jnp.dot(columns[0], sin_y, precision=high)
    count_x = columns.shape[2] * lax.axis_size("gx")
    cos_x, sin_x = dft_tables(count_x)
    piece = lax.all_to_all(
        jnp.stack([fwd_re, fwd_im]), "gx", split_axis=3, concat_axis=2, tiled=True
    )
    ar = jnp.einsum("zxk,xq->zkq", piece[0], cos_x, precision=high) + jnp.einsum(
        "zxk,xq->zkq", piece[1], sin_x, precision=high
    )
    ai = jnp.einsum("zxk,xq->zkq", piece[1], cos_x, precision=high) - jnp.einsum(
        "zxk,xq->zkq", piece[0], sin_x, precision=high
    )
    br = spectral[0] * ar - spectral[1] * ai
    bi = spectral[0] * ai + spectral[1] * ar
    gr = jnp.einsum("zkq,qx->zxk", br, cos_x, precision=high) - jnp.einsum(
        "zkq,qx->zxk", bi, sin_x, precision=high
    )
    gi = jnp.einsum("zkq,qx->zxk", bi, cos_x, precision=high) + jnp.einsum(
        "zkq,qx->zxk", br, sin_x, precision=high
    )
    spread = jnp.stack([gr, gi]) / count_x
    rows = lax.all_to_all(spread, "gx", split_axis=2, concat_axis=3, tiled=True)
    inv_re = jnp.dot(rows[0], cos_y, precision=high) - jnp.dot(rows[1], sin_y, precision=high)
    inv_im = jnp.dot(rows[1], cos_y, precision=high) + jnp.dot(rows[0], sin_y, precision=high)
    scattered = jnp.stack([inv_re, inv_im]) / count_y
    return lax.all_to_all(scattered, "gy", split_axis=3, concat_axis=1, tiled=True)


def general_device(incident, material, contrast, w_first, w_middle, w_last, z_kernel, spectral):
    high = lax.Precision.HIGHEST
    classes = contrast.shape[0]
    selector = (material[None] == jnp.arange(classes, dtype=jnp.int32)[:, None, None, None]).astype(
        jnp.float32
    )
    chi_re = jnp.einsum("k,kzxy->zxy", contrast[:, 0], selector, precision=high)
    chi_im = jnp.einsum("k,kzxy->zxy", contrast[:, 1], selector, precision=high)
    field = incident
    pol_re = chi_re * field[0] - chi_im * field[1]
    pol_im = chi_re * field[1] + chi_im * field[0]
    features = jnp.stack([field[0], field[1], pol_re, pol_im]).astype(jnp.bfloat16)
    padded = padded_2(features, (("gx", 2), ("gy", 3)), 3)
    hidden = activate(conv_layer(padded, w_first))
    hidden = activate(conv_layer(hidden, w_middle))
    correction = conv_layer(hidden, w_last)
    source = jnp.stack([pol_re, pol_im]) + correction
    field = incident + green_apply(source, z_kernel, spectral)
    return field


def split(values):
    high = values.astype(BF16)
    low = (values - high.astype(F32)).astype(BF16)
    return high, low


def cosine(steps, length):
    turn = 2.0 * math.pi / length
    angle = (length // 4 - jnp.minimum(steps, length - steps)).astype(F32) * turn
    square = angle * angle
    total = jnp.full_like(angle, 1.0 / math.factorial(13))
    for power in (11, 9, 7, 5, 3, 1):
        sign = 1.0 if power % 4 == 1 else -1.0
        total = total * square + sign / math.factorial(power)
    return total * angle


def dft_parts(rows, cols, length, axis, along, scale=1.0):
    steps = lax.rem(rows * cols, length)
    later = lax.rem(steps + 3 * length // 4, length)
    high, low = split(jnp.concatenate([cosine(steps, length), cosine(later, length)], axis=axis) * scale)
    return jnp.concatenate([high, high, low], axis=along)


def left_split(values):
    high, low = split(values)
    return jnp.concatenate([high, low, high], axis=1)


def right_split(values):
    high, low = split(values)
    return jnp.concatenate([high, low, high], axis=0)


def mm(a, b):
    return jnp.dot(a, b, preferred_element_type=F32)


def iota(shape, dim):
    return lax.broadcasted_iota(jnp.int32, shape, dim)


def turned(values, nz):
    real = (iota(values.shape, 1) // nz) % 2 == 0
    ahead = pltpu.roll(values, values.shape[1] - nz, 1)
    return jnp.where(real, -ahead, pltpu.roll(values, nz, 1))


def mixed(made, nz, sign):
    half = made.shape[1] // 2
    blocks = []
    for top in range(0, made.shape[0], 2 * nz):
        re, im = made[top : top + nz], made[top + nz : top + 2 * nz]
        blocks.append(re[:, :half] + sign * im[:, half:])
        blocks.append(im[:, :half] - sign * re[:, half:])
    return blocks


def swap_blocks(ref, count):
    pieces = [ref[:, q, :] for q in range(count)]
    inner = pieces[0].shape[1] // count
    block = iota(pieces[0].shape, 1) // inner
    places = [block == q for q in range(count)]

    def chosen(options):
        total = options[0]
        for place, option in zip(places[1:], options[1:]):
            total = jnp.where(place, option, total)
        return total

    moved = []
    for step in range(count):
        total = chosen([pieces[(x + step) % count] for x in range(count)])
        moved.append(pltpu.roll(total, step * inner, 1) if step else total)
    rows = [chosen([moved[(q - x) % count] for q in range(count)]) for x in range(count)]
    return jnp.concatenate(rows, axis=0)


def spread_classes(con_ref, shape):
    return [
        [jnp.broadcast_to(con_ref[part : part + 1, k : k + 1], shape) for part in range(2)]
        for k in range(con_ref.shape[1])
    ]


def unpacked(ref, x, classes):
    high_re, high_im, cells, low_re, low_im = [ref[x, i].astype(F32) for i in range(5)]
    re, im = high_re + low_re, high_im + low_im
    chi_re = jnp.zeros_like(re)
    chi_im = jnp.zeros_like(re)
    for k, (class_re, class_im) in enumerate(classes):
        here = cells == float(k)
        chi_re = jnp.where(here, class_re, chi_re)
        chi_im = jnp.where(here, class_im, chi_im)
    return [high_re, high_im, chi_re * re - chi_im * im, chi_re * im + chi_im * re]


def near_kernel(class_count, own_ref, whole_ref, near_ref):
    xl, _, nz, ny = whole_ref.shape
    classes = [
        [jnp.broadcast_to(own_ref[3, 0, part : part + 1, k : k + 1], (nz, ny)) for part in range(2)]
        for k in range(class_count)
    ]
    for x in range(2):
        for i, plane in enumerate(unpacked(whole_ref, xl - 2 + x, classes)):
            near_ref[x, i] = plane.astype(BF16)


def table_kernel(xl, shift, dft_ref, fwd_ref, inv_ref, back_ref):
    nx, ny = inv_ref.shape[0], dft_ref.shape[1] // 2
    dft_ref[...] = dft_parts(iota((ny, ny), 0), iota((ny, ny), 1), ny, 1, 0)
    first, second = iota((nx, nx), 0), iota((nx, nx), 1)
    inv_ref[...] = dft_parts(lax.rem(first + shift, nx), second, nx, 1, 1, 1.0 / (nx * ny))
    count = nx // xl
    second = lax.rem(second, count) * xl + second // count
    fwd_ref[...] = dft_parts(first, second, nx, 0, 1)
    first, second = iota((ny, ny), 0), iota((ny, ny), 1)
    count = ny // xl
    back_ref[...] = dft_parts(lax.rem(first, count) * xl + first // count, second, ny, 1, 0)


def features_of(column, ny):
    planes = [plane.astype(F32) for plane in column]
    half = planes[0].shape[0] // 2
    lower = jnp.concatenate([plane[:half] for plane in planes], axis=0)
    upper = jnp.concatenate([plane[half:] for plane in planes], axis=0)
    rows = [plane[half : half + 1] for plane in planes] + [plane[half - 1 : half] for plane in planes]
    edge = jnp.concatenate(rows, axis=0)
    made = []
    for part in (lower, upper, edge):
        made += [pltpu.roll(part, 1, 1), part, pltpu.roll(part, ny - 1, 1)]
    return jnp.concatenate(made + [jnp.zeros_like(edge)], axis=0).astype(BF16)


def first_product(t1_ref, rows_of, places):
    made = []
    depth = t1_ref.shape[2] // 3
    for part in range(2):
        pieces = []
        for place in places:
            taps = []
            for b in range(3):
                rows = rows_of(place + b)
                edge = 2 * depth - rows.shape[0]
                main = depth - edge
                taps += [rows[part * main : (part + 1) * main], rows[2 * main :]]
            pieces.append(jnp.concatenate(taps, axis=0))
        made.append(mm(t1_ref[part], jnp.concatenate(pieces, axis=1)))
    return jnp.concatenate(made, axis=0)


def banded(spread, place, start):
    rows = jnp.zeros_like(spread[0])
    for a in range(3):
        rows = jnp.where(place == start + a, spread[a], rows)
    return rows.astype(BF16)


def weight_kernel(
    nz, con_ref, whole_ref, w1_ref, w2_ref, w3_ref, zk_ref, sp_ref, dft_ref,
    t1_ref, t2_ref, t2m_ref, t3_ref, z_ref, sr_ref, si_ref, feat_ref, hid_ref, pol_ref,
):
    hid = w2_ref.shape[3]
    half = nz // 2
    wide = half * hid
    pick = (iota((hid, wide), 0) == iota((hid, wide), 1) % hid).astype(BF16)
    place = iota((hid, wide), 1) // hid
    tall = (half - 1) * hid
    for b in range(3):
        for d in range(3):
            spread = [mm(w2_ref[a, b, d], pick) for a in range(3)]
            for r in range(half):
                block = banded(spread, place, r - 1)
                lanes = slice(b * wide, (b + 1) * wide)
                if r < half - 1:
                    t2_ref[0, d * tall + r * hid : d * tall + (r + 1) * hid, lanes] = block
                if r > 0:
                    t2_ref[1, d * tall + (r - 1) * hid : d * tall + r * hid, lanes] = block
                if 0 < r < 3:
                    top = (d * 2 + r - 1) * hid
                    t2m_ref[top : top + hid, b * 4 * hid : (b + 1) * 4 * hid] = block[:, : 4 * hid]
    channels = w1_ref.shape[3]
    taps, cols = 9 * channels, t1_ref.shape[2]
    depth = cols // 3
    main = 3 * channels * half
    row = iota((1, cols), 1) % depth
    beyond = row - main
    spot = jnp.where(beyond < 0, row // half, beyond // (2 * channels) * channels + beyond % channels)
    tap = iota((1, cols), 1) // depth * 3 * channels + spot
    pick = (iota((taps, cols), 0) == tap).astype(BF16)
    spread = []
    for a in range(3):
        stack = jnp.concatenate(
            [w1_ref[a, b, d].astype(F32) for b in range(3) for d in range(3)], axis=0
        ).astype(BF16)
        spread.append(
            lax.dot_general(stack, pick, (((0,), (0,)), ((), ())), preferred_element_type=F32)
        )
    outer = beyond % (2 * channels) // channels
    for part, cell in ((0, half), (1, -1)):
        place = jnp.where((outer == part) & (spot < 3 * channels), cell, -9)
        place = jnp.broadcast_to(jnp.where(beyond < 0, row % half, place), (hid, cols))
        for z in range(half):
            t1_ref[part, z * hid : (z + 1) * hid, :] = banded(spread, place, z - 1)
    rows3, cols3 = t3_ref.shape
    taps = rows3 // nz
    pick = (iota((hid, cols3), 0) == iota((hid, cols3), 1) % hid).astype(BF16)
    offset = iota((nz, cols3), 1) // hid - iota((nz, cols3), 0)
    spread = []
    for a in range(3):
        stack = jnp.concatenate(
            [w3_ref[a, b, d].astype(F32) for b in range(3) for d in range(3)], axis=0
        ).astype(BF16)
        spread.append(mm(stack, pick))
    for r in range(taps):
        rows = [jnp.broadcast_to(spread[a][r : r + 1], (nz, cols3)) for a in range(3)]
        t3_ref[r * nz : (r + 1) * nz, :] = banded(rows, offset, -1)
    kr, ki = zk_ref[0], zk_ref[1]
    top = jnp.concatenate([kr, -ki], axis=1)
    bottom = jnp.concatenate([ki, kr], axis=1)
    high, low = split(jnp.concatenate([top, bottom], axis=0))
    z_ref[...] = jnp.concatenate([high, high, low], axis=1)
    count, lanes = sp_ref.shape[1], sr_ref.shape[1]
    pick = (iota((count, lanes), 0) == iota((count, lanes), 1) // (lanes // count)).astype(F32)
    for part, ref in ((0, sr_ref), (1, si_ref)):
        ref[...] = lax.dot_general(
            sp_ref[part],
            pick,
            (((0,), (0,)), ((), ())),
            precision=lax.Precision.HIGHEST,
            preferred_element_type=F32,
        )
    ny = whole_ref.shape[3]
    deep = feat_ref.shape[0] // whole_ref.shape[0]
    classes = spread_classes(con_ref, whole_ref.shape[2:])
    for x in range(whole_ref.shape[0]):
        column = unpacked(whole_ref, x, classes)
        if x == 0:
            pol_ref[...] = jnp.concatenate(column[2:], axis=0)
        feat_ref[x * deep : (x + 1) * deep, :] = features_of(column, ny)
    made = first_product(t1_ref, lambda x: feat_ref[x * deep : (x + 1) * deep, :], (0, 1))
    hid_ref[...] = gelu(made).astype(BF16)


def gelu(values):
    half = 0.5 * values
    return half + half * lax.erf(values * math.sqrt(0.5))


def corrector_kernel(
    con_ref, first_ref, second_ref, own_feat, own_hid, own_pol, t1_ref, t2_ref, t2m_ref, t3_ref,
    z_ref, dft_ref, green_ref, out_ref, feat, hid1, hid2,
):
    nz, ny = first_ref.shape[2:]
    ahead = first_ref.shape[0] + second_ref.shape[0]
    xl = first_ref.shape[0]
    depth = feat.shape[0] // ahead
    half = hid1.shape[0] // 2
    hid = 2 * half // nz
    tall = half - hid
    deep = 2 * nz
    classes = spread_classes(con_ref, (nz, ny))
    own = {}
    last = {}

    def features(place):
        if place < 2:
            column = [second_ref[place, i] for i in range(4)]
        else:
            column = unpacked(first_ref, place - 2, classes)
        if place > 2:
            own[place - 3] = jnp.concatenate(column[2:], axis=0)
        feat[place * depth : (place + 1) * depth, :] = features_of(column, ny)

    def feature_rows(place):
        if place < ahead:
            return feat[place * depth : (place + 1) * depth, :]
        return own_feat[(place - ahead) * depth : (place - ahead + 1) * depth, :]

    def first_layer(j):
        return first_product(t1_ref, feature_rows, (j, j + 1))

    def first_done(j, made):
        hid1[:, j * ny : (j + 2) * ny] = gelu(made).astype(BF16)

    def hidden(place, top, bottom):
        if place < ahead:
            return hid1[top:bottom, place * ny : (place + 1) * ny]
        return own_hid[top:bottom, (place - ahead) * ny : (place - ahead + 1) * ny]

    def tap_sum(weights, top, bottom, j):
        window = [
            jnp.concatenate([hidden(j + b + i, top, bottom) for i in range(ahead)], axis=1) for b in range(3)
        ]
        made = mm(weights, jnp.concatenate(window, axis=0))
        rows = weights.shape[0] // 3
        sides = []
        for i in range(ahead):
            lanes = slice(i * ny, (i + 1) * ny)
            sides.append(
                pltpu.roll(made[:rows, lanes], 1, 1)
                + made[rows : 2 * rows, lanes]
                + pltpu.roll(made[2 * rows :, lanes], ny - 1, 1)
            )
        return jnp.concatenate(sides, axis=1)

    def second_layer(j):
        return [
            tap_sum(t2_ref[0], 0, half, j),
            tap_sum(t2m_ref[...], half - 2 * hid, half + 2 * hid, j),
            tap_sum(t2_ref[1], half, 2 * half, j),
        ]

    def second_done(j, made):
        lanes = slice(j * ny, (j + ahead) * ny)
        for top, part in zip((0, tall, tall + 2 * hid), made):
            hid2[top : top + part.shape[0], lanes] = gelu(part).astype(BF16)

    def third_layer(j):
        made = mm(t3_ref[...], hid2[:, j * ny : (j + 2) * ny])
        last[j], last[j + 1] = made[:, :ny], made[:, ny:]

    def source(x):
        parts = []
        for d in range(3):
            total = None
            for b in range(3):
                top = (b * 3 + d) * deep
                piece = last[x + b][top : top + deep]
                total = piece if total is None else total + piece
            parts.append(total)
        return own[x] + (pltpu.roll(parts[0], 1, 1) + parts[1] + pltpu.roll(parts[2], ny - 1, 1))

    def transformed(places):
        lifted = mm(z_ref[...], right_split(jnp.concatenate([source(x) for x in places], axis=1)))
        rows = [lifted[:, i * ny : (i + 1) * ny] for i in range(len(places))]
        made = mm(left_split(jnp.concatenate(rows, axis=0)), dft_ref[...])
        return jnp.concatenate(mixed(made, nz, 1.0), axis=0)

    own[xl - 1] = own_pol[...]
    for place in range(ahead):
        features(place)
    hid1[...] = gelu(first_product(t1_ref, feature_rows, range(ahead))).astype(BF16)
    second_done(0, second_layer(0))
    made = mm(t3_ref[...], hid2[...])
    for x in range(ahead):
        last[x] = made[:, x * ny : (x + 1) * ny]
    out_ref[...] = jnp.transpose(transformed(range(xl))).reshape(out_ref.shape)


def green_kernel(fwd_ref, inv_ref, sr_ref, si_ref, green_ref):
    nx = inv_ref.shape[0]
    table = fwd_ref[:, :nx].astype(F32) + fwd_ref[:, 2 * nx :].astype(F32)
    cos, sin = table[:nx], table[nx:]
    count = green_ref.shape[0] // nx
    inner = sr_ref.shape[1] // count
    for q in range(count):
        re, im = sr_ref[:, q * inner : q * inner + 1], si_ref[:, q * inner : q * inner + 1]
        same, cross = re * cos + im * sin, re * sin - im * cos
        top = jnp.concatenate([same, -cross], axis=1)
        bottom = jnp.concatenate([cross, same], axis=1)
        high, low = split(mm(inv_ref[...], right_split(jnp.concatenate([top, bottom], axis=0))))
        green_ref[q * nx : (q + 1) * nx, :] = jnp.concatenate([high, high, low], axis=1)


def spectral_kernel(nz, in_ref, green_ref, out_ref):
    values = swap_blocks(in_ref, in_ref.shape[1])
    both = jnp.concatenate([values, turned(values, nz)], axis=0)
    made = mm(green_ref[...], right_split(both))
    nx, lanes = values.shape
    count = made.shape[0] // nx
    block = iota((nx, lanes), 1) // (lanes // count)
    total = made[:nx]
    for q in range(1, count):
        total = jnp.where(block == q, made[q * nx : (q + 1) * nx], total)
    out_ref[...] = total.reshape(out_ref.shape)


def finish_kernel(nz, in_ref, back_ref, inc_ref, out_ref):
    values = jnp.transpose(swap_blocks(in_ref, in_ref.shape[1]))
    blocks = mixed(mm(left_split(values), back_ref[...]), nz, -1.0)
    for x in range(out_ref.shape[2]):
        for part in range(2):
            out_ref[part, :, x, :] = inc_ref[part, :, x, :] + blocks[2 * x + part]


def call(kernel, out_shapes, args, scratch=(), flops=0):
    vmem = pl.BlockSpec(memory_space=pltpu.VMEM)
    single = not isinstance(out_shapes, list)
    return pl.pallas_call(
        kernel,
        out_shape=out_shapes,
        in_specs=[vmem] * len(args),
        out_specs=vmem if single else [vmem] * len(out_shapes),
        scratch_shapes=scratch,
        compiler_params=pltpu.CompilerParams(vmem_limit_bytes=VMEM_LIMIT),
        cost_estimate=pl.CostEstimate(flops=flops, bytes_accessed=4 * 1024 * 1024, transcendentals=0),
    )(*args)


def lane_device(incident, material, contrast, w_first, w_middle, w_last, z_kernel, spectral):
    count = lax.axis_size("gx")
    nz, xl, ny = material.shape
    hid = w_middle.shape[0]
    ql, nx = spectral.shape[1], spectral.shape[2]
    struct = jax.ShapeDtypeStruct
    classes = jnp.transpose(contrast)
    still = ((0, 0),) * 3
    own = jnp.pad(material[None], ((2, 1),) + still).astype(F32) + jnp.pad(incident, ((0, 2),) + still)
    parts, kinds = classes.shape
    own += jnp.pad(classes[None, None], ((3, 0), (0, nz - 1), (0, xl - parts), (0, ny - kinds)))
    planes = jnp.transpose(own, (2, 0, 1, 3))[:, :3]
    again = jnp.pad(planes, ((0, 0), (0, 2), (0, 0), (0, 0)))
    again += jnp.pad(planes[:, :2], ((0, 0), (3, 0), (0, 0), (0, 0)))
    high = lax.reduce_precision(again, 8, 7)
    later = lax.broadcasted_iota(jnp.int32, (1, 5, 1, 1), 1) > 2
    whole = jnp.where(later, again - high, high).astype(BF16)
    first = lax.ppermute(whole, "gx", [(i, (i + 1) % count) for i in range(count)])
    near = call(
        functools.partial(near_kernel, kinds), struct((2, 4, nz, ny), BF16), (own, whole), flops=10**6
    )
    second = lax.ppermute(near, "gx", [(i, (i + 2) % count) for i in range(count)])
    lanes = 2 * nz * xl
    depth, deep = 6 * nz + 32, 12 * nz + 32
    dft, fwd, inv, back = call(
        functools.partial(table_kernel, xl, 3),
        [
            struct((3 * ny, 2 * ny), BF16),
            struct((2 * nx, 3 * nx), BF16),
            struct((nx, 6 * nx), BF16),
            struct((3 * ny, 2 * ny), BF16),
        ],
        (),
        flops=10**9,
    )
    t1, t2, t2m, t3, zmat, sr, si, feat, hidden, pol = call(
        functools.partial(weight_kernel, nz),
        [
            struct((2, nz // 2 * hid, 3 * depth), BF16),
            struct((2, 3 * (nz // 2 - 1) * hid, 3 * nz // 2 * hid), BF16),
            struct((6 * hid, 12 * hid), BF16),
            struct((18 * nz, nz * hid), BF16),
            struct((2 * nz, 6 * nz), BF16),
            struct((nx, ql * 2 * nz), F32),
            struct((nx, ql * 2 * nz), F32),
            struct((xl * deep, ny), BF16),
            struct((nz * hid, 2 * ny), BF16),
            struct((2 * nz, ny), F32),
        ],
        (
            classes,
            whole,
            jnp.transpose(w_first, (2, 3, 4, 1, 0)),
            jnp.transpose(w_middle, (2, 3, 4, 0, 1)),
            jnp.transpose(w_last, (2, 3, 4, 0, 1)),
            z_kernel,
            spectral,
            dft,
        ),
        flops=10**9,
    )
    green = call(
        green_kernel, struct((ql * nx, 6 * nx), BF16), (fwd, inv, sr, si), flops=10**9
    )
    spectrum = call(
        corrector_kernel,
        struct((count, ql, lanes), F32),
        (classes, first, second, feat, hidden, pol, t1, t2, t2m, t3, zmat, dft, green),
        scratch=[
            pltpu.VMEM(((xl + 2) * deep, ny), BF16),
            pltpu.VMEM((nz * hid, (xl + 2) * ny), BF16),
            pltpu.VMEM((nz * hid, (xl + 2) * ny), BF16),
        ],
        flops=10**9,
    )
    piece = lax.all_to_all(spectrum, "gx", 0, 0, tiled=True)
    spread = call(
        functools.partial(spectral_kernel, nz),
        struct((count, xl, lanes), F32),
        (piece, green),
        flops=10**8,
    )
    rows = lax.all_to_all(spread, "gx", 0, 0, tiled=True)
    return call(
        functools.partial(finish_kernel, nz),
        struct(incident.shape, F32),
        (rows, back, own),
        flops=10**8,
    )


def per_device(incident, material, contrast, w_first, w_middle, w_last, z_kernel, spectral):
    nz, xl, ny = material.shape
    ql, nx = spectral.shape[1], spectral.shape[2]
    lanes = (
        lax.axis_size("gy") == 1
        and ny == 128
        and nx == 128
        and xl == 4
        and ql == 4
        and 2 * nz * xl == 128
        and w_middle.shape[0] == 32
    )
    device = lane_device if lanes else general_device
    return device(incident, material, contrast, w_first, w_middle, w_last, z_kernel, spectral)


def solution(mesh):
    placed = (
        P("grp", None, "gx", "gy"),
        P("grp", "gx", "gy"),
        P("grp", None),
        P(),
        P(),
        P(),
        P("grp", None, None),
        P("grp", "gx", None),
    )
    return jax.shard_map(
        per_device,
        mesh=mesh,
        in_specs=placed,
        out_specs=P("grp", None, "gx", "gy"),
        check_vma=False,
    )
```
